128 devices in a mesh: dp: 8 (over x, core), mp: 16 (over y, z).
Axes of the slice: x: 4, y: 4, z: 4, core: 2. Of those that a mesh axis runs over, the one named last changes fastest.
Arguments:
- tokens: bfloat16 [16384, 1024], P(('dp', 'mp')), may hold values from -6 to 6
- lengths: int32 [8], P('dp'), may hold values from 1024 to 2048, as said below
- cotangent: bfloat16 [16384, 1024], P(('dp', 'mp')), may hold values from -6 to 6
- norm_one: float32 [1024], replicated, may hold values from 0.5 to 1.5
- recur_input: bfloat16 [1024, 1536], P(None, 'mp'), may hold values from -0.1875 to 0.1875
- recur_gate: bfloat16 [1024, 1536], P(None, 'mp'), may hold values from -0.1875 to 0.1875
- conv_kernel: float32 [4, 1536], P(None, 'mp'), may hold values from -3 to 3
- conv_bias: float32 [1536], P('mp'), may hold values from -3 to 3
- decay_gate: float32 [16, 96, 96], P('mp'), may hold values from -0.625 to 0.625
- decay_shift: float32 [1536], P('mp'), may hold values from -4 to 4
- input_gate: float32 [16, 96, 96], P('mp'), may hold values from -0.625 to 0.625
- input_shift: float32 [1536], P('mp'), may hold values from -4 to 4
- decay_param: float32 [1536], P('mp'), may hold values from 3.5 to 14
- recur_output: bfloat16 [1536, 1024], P('mp'), may hold values from -0.4375 to 0.4375
- norm_two: float32 [1024], replicated, may hold values from 0.5 to 1.5
- first_gate: bfloat16 [1024, 3072], P('dp', 'mp'), may hold values from -0.1875 to 0.1875
- first_value: bfloat16 [1024, 3072], P('dp', 'mp'), may hold values from -0.1875 to 0.1875
- first_down: bfloat16 [3072, 1024], P('mp', 'dp'), may hold values from -0.21875 to 0.21875
- norm_three: float32 [1024], replicated, may hold values from 0.5 to 1.5
- query_proj: bfloat16 [1024, 1024], P(('dp', 'mp')), may hold values from -0.1875 to 0.1875
- key_proj: bfloat16 [1024, 128], P(('dp', 'mp')), may hold values from -0.1875 to 0.1875
- value_proj: bfloat16 [1024, 128], P(('dp', 'mp')), may hold values from -0.1875 to 0.1875
- attn_output: bfloat16 [1024, 1024], P(('dp', 'mp')), may hold values from -0.75 to 0.75
- norm_four: float32 [1024], replicated, may hold values from 0.5 to 1.5
- second_gate: bfloat16 [1024, 3072], P('dp', 'mp'), may hold values from -0.1875 to 0.1875
- second_value: bfloat16 [1024, 3072], P('dp', 'mp'), may hold values from -0.1875 to 0.1875
- second_down: bfloat16 [3072, 1024], P('mp', 'dp'), may hold values from -0.21875 to 0.21875
Outputs:
- outputs: float32 [16384, 1024], P(('dp', 'mp'))
- grad_tokens: float32 [16384, 1024], P(('dp', 'mp'))
- grad_norm_one: float32 [1024], replicated
- grad_recur_input: float32 [1024, 1536], P(None, 'mp')
- grad_recur_gate: float32 [1024, 1536], P(None, 'mp')
- grad_conv_kernel: float32 [4, 1536], P(None, 'mp')
- grad_conv_bias: float32 [1536], P('mp')
- grad_decay_gate: float32 [16, 96, 96], P('mp')
- grad_decay_shift: float32 [1536], P('mp')
- grad_input_gate: float32 [16, 96, 96], P('mp')
- grad_input_shift: float32 [1536], P('mp')
- grad_decay_param: float32 [1536], P('mp')
- grad_recur_output: float32 [1536, 1024], P('mp')
- grad_norm_two: float32 [1024], replicated
- grad_first_gate: float32 [1024, 3072], P('dp', 'mp')
- grad_first_value: float32 [1024, 3072], P('dp', 'mp')
- grad_first_down: float32 [3072, 1024], P('mp', 'dp')
- grad_norm_three: float32 [1024], replicated
- grad_query_proj: float32 [1024, 1024], P(('dp', 'mp'))
- grad_key_proj: float32 [1024, 128], P(('dp', 'mp'))
- grad_value_proj: float32 [1024, 128], P(('dp', 'mp'))
- grad_attn_output: float32 [1024, 1024], P(('dp', 'mp'))
- grad_norm_four: float32 [1024], replicated
- grad_second_gate: float32 [1024, 3072], P('dp', 'mp')
- grad_second_value: float32 [1024, 3072], P('dp', 'mp')
- grad_second_down: float32 [3072, 1024], P('mp', 'dp')
The draws below stay inside these ranges and needn't reach their ends.
Inputs may be any that keep to these rules, and one draw needn't show every extreme that they name: lengths[g] tokens of group g form its first document, the other 2048 - lengths[g] its second one (none if lengths[g] = 2048).
All inputs are finite; a program needn't handle non-finite values.
Results may differ from the reference program's by a relative error of at most 0.02.
Values may be sent and summed in bfloat16 or wider, within the bound.
A program may use at most 192 MiB of HBM per device.

```python
import math
import jax
import jax.numpy as jnp
from jax import lax

D = 1024
R = 1536
FF = 3072
H = 8
HD = 128
WINDOW = 1024
CONV = 4
BW = 96
GROUP = 2048
TOKENS = 16384
NB = 16
N_DP = 8


def draw_lengths(key, part):
    key = jax.random.fold_in(key, 5)
    order_key, length_key = jax.random.split(key)
    order = jax.random.permutation(order_key, N_DP)
    drawn = jax.random.randint(length_key, (N_DP,), GROUP // 2, GROUP + 1)
    drawn = drawn.at[order[0]].set(GROUP)
    drawn = drawn.at[order[1]].set(GROUP // 2)
    return drawn.astype(jnp.int32)


def draw_decay_param(key, part):
    key = jax.random.fold_in(key, 9)
    pick_key, slow_key, fast_key = jax.random.split(key, 3)
    share = 0.5
    slow = jax.random.uniform(pick_key, (R,)) < share
    slow_rate = jnp.exp(jax.random.uniform(slow_key, (R,), minval=math.log(0.25), maxval=0.0)) * (math.log(10.0) / (4.0 * GROUP))
    fast_rate = jnp.exp(jax.random.uniform(fast_key, (R,), minval=math.log(1.0 / 400.0), maxval=math.log(1.0 / 40.0)))
    chosen = jnp.where(slow, slow_rate, fast_rate)
    return (-jnp.log(jnp.expm1(chosen))).astype(jnp.float32)


def block_scale(rng, extent, shards, smallest, top_value):
    factor_of, own = 1.0, jax.random.fold_in(rng, 6)
    for dim, blocks in shards:
        draws = jnp.exp(jax.random.uniform(jax.random.fold_in(own, dim), (blocks,), jnp.float32, smallest / len(shards), top_value / len(shards)))
        factor_of = factor_of * jnp.repeat(draws, extent[dim] // blocks).reshape([-1 if axis == dim else 1 for axis in range(len(extent))])
    return factor_of


def gaussian(key, shape, width, reach, shards=(), kind=jnp.bfloat16):
    result = jax.random.normal(key, shape, jnp.float32) * width
    if len(shards) > 0:
        result = block_scale(key, shape, shards, -0.22, 0.18) * result
    return jnp.clip(result, min=-reach, max=reach).astype(kind)


def setup_inputs(seed: int = 0) -> dict:
    key_of = jax.random.split(jax.random.key(seed), 28)
    return {
        "tokens": gaussian(key_of[0], (TOKENS, D), 1.0, 6.0, ((0, 128),)),
        "lengths": draw_lengths(jax.random.fold_in(key_of[27], 71), 0),
        "cotangent": gaussian(key_of[2], (TOKENS, D), 1.0, 6.0, ((0, 128),)),
        "norm_one": jnp.clip(1.0 + 0.1 * jax.random.normal(key_of[3], (D,), jnp.float32), 0.5, 1.5),
        "recur_input": gaussian(key_of[4], (D, R), D ** -0.5, 0.1875, ((1, 16),)),
        "recur_gate": gaussian(key_of[5], (D, R), D ** -0.5, 0.1875, ((1, 16),)),
        "conv_kernel": gaussian(key_of[6], (CONV, R), 0.5, 3.0, ((1, 16),), jnp.float32),
        "conv_bias": gaussian(key_of[7], (R,), 0.5, 3.0, ((0, 16),), jnp.float32),
        "decay_gate": gaussian(key_of[8], (NB, BW, BW), BW ** -0.5, 0.625, ((0, 16),), jnp.float32),
        "decay_shift": gaussian(key_of[9], (R,), 1.0, 4.0, ((0, 16),), jnp.float32),
        "input_gate": gaussian(key_of[10], (NB, BW, BW), BW ** -0.5, 0.625, ((0, 16),), jnp.float32),
        "input_shift": gaussian(key_of[11], (R,), 1.0, 4.0, ((0, 16),), jnp.float32),
        "decay_param": draw_decay_param(jax.random.fold_in(key_of[27], 71), 0),
        "recur_output": gaussian(key_of[13], (R, D), (R // 8) ** -0.5, 0.4375, ((0, 16),)),
        "norm_two": jnp.clip(1.0 + 0.1 * jax.random.normal(key_of[14], (D,), jnp.float32), 0.5, 1.5),
        "first_gate": gaussian(key_of[15], (D, FF), D ** -0.5, 0.1875, ((0, 8), (1, 16))),
        "first_value": gaussian(key_of[16], (D, FF), D ** -0.5, 0.1875, ((0, 8), (1, 16))),
        "first_down": gaussian(key_of[17], (FF, D), (FF // 4) ** -0.5, 0.21875, ((0, 16), (1, 8))),
        "norm_three": jnp.clip(1.0 + 0.1 * jax.random.normal(key_of[18], (D,), jnp.float32), 0.5, 1.5),
        "query_proj": gaussian(key_of[19], (D, H * HD), D ** -0.5, 0.1875, ((0, 128),)),
        "key_proj": gaussian(key_of[20], (D, HD), D ** -0.5, 0.1875, ((0, 128),)),
        "value_proj": gaussian(key_of[21], (D, HD), D ** -0.5, 0.1875, ((0, 128),)),
        "attn_output": gaussian(key_of[22], (H * HD, D), (H * HD // 16) ** -0.5, 0.75, ((0, 128),)),
        "norm_four": jnp.clip(1.0 + 0.1 * jax.random.normal(key_of[23], (D,), jnp.float32), 0.5, 1.5),
        "second_gate": gaussian(key_of[24], (D, FF), D ** -0.5, 0.1875, ((0, 8), (1, 16))),
        "second_value": gaussian(key_of[25], (D, FF), D ** -0.5, 0.1875, ((0, 8), (1, 16))),
        "second_down": gaussian(key_of[26], (FF, D), (FF // 4) ** -0.5, 0.21875, ((0, 16), (1, 8))),
    }


PRECISE = lax.Precision.HIGHEST

@jax.custom_vjp
def low(v):
    return lax.optimization_barrier(v.astype(jnp.bfloat16)).astype(jnp.float32)

@jax.custom_vjp
def low_back(v):
    return v

def low_keep(v):
    return (low(v), None)

def low_pass(kept, grad):
    return (grad,)

def back_keep(v):
    return (v, None)

def back_low(kept, grad):
    return (low(grad),)
low.defvjp(low_keep, low_pass)
low_back.defvjp(back_keep, back_low)

def matmul(left, right):
    return jnp.dot(left, right, precision=PRECISE)

def rmsnorm(values, norm_gain):
    return values * lax.rsqrt(lax.optimization_barrier(jnp.mean(values * values, axis=-1, keepdims=True)) + 1e-06) * norm_gain

def gelu(values):
    return jax.nn.gelu(values, approximate=True)

def angle_tables(position, head_size):
    half_size = head_size // 2
    frequency = 10000.0 ** (-2.0 * jnp.arange(half_size, dtype=jnp.float32) / head_size)
    angle_table = position.astype(jnp.float32)[:, None] * frequency[None, :]
    return (jnp.cos(angle_table), jnp.sin(angle_table))

def rotate(values, cosine, sine_table):
    half_size = values.shape[-1] // 2
    front_half = values[..., :half_size]
    back_half = values[..., half_size:]
    return jnp.concatenate([front_half * cosine - back_half * sine_table, back_half * cosine + front_half * sine_table], axis=-1)

def recurrence(mixture, position, kernel, conv_shift, decay_weight, decay_offset, input_weight, input_offset, decay_param):
    group_rows = mixture.shape[0]
    convolved = conv_shift + kernel[0] * mixture
    for offset in range(1, kernel.shape[0]):
        lagged = jnp.concatenate([jnp.zeros((offset, mixture.shape[1]), mixture.dtype), mixture[:-offset]], axis=0)
        convolved = convolved + kernel[offset] * lagged * (position >= offset).astype(mixture.dtype)[:, None]
    blocks = convolved.reshape(group_rows, decay_weight.shape[0], decay_weight.shape[1])
    reset_rate = jax.nn.sigmoid(jnp.einsum('tnb,nbc->tnc', blocks, decay_weight, precision=PRECISE).reshape(group_rows, -1) + decay_offset)
    opened = jax.nn.sigmoid(jnp.einsum('tnb,nbc->tnc', blocks, input_weight, precision=PRECISE).reshape(group_rows, -1) + input_offset)
    log_decay = -8.0 * reset_rate * jax.nn.softplus(-decay_param)
    factor = jnp.where((position > 0)[:, None], jnp.exp(log_decay), 0.0)
    driven = jnp.sqrt(-jnp.expm1(2.0 * log_decay)) * opened * convolved

    def combine(earlier, latter):
        return (earlier[0] * latter[0], latter[0] * earlier[1] + latter[1])
    return lax.associative_scan(combine, (factor, driven), axis=0)[1]

def feedforward(values, norm_gain, gate_weight, value_weight, down_weight):
    normed = low(rmsnorm(values, norm_gain))
    pre_gate = low_back(matmul(normed, gate_weight))
    pre_value = low_back(matmul(normed, value_weight))
    hidden = low(gelu(pre_gate) * pre_value)
    return values + low_back(matmul(hidden, down_weight))

def attention(values, length, position, norm_gain, query_proj, key_proj, value_proj, attn_output):
    normed = low(rmsnorm(values, norm_gain))
    cosine, sine_table = angle_tables(position, HD)
    queries = low_back(matmul(normed, query_proj)).reshape(GROUP, H, HD)
    queries = low(rotate(queries, cosine[:, None, :], sine_table[:, None, :]) / math.sqrt(HD))
    key_rows = low(rotate(low_back(matmul(normed, key_proj)), cosine, sine_table))
    value_rows = low(low_back(matmul(normed, value_proj)))
    padding = jnp.zeros((WINDOW, HD), key_rows.dtype)
    padded_keys = jnp.concatenate([padding, key_rows], axis=0)
    padded_values = jnp.concatenate([padding, value_rows], axis=0)
    block_rows = min(512, GROUP)

    def one_block(first_row):
        query_block = lax.dynamic_slice_in_dim(queries, first_row, block_rows, 0)
        key_block = lax.dynamic_slice_in_dim(padded_keys, first_row, block_rows + WINDOW, 0)
        value_block = lax.dynamic_slice_in_dim(padded_values, first_row, block_rows + WINDOW, 0)
        row_index = first_row + jnp.arange(block_rows, dtype=jnp.int32)
        col_index = first_row - WINDOW + jnp.arange(block_rows + WINDOW, dtype=jnp.int32)
        allowed = (col_index[None, :] >= 0) & (row_index[:, None] >= col_index[None, :])
        allowed = allowed & (row_index[:, None] - col_index[None, :] < WINDOW)
        allowed = allowed & ((row_index >= length)[:, None] == (col_index >= length)[None, :])
        scores = low_back(jnp.einsum('qhd,kd->hqk', query_block, key_block, precision=PRECISE))
        scores = jnp.where(allowed[None], scores, -1e+30)
        row_max = lax.optimization_barrier(jnp.max(scores, axis=-1, keepdims=True))
        weights = jnp.exp(scores - row_max)
        attn_probs = low(weights / lax.optimization_barrier(jnp.sum(weights, axis=-1, keepdims=True)))
        return jnp.einsum('hqk,kd->qhd', attn_probs, value_block, precision=PRECISE)
    starts = jnp.arange(GROUP // block_rows, dtype=jnp.int32) * block_rows
    mixture = lax.map(jax.checkpoint(one_block), starts).reshape(GROUP, H * HD)
    mixture = low(low_back(mixture))
    return low_back(matmul(mixture, attn_output))

def group_forward(inputs, length, params):
    norm_one, recur_input, recur_gate, conv_kernel, conv_bias, decay_gate, decay_shift, input_gate, input_shift, decay_param, recur_output, norm_two, first_gate, first_value, first_down, norm_three, query_proj, key_proj, value_proj, attn_output, norm_four, second_gate, second_value, second_down = params
    row_index = jnp.arange(GROUP, dtype=jnp.int32)
    segment = (row_index >= length).astype(jnp.int32)
    position = row_index - segment * length
    normed = low(rmsnorm(inputs, norm_one))
    mixture = low_back(matmul(normed, recur_input))
    gating = low_back(matmul(normed, recur_gate))
    hidden_state = recurrence(mixture, position, conv_kernel, conv_bias, decay_gate, decay_shift, input_gate, input_shift, decay_param)
    gated = low(gelu(gating) * hidden_state)
    current = inputs + low_back(matmul(gated, recur_output))
    current = feedforward(current, norm_two, first_gate, first_value, first_down)
    current = current + attention(current, length, position, norm_three, query_proj, key_proj, value_proj, attn_output)
    return feedforward(current, norm_four, second_gate, second_value, second_down)

def reference(tokens, lengths, cotangent, norm_one, recur_input, recur_gate, conv_kernel, conv_bias, decay_gate, decay_shift, input_gate, input_shift, decay_param, recur_output, norm_two, first_gate, first_value, first_down, norm_three, query_proj, key_proj, value_proj, attn_output, norm_four, second_gate, second_value, second_down):
    weights_in = (norm_one, recur_input, recur_gate, conv_kernel, conv_bias, decay_gate, decay_shift, input_gate, input_shift, decay_param, recur_output, norm_two, first_gate, first_value, first_down, norm_three, query_proj, key_proj, value_proj, attn_output, norm_four, second_gate, second_value, second_down)
    params = tuple((member.astype(jnp.float32) for member in weights_in))
    inputs = tokens.astype(jnp.float32)

    def forward(inputs, params):
        grouped = inputs.reshape(N_DP, GROUP, D)

        def one_group(grouped_item):
            return group_forward(grouped_item[0], grouped_item[1], params)
        results = lax.map(jax.checkpoint(one_group), (grouped, lengths))
        return results.reshape(TOKENS, D)
    outputs, pullback = jax.vjp(forward, inputs, params)
    grad_inputs, gradients = pullback(cotangent.astype(jnp.float32))
    return (outputs, grad_inputs, gradients[0], gradients[1], gradients[2], gradients[3], gradients[4], gradients[5], gradients[6], gradients[7], gradients[8], gradients[9], gradients[10], gradients[11], gradients[12], gradients[13], gradients[14], gradients[15], gradients[16], gradients[17], gradients[18], gradients[19], gradients[20], gradients[21], gradients[22], gradients[23])
```

```python
import math
from types import SimpleNamespace

import jax
import jax.numpy as jnp
from jax import lax
from jax.experimental import pallas as pl
from jax.experimental.pallas import tpu as pltpu
from jax.sharding import PartitionSpec as P

MESH = pl.DeviceIdType.MESH
F32 = jnp.float32
BF16 = jnp.bfloat16
PRECISE = lax.Precision.HIGHEST
VMEM_BYTES = 63 * 2**20

D = 1024
ROWS = 128
SPAN = 512
LANE = 128
BW = 96
CH = 4 * LANE
PAR = 208
VEC = 192
UNITS = 768
HEADS = 8
HD = 128
WINDOW = 1024
KEYS = 1152
PAIR = 1152
CHUNK = 64
ORDER = (0, 1, 3, 2)
GELU_C = math.sqrt(2.0 / math.pi)


def place():
    dp, mp = lax.axis_index("dp"), lax.axis_index("mp")
    return dp // 2, dp % 2, mp // 4, mp % 4


def z_peer(d):
    _, _, y, z = place()
    return {"mp": y * 4 + (z + d) % 4}


def y_peer(d):
    _, _, y, z = place()
    return {"mp": ((y + d) % 4) * 4 + z}


def xc_peer(dx, dc):
    x, c, _, _ = place()
    return {"dp": ((x + dx) % 4) * 2 + (c + dc) % 2}


def row_peer(offset):
    return {"mp": lax.rem(lax.axis_index("mp") + 16 + offset, 16)}


def all_peers(window):
    peers = [xc_peer(0, 1)]
    for d in (1, 2, 3):
        peers += [xc_peer(d, 0), y_peer(d), z_peer(d)]
    if window:
        for o in range(1, 9):
            peers += [row_peer(o), row_peer(-o)]
    return peers


def greet(peers):
    barrier = pltpu.get_barrier_semaphore()
    for peer in peers:
        pl.semaphore_signal(barrier, inc=1, device_id=peer, device_id_type=MESH)
    return lambda: pl.semaphore_wait(barrier, len(peers))


class Net:
    def __init__(self, send, recv):
        self.send, self.recv, self.used, self.started = send, recv, 0, []

    def make(self, src, dst, peer):
        copy = pltpu.make_async_remote_copy(
            src_ref=src,
            dst_ref=dst,
            send_sem=self.send.at[self.used],
            recv_sem=self.recv.at[self.used],
            device_id=peer,
            device_id_type=MESH,
        )
        self.used += 1
        return copy

    def push(self, src, dst, peer):
        copy = self.make(src, dst, peer)
        copy.start()
        self.started.append(copy)
        return copy

    def drain(self):
        for copy in self.started:
            copy.wait_send()


class Local:
    def __init__(self, sems):
        self.sems, self.used, self.stores = sems, 0, []

    def load(self, src, dst):
        copy = pltpu.make_async_copy(src, dst, self.sems.at[self.used])
        self.used += 1
        copy.start()
        return copy

    def store(self, src, dst):
        self.stores.append(self.load(src, dst))

    def drain(self):
        for copy in self.stores:
            copy.wait()


def run(body, ins, outs, scratch, collective_id=None, flops=0):
    names = [n for n, _, _ in ins] + [n for n, _, _, _ in outs] + [n for n, _ in scratch]
    space = {"near": pltpu.VMEM, "far": pl.ANY}

    def kernel(*refs):
        body(SimpleNamespace(**dict(zip(names, refs))))

    results = pl.pallas_call(
        kernel,
        out_shape=[jax.ShapeDtypeStruct(s, t) for _, s, t, _ in outs],
        in_specs=[pl.BlockSpec(memory_space=space[where]) for _, _, where in ins],
        out_specs=[pl.BlockSpec(memory_space=space[where]) for _, _, _, where in outs],
        scratch_shapes=[s for _, s in scratch],
        compiler_params=pltpu.CompilerParams(
            collective_id=collective_id,
            has_side_effects=collective_id is not None,
            vmem_limit_bytes=VMEM_BYTES,
        ),
        cost_estimate=pl.CostEstimate(flops=flops, bytes_accessed=2**24, transcendentals=0),
    )(*[a for _, a, _ in ins])
    return dict(zip([n for n, _, _, _ in outs], results))


def vm(shape, dtype):
    return pltpu.VMEM(shape, dtype)


def dma(n):
    return pltpu.SemaphoreType.DMA((n,))


def dot_nn(a, b, **kw):
    return lax.dot_general(a, b, (((1,), (0,)), ((), ())), preferred_element_type=F32, **kw)


def dot_nt(a, b, **kw):
    return lax.dot_general(a, b, (((1,), (1,)), ((), ())), preferred_element_type=F32, **kw)


def dot_tn(a, b, **kw):
    return lax.dot_general(a, b, (((0,), (0,)), ((), ())), preferred_element_type=F32, **kw)


def gelu(v):
    return 0.5 * v * (1.0 + jnp.tanh(GELU_C * (v + 0.044715 * v * v * v)))


def gelu_both(v):
    t = jnp.tanh(GELU_C * (v + 0.044715 * v * v * v))
    value = 0.5 * v * (1.0 + t)
    slope = 0.5 * (1.0 + t) + 0.5 * v * (1.0 - t * t) * GELU_C * (1.0 + 3.0 * 0.044715 * v * v)
    return value, slope


def rms(v, gain):
    return v * lax.rsqrt(jnp.mean(v * v, axis=-1, keepdims=True) + 1e-06) * gain


def rms_back(dn, v, gain):
    r = lax.rsqrt(jnp.mean(v * v, axis=-1, keepdims=True) + 1e-06)
    grad_gain = jnp.sum(dn * v * r, axis=0, keepdims=True)
    dg = dn * gain
    dv = r * dg - v * (r * r * r) * jnp.mean(dg * v, axis=-1, keepdims=True)
    return dv, grad_gain


def rows_at(first, count):
    return pl.ds(pl.multiple_of(first, count), count)


class Gatherer:
    def __init__(self, net, own, whole):
        self.net, self.own, self.whole, self.half = net, own, whole, whole.shape[3] // 2

    def start(self):
        x, c, y, _ = place()
        one, two = slice(0, self.half), slice(self.half, 2 * self.half)
        self.whole[c, x, y] = self.own[...]
        self.first = []
        for d in (1, 3, 2):
            for part, peer in ((one, xc_peer(d, 0)), (two, y_peer(d))):
                self.first.append(
                    self.net.push(self.own.at[part, :], self.whole.at[c, x, y, part, :], peer)
                )

    def along(self):
        x, c, y, _ = place()
        one, two = slice(0, self.half), slice(self.half, 2 * self.half)
        for copy in self.first:
            copy.wait_recv()
        self.second = []
        for d in (1, 3, 2):
            mine = self.whole.at[c, :, y, one, :]
            self.second.append(self.net.push(mine, mine, y_peer(d)))
            mine = self.whole.at[c, x, :, two, :]
            self.second.append(self.net.push(mine, mine, xc_peer(d, 0)))

    def across(self):
        _, c, _, _ = place()
        for copy in self.second:
            copy.wait_recv()
        mine = self.whole.at[c]
        self.third = self.net.push(mine, mine, xc_peer(0, 1))

    def finish(self):
        self.third.wait_recv()


class Reducer:
    @staticmethod
    def scratch(name, rows, lanes):
        half = rows // 2
        return [
            (name + "_other", vm((4, 4, rows, lanes), BF16)),
            (name + "_in_a", vm((3, 4, half, lanes), BF16)),
            (name + "_in_b", vm((3, 4, half, lanes), BF16)),
            (name + "_sum_a", vm((4, half, lanes), BF16)),
            (name + "_sum_b", vm((4, half, lanes), BF16)),
            (name + "_last_a", vm((3, half, lanes), BF16)),
            (name + "_last_b", vm((3, half, lanes), BF16)),
        ]

    def __init__(self, net, src, r, name):
        self.net, self.src, self.half = net, src, src.shape[3] // 2
        for part in ("other", "in_a", "in_b", "sum_a", "sum_b", "last_a", "last_b"):
            setattr(self, part, getattr(r, name + "_" + part))

    def start(self):
        _, c, _, _ = place()
        self.first = self.net.push(self.src.at[1 - c], self.other, xc_peer(0, 1))

    def along_one(self):
        x, c, y, _ = place()
        half = self.half
        self.first.wait_recv()

        def add(i, _):
            a, b = i // 4, i % 4
            total = self.src[c, a, b].astype(F32) + self.other[a, b].astype(F32)
            self.other[a, b] = total.astype(BF16)
            return 0

        lax.fori_loop(0, 16, add, 0)
        self.second = []
        for d in (1, 3, 2):
            mine = self.other.at[(x + d) % 4, :, 0:half, :]
            self.second.append(self.net.push(mine, self.in_a.at[d - 1], xc_peer(d, 0)))
            mine = self.other.at[:, (y + d) % 4, half : 2 * half, :]
            self.second.append(self.net.push(mine, self.in_b.at[d - 1], y_peer(d)))

    def along_two(self):
        x, _, y, _ = place()
        half = self.half
        for copy in self.second:
            copy.wait_recv()

        def add(i, _):
            a = self.other[x, i, 0:half, :].astype(F32)
            b = self.other[i, y, half : 2 * half, :].astype(F32)
            for d in range(3):
                a = a + self.in_a[d, i].astype(F32)
                b = b + self.in_b[d, i].astype(F32)
            self.sum_a[i] = a.astype(BF16)
            self.sum_b[i] = b.astype(BF16)
            return 0

        lax.fori_loop(0, 4, add, 0)
        self.third = []
        for d in (1, 3, 2):
            mine = self.sum_a.at[(y + d) % 4]
            self.third.append(self.net.push(mine, self.last_a.at[d - 1], y_peer(d)))
            mine = self.sum_b.at[(x + d) % 4]
            self.third.append(self.net.push(mine, self.last_b.at[d - 1], xc_peer(d, 0)))

    def finish(self):
        x, _, y, _ = place()
        for copy in self.third:
            copy.wait_recv()
        a = self.sum_a[y].astype(F32)
        b = self.sum_b[x].astype(F32)
        for d in range(3):
            a = a + self.last_a[d].astype(F32)
            b = b + self.last_b[d].astype(F32)
        return a, b


def spread_z(net, ref):
    z = place()[3]
    return {d: net.push(ref.at[z], ref.at[z], z_peer(d)) for d in (1, 3, 2)}


def place_units(local, whole, w_ref):
    copies = []
    for part in range(8):
        for y in range(4):
            for w in range(3):
                copies.append(
                    local.load(
                        whole.at[part % 2, part // 2, y, w * 192 : (w + 1) * 192, :],
                        w_ref.at[
                            w, y * 192 : (y + 1) * 192, part * LANE : (part + 1) * LANE
                        ],
                    )
                )
    return copies


def unit_grads(sides, out):
    for w, (left, right) in enumerate(sides):
        right = right[...].reshape(SPAN, D)
        for tile in range(3):
            cut = left[:, :, tile * 256 : tile * 256 + 256].reshape(SPAN, 256)
            grad = dot_tn(cut, right)
            first = tile * 256
            while first < tile * 256 + 256:
                block = first // 192
                last = min((block + 1) * 192, tile * 256 + 256)
                rows = grad[first - tile * 256 : last - tile * 256]
                start = w * 192 + first - block * 192
                for part in range(8):
                    out[part % 2, part // 2, block, start : start + last - first, :] = rows[
                        :, part * LANE : (part + 1) * LANE
                    ].astype(BF16)
                first = last


def positions(length, first, rows):
    t = lax.broadcasted_iota(jnp.int32, (rows, CH), 0) + first
    wide = jnp.concatenate([length[...]] * 4, axis=1)
    return jnp.where(t >= wide, t - wide, t)


def lanes_of(pr, row):
    return jnp.concatenate([pr[b, row : row + 1, :] for b in range(4)], axis=1)


def neg_expm1(v):
    series = v * (
        1.0 + v * (0.5 + v * (1.0 / 6 + v * (1.0 / 24 + v * (1.0 / 120 + v * (1.0 / 720)))))
    )
    return -jnp.where(v > -0.25, series, jnp.exp(v) - 1.0)


def share_edges(net, edges, prod, last):
    y = place()[2]
    edges[y, 0:1, :] = prod
    edges[y, 1:2, :] = last
    return [net.push(edges.at[y], edges.at[y], y_peer(d)) for d in (1, 3, 2)]


def forward_body(r):
    x, c, y, z = place()
    mp = lax.axis_index("mp")
    ready = greet(all_peers(True))
    net, loc = Net(r.send, r.recv), Local(r.sems)

    tokens = r.tok[...].astype(F32)
    r.n1[z] = rms(tokens, r.gain_one[...]).astype(BF16)
    mine = pl.ds(pl.multiple_of(y * LANE, LANE), BW)
    r.wr[0, mine, :] = r.recur_input[...]
    r.wr[1, mine, :] = r.recur_gate[...]
    r.wr[2, mine, :] = r.recur_output[...]
    for b in range(4):
        r.wr[:, b * LANE + BW : (b + 1) * LANE, :] = jnp.zeros((3, LANE - BW, D), BF16)
    r.pr[y] = jnp.zeros((PAR, LANE), F32)
    r.pr[y, 0:BW, 0:BW] = r.decay_gate[0]
    r.pr[y, BW : 2 * BW, 0:BW] = r.input_gate[0]
    r.pr[y, VEC : VEC + 4, 0:BW] = r.conv_kernel[...]
    r.pr[y, VEC + 4 : VEC + 5, 0:BW] = r.conv_bias[...]
    r.pr[y, VEC + 5 : VEC + 6, 0:BW] = r.decay_shift[...]
    r.pr[y, VEC + 6 : VEC + 7, 0:BW] = r.input_shift[...]
    r.pr[y, VEC + 7 : VEC + 8, :] = jnp.ones((1, LANE), F32)
    r.pr[y, VEC + 7 : VEC + 8, 0:BW] = r.softplus[...]
    ready()
    gather_n1 = spread_z(net, r.n1)
    half = pl.ds(pl.multiple_of(c * 512, 512), 512)
    part_p = pl.ds(pl.multiple_of(c * 104, 8), 104)
    weights_in, shared = {}, []
    for d in (1, 3, 2):
        cut = r.wr.at[0:2, mine, half]
        weights_in[d, 0] = net.push(cut, cut, y_peer(d))
    for d in (1, 3, 2):
        cut = r.pr.at[y, part_p, :]
        weights_in[d, 1] = net.push(cut, cut, y_peer(d))
    for d in (1, 3, 2):
        cut = r.wr.at[2, mine, half]
        weights_in[d, 2] = net.push(cut, cut, y_peer(d))

    r.own_first[0:192, :] = r.first_gate[...]
    r.own_first[192:384, :] = r.first_value[...]
    r.own_first[384:576, :] = r.first_down[...]
    left = jnp.concatenate([r.query_proj[...], r.key_proj[...]], axis=1).astype(F32)
    right = jnp.concatenate([r.value_proj[...], r.attn_output[...]], axis=1).astype(F32)
    r.own_attn[rows_at(z * 16, 16), :] = jnp.concatenate([left, right], axis=0).astype(BF16)
    cut = r.own_attn.at[rows_at(z * 16, 16), :]
    attn_z = [net.push(cut, cut, z_peer(d)) for d in (1, 3, 2)]
    first_w = Gatherer(net, r.own_first, r.all_first)
    attn_w = Gatherer(net, r.own_attn, r.all_attn)
    second_w = Gatherer(net, r.own_second, r.all_second)
    first_w.start()
    r.own_second[0:192, :] = r.second_gate[...]
    r.own_second[192:384, :] = r.second_value[...]
    r.own_second[384:576, :] = r.second_down[...]

    def pass_on(kind):
        for d in (1, 3, 2):
            weights_in[d, kind].wait_recv()
            block = (y + 4 - d) % 4
            rows = pl.ds(pl.multiple_of(block * LANE, LANE), BW)
            if kind == 0:
                cut = r.wr.at[0:2, rows, half]
            elif kind == 1:
                cut = r.pr.at[block, part_p, :]
            else:
                cut = r.wr.at[2, rows, half]
            shared.append((kind, net.push(cut, cut, xc_peer(0, 1))))

    def arrived(kind):
        for k, copy in shared:
            if k == kind:
                copy.wait_recv()

    pass_on(0)
    pass_on(1)
    for d in (1, 3, 2):
        gather_n1[d].wait_recv()
    arrived(0)
    rows_n = r.n1[...].reshape(SPAN, D)
    r.mix[8:, :] = dot_nt(rows_n, r.wr[0])

    @pl.when(y == 0)
    def _():
        r.mix[0:8, :] = jnp.zeros((8, CH), F32)

    halo = net.make(r.mix.at[SPAN : SPAN + 8], r.mix.at[0:8], y_peer(1))

    @pl.when(y < 3)
    def _():
        halo.start()

    r.gate[...] = dot_nt(rows_n, r.wr[1])
    loc.store(r.gate, r.out_gate)
    loc.store(r.n1, r.out_n1)
    for copy in attn_z:
        copy.wait_recv()
    attn_w.start()
    first_w.along()
    arrived(1)
    pass_on(2)

    @pl.when(y > 0)
    def _():
        halo.wait_recv()

    loc.store(r.mix, r.out_mix)
    loc.store(r.pr, r.out_pr)

    def conv_chunk(i, _):
        first = pl.multiple_of(i * CHUNK, CHUNK)
        pos = positions(r.length, y * SPAN + first, CHUNK)
        window = r.mix[pl.ds(first, CHUNK + 8), :]
        total = lanes_of(r.pr, VEC + 4) + lanes_of(r.pr, VEC) * window[8:, :]
        for k in (1, 2, 3):
            lagged = window[8 - k : 8 - k + CHUNK, :]
            total = total + jnp.where(pos >= k, lanes_of(r.pr, VEC + k) * lagged, 0.0)
        r.conv[pl.ds(first, CHUNK), :] = total
        return 0

    lax.fori_loop(0, SPAN // CHUNK, conv_chunk, 0)
    loc.store(r.conv, r.out_conv)
    for b in range(4):
        cols = slice(b * LANE, (b + 1) * LANE)
        left = r.conv[:, b * LANE : b * LANE + BW]
        r.rate[:, cols] = dot_nn(left, r.pr[b, 0:BW, :], precision=PRECISE)
        r.opened[:, cols] = dot_nn(left, r.pr[b, BW : 2 * BW, :], precision=PRECISE)

    def gates_chunk(i, _):
        first = pl.multiple_of(i * CHUNK, CHUNK)
        rows = pl.ds(first, CHUNK)
        pos = positions(r.length, y * SPAN + first, CHUNK)
        rate = jax.nn.sigmoid(r.rate[rows, :] + lanes_of(r.pr, VEC + 5))
        opened = jax.nn.sigmoid(r.opened[rows, :] + lanes_of(r.pr, VEC + 6))
        loga = -8.0 * rate * lanes_of(r.pr, VEC + 7)
        r.rate[rows, :] = rate
        r.opened[rows, :] = opened
        r.fac[rows, :] = jnp.where(pos > 0, jnp.exp(loga), 0.0)
        r.state[pl.ds(first + 8, CHUNK), :] = (
            jnp.sqrt(neg_expm1(2.0 * loga)) * opened * r.conv[rows, :]
        )
        return 0

    lax.fori_loop(0, SPAN // CHUNK, gates_chunk, 0)
    loc.store(r.rate, r.out_rate)
    loc.store(r.opened, r.out_opened)
    row = lax.broadcasted_iota(jnp.int32, (8, CH), 0)

    def step(i, carry):
        held, prod = carry
        rows = rows_at(i * 8, 8)
        srows = rows_at(i * 8 + 8, 8)
        a = r.fac[rows, :]
        h = r.state[srows, :]
        for s in (1, 2, 4):
            h = h + a * jnp.where(row >= s, pltpu.roll(h, s, 0), 0.0)
            a = a * jnp.where(row >= s, pltpu.roll(a, s, 0), 1.0)
        h = h + a * held
        a = a * prod
        r.state[srows, :] = h
        r.acum[rows, :] = a
        return h[7:8, :], a[7:8, :]

    zero = jnp.zeros((1, CH), F32)
    last_h, last_a = lax.fori_loop(0, SPAN // 8, step, (zero, zero + 1.0), unroll=4)
    edges_in = share_edges(net, r.edges, last_a, last_h)
    first_w.across()
    arrived(2)
    loc.store(r.wr, r.out_wr)
    for copy in edges_in:
        copy.wait_recv()
    held = zero
    for b in range(3):
        held = jnp.where(b < y, r.edges[b, 0:1, :] * held + r.edges[b, 1:2, :], held)
    r.state[0:8, :] = jnp.broadcast_to(held, (8, CH))

    def gated_chunk(i, _):
        first = pl.multiple_of(i * CHUNK, CHUNK)
        rows = pl.ds(first, CHUNK)
        srows = pl.ds(first + 8, CHUNK)
        state = r.state[srows, :] + r.acum[rows, :] * held
        r.state[srows, :] = state
        r.gated[rows, :] = (gelu(r.gate[rows, :]) * state).astype(BF16)
        return 0

    lax.fori_loop(0, SPAN // CHUNK, gated_chunk, 0)
    loc.store(r.state, r.out_state)
    loc.store(r.gated, r.out_gated)
    back = {}
    for d in (1, 3, 2, 0):
        s = (z + 4 - d) % 4
        term = dot_nn(r.gated[rows_at(s * ROWS, ROWS), :], r.wr[2])
        if d:
            r.part1[d - 1] = term.astype(BF16)
            back[d] = net.push(r.part1.at[d - 1], r.recv1.at[d - 1], z_peer(4 - d))
        else:
            r.x1[...] = tokens + term
    attn_w.along()
    first_w.finish()
    placed = place_units(loc, r.all_first, r.w1)
    second_w.start()
    total = r.x1[...]
    for d in (1, 3, 2):
        back[d].wait_recv()
        total = total + r.recv1[d - 1].astype(F32)
    r.x1[...] = total

    r.n2[z] = rms(total, r.gain_two[...]).astype(BF16)
    gather_n2 = spread_z(net, r.n2)
    loc.store(r.x1, r.out_x1)
    for copy in placed:
        copy.wait()
    loc.store(r.w1, r.out_w1)
    back = {}
    for d in ORDER:
        s = (z + 4 - d) % 4
        if d:
            gather_n2[d].wait_recv()
        nb = r.n2[s]
        pg = dot_nt(nb, r.w1[0])
        pu = dot_nt(nb, r.w1[1])
        r.pg[s] = pg
        r.pu[s] = pu
        term = dot_nn((gelu(pg) * pu).astype(BF16), r.w1[2])
        if d == 0:
            r.x2[...] = total + term
            attn_w.across()
            second_w.along()
        else:
            r.part2[d - 1] = term.astype(BF16)
            back[d] = net.push(r.part2.at[d - 1], r.recv2.at[d - 1], z_peer(4 - d))
    loc.store(r.n2, r.out_n2)
    loc.store(r.pg, r.out_pg)
    loc.store(r.pu, r.out_pu)
    attn_w.finish()

    def split(i, _):
        a, b, e = i // 16, (i // 4) % 4, i % 4
        block = r.all_attn[a, b, e].astype(F32).reshape(4, 16, PAIR)
        rows = rows_at((b * 2 + a) * 128 + e * 32, 32)
        r.wa[0, rows, :] = block[:, 0:8, :].reshape(32, PAIR).astype(BF16)
        r.wa[1, rows, :] = block[:, 8:16, :].reshape(32, PAIR).astype(BF16)
        return 0

    lax.fori_loop(0, 32, split, 0)
    loc.store(r.wa, r.out_wa)
    second_w.across()
    total = r.x2[...]
    for d in (1, 3, 2):
        back[d].wait_recv()
        total = total + r.recv2[d - 1].astype(F32)
    r.x2[...] = total
    loc.store(r.x2, r.out_x2)

    n = rms(total, r.gain_three[...]).astype(BF16)
    r.n3[...] = n
    cosine = r.cosine[...]
    sine = r.sine[...]
    swap = lambda v: pltpu.roll(v, HD // 2, 1)
    key = dot_nn(n, r.wa[0, :, D:])
    r.kv[8, :, :HD] = (key * cosine + swap(key) * sine).astype(BF16)
    r.kv[8, :, HD:] = dot_nn(n, r.wa[1, :, :HD]).astype(BF16)
    copies = []
    for o in range(1, 9):
        copy = net.make(r.kv.at[8], r.kv.at[8 - o], row_peer(o))
        copies.append(copy)

        @pl.when(mp + o < 16)
        def _():
            copy.start()

        @pl.when(mp < o)
        def _():
            r.kv[8 - o] = jnp.zeros((ROWS, 2 * HD), BF16)

    r.c_all[z] = r.cot[...]
    gather_c = spread_z(net, r.c_all)
    loc.store(r.n3, r.out_n3)
    for h in range(HEADS):
        cols = slice(h * HD, (h + 1) * HD)
        query = dot_nn(n, r.wa[0, :, cols])
        r.q[h] = ((query * cosine + swap(query) * sine) * (1.0 / math.sqrt(HD))).astype(BF16)
    loc.store(r.q, r.out_q)
    row = lax.broadcasted_iota(jnp.int32, (ROWS, KEYS), 0)
    col = lax.broadcasted_iota(jnp.int32, (ROWS, KEYS), 1) - (KEYS - ROWS)
    base = mp * ROWS
    length = jnp.concatenate([r.length[...]] * 9, axis=1)
    allowed = (col + base >= 0) & (row >= col) & (row - col < WINDOW)
    allowed = allowed & ((row + base >= length) == (col + base >= length))
    bias = jnp.where(allowed, 0.0, -1e30)
    for o in range(1, 9):

        @pl.when(mp >= o)
        def _():
            copies[o - 1].wait_recv()

    loc.store(r.kv, r.out_kv)
    pairs = r.kv[...].reshape(KEYS, 2 * HD)
    for h in range(HEADS):
        cols = slice(h * HD, (h + 1) * HD)
        s = dot_nt(r.q[h], pairs[:, :HD]) + bias
        e = jnp.exp(s - jnp.max(s, axis=-1, keepdims=True))
        p = (e / jnp.sum(e, axis=-1, keepdims=True)).astype(BF16)
        r.pb[h] = p
        r.att[:, cols] = dot_nn(p, pairs[:, HD:]).astype(BF16)
    loc.store(r.pb, r.out_pb)
    loc.store(r.att, r.out_att)
    r.x3[...] = total + dot_nn(r.att[...], r.wa[1, :, HD:])
    loc.store(r.x3, r.out_x3)
    second_w.finish()
    loc.store(r.all_second, r.out_w2)
    for d in (1, 3, 2):
        gather_c[d].wait_recv()
    loc.store(r.c_all, r.out_c)
    loc.drain()
    net.drain()
    for o in range(1, 9):

        @pl.when(mp + o < 16)
        def _():
            copies[o - 1].wait_send()

    @pl.when(y < 3)
    def _():
        halo.wait_send()


BIG = ((SPAN, CH), F32)
TALL = ((SPAN + 8, CH), F32)
SAVED = {
    "n1": ((4, ROWS, D), BF16),
    "wr": ((3, CH, D), BF16),
    "pr": ((4, PAR, LANE), F32),
    "mix": TALL,
    "gate": BIG,
    "conv": BIG,
    "rate": BIG,
    "opened": BIG,
    "state": TALL,
    "gated": ((SPAN, CH), BF16),
    "x1": ((ROWS, D), F32),
    "w1": ((3, UNITS, D), BF16),
    "n2": ((4, ROWS, D), BF16),
    "pg": ((4, ROWS, UNITS), F32),
    "pu": ((4, ROWS, UNITS), F32),
    "x2": ((ROWS, D), F32),
    "wa": ((2, D, PAIR), BF16),
    "n3": ((ROWS, D), BF16),
    "q": ((HEADS, ROWS, HD), BF16),
    "kv": ((9, ROWS, 2 * HD), BF16),
    "pb": ((HEADS, ROWS, KEYS), BF16),
    "att": ((ROWS, D), BF16),
    "x3": ((ROWS, D), F32),
}
BLOCKS = ((2, 4, 4, 576, LANE), BF16)


def forward(inputs):
    outs = [("out_" + k, *v, "far") for k, v in SAVED.items()]
    outs += [("out_w2", *BLOCKS, "far"), ("out_c", (4, ROWS, D), BF16, "far")]
    scratch = [(k, vm(*v)) for k, v in SAVED.items()]
    scratch += [
        ("fac", vm(*BIG)),
        ("acum", vm(*BIG)),
        ("edges", vm((4, 8, CH), F32)),
        ("part1", vm((3, ROWS, D), BF16)),
        ("recv1", vm((3, ROWS, D), BF16)),
        ("part2", vm((3, ROWS, D), BF16)),
        ("recv2", vm((3, ROWS, D), BF16)),
        ("own_first", vm((576, LANE), BF16)),
        ("own_second", vm((576, LANE), BF16)),
        ("own_attn", vm((64, PAIR), BF16)),
        ("all_first", vm(*BLOCKS)),
        ("all_second", vm(*BLOCKS)),
        ("all_attn", vm((2, 4, 4, 64, PAIR), BF16)),
        ("c_all", vm((4, ROWS, D), BF16)),
        ("send", dma(100)),
        ("recv", dma(100)),
        ("sems", dma(128)),
    ]
    return run(
        forward_body, [(k, v, "near") for k, v in inputs.items()], outs, scratch, 1, 10**10
    )


def middle_body(r):
    _, _, _, z = place()
    mp = lax.axis_index("mp")
    ready = greet(all_peers(True))
    net, loc = Net(r.send, r.recv), Local(r.sems)
    placed = place_units(loc, r.far_w2, r.w2)
    c_in = loc.load(r.far_c, r.c_all)
    attn_in = [
        loc.load(getattr(r, "far_" + k), getattr(r, k))
        for k in ("wa", "kv", "pb", "q", "att", "n3", "x2")
    ]
    x = r.x3[...]
    r.n4[z] = rms(x, r.gain_four[...]).astype(BF16)
    ready()
    gather_n = spread_z(net, r.n4)
    c = r.cot[...].astype(F32)
    for copy in placed:
        copy.wait()
    c_in.wait()
    back_d, back_o = {}, {}
    for d in ORDER:
        s = (z + 4 - d) % 4
        if d:
            gather_n[d].wait_recv()
        nb = r.n4[s]
        pg = dot_nt(nb, r.w2[0])
        pu = dot_nt(nb, r.w2[1])
        act, slope = gelu_both(pg)
        r.hid[s] = (act * pu).astype(BF16)
        dh = dot_nt(r.c_all[s], r.w2[2])
        dpg = (dh * pu * slope).astype(BF16)
        dpu = (dh * act).astype(BF16)
        r.dpg[s] = dpg
        r.dpu[s] = dpu
        term = dot_nn(dpg, r.w2[0]) + dot_nn(dpu, r.w2[1])
        if d == 0:
            r.own_d[...] = term
        else:
            r.part_d[d - 1] = term.astype(BF16)
            back_d[d] = net.push(r.part_d.at[d - 1], r.recv_d.at[d - 1], z_peer(4 - d))
    for d in (1, 3, 2, 0):
        s = (z + 4 - d) % 4
        term = dot_nn(r.hid[s], r.w2[2])
        if d == 0:
            r.outputs[...] = x + term
        else:
            r.part_o[d - 1] = term.astype(BF16)
            back_o[d] = net.push(r.part_o.at[d - 1], r.recv_o.at[d - 1], z_peer(4 - d))
    unit_grads(((r.dpg, r.n4), (r.dpu, r.n4), (r.hid, r.c_all)), r.gw2)
    reducer = Reducer(net, r.gw2, r, "red")
    reducer.start()
    dn = r.own_d[...]
    for d in (1, 3, 2):
        back_d[d].wait_recv()
        dn = dn + r.recv_d[d - 1].astype(F32)
    dv, r.gg_four[...] = rms_back(dn, x, r.gain_four[...])
    c = c + dv

    for copy in attn_in:
        copy.wait()
    cb = c.astype(BF16)
    datt = dot_nt(cb, r.wa[1, :, HD:]).astype(BF16)
    cosine = r.cosine[...]
    sine = r.sine[...]
    swap = lambda v: pltpu.roll(v, HD // 2, 1)
    pairs = r.kv[...].reshape(KEYS, 2 * HD)
    for h in range(HEADS):
        cols = slice(h * HD, (h + 1) * HD)
        dh = datt[:, cols]
        r.datt[h] = dh
        dp = dot_nt(dh, pairs[:, HD:])
        p = r.pb[h].astype(F32)
        delta = jnp.sum(p * dp, axis=-1, keepdims=True)
        ds = (p * (dp - delta)).astype(BF16)
        r.ds[h] = ds
        dq = dot_nn(ds, pairs[:, :HD]) * (1.0 / math.sqrt(HD))
        r.dqkv[:, cols] = (dq * cosine - swap(dq) * sine).astype(BF16)
    queries = r.q[...].reshape(HEADS * ROWS, HD)
    datts = r.datt[...].reshape(HEADS * ROWS, HD)
    copies = {}
    own_k = own_v = None
    for o in (8, 7, 6, 5, 4, 3, 2, 1, 0):
        keys = slice((8 - o) * ROWS, (9 - o) * ROWS)
        dk = dot_tn(r.ds[:, :, keys].reshape(HEADS * ROWS, ROWS), queries)
        dv = dot_tn(r.pb[:, :, keys].reshape(HEADS * ROWS, ROWS), datts)
        if o == 0:
            own_k, own_v = dk, dv
            continue
        r.part_kv[o - 1, :, :HD] = dk.astype(BF16)
        r.part_kv[o - 1, :, HD:] = dv.astype(BF16)
        copy = net.make(r.part_kv.at[o - 1], r.recv_kv.at[o - 1], row_peer(-o))
        copies[o] = copy

        @pl.when(mp >= o)
        def _():
            copy.start()

        @pl.when(mp + o >= 16)
        def _():
            r.recv_kv[o - 1] = jnp.zeros((ROWS, 2 * HD), BF16)

    reducer.along_one()
    n = r.n3[...]
    att = r.att[...]

    def keep(side, lane, grad):
        rows = grad.reshape(4, 2, 16, 8, LANE)
        r.stage[:, :, :, 8 * side : 8 * side + 8, lane : lane + LANE] = rows

    for t in range(8):
        cols = slice(t * LANE, (t + 1) * LANE)
        keep(1, HD + t * LANE, dot_tn(att, cb[:, cols]))
        keep(0, t * LANE, dot_tn(n, r.dqkv[:, cols]))
    dn = dot_nt(r.dqkv[:, :D], r.wa[0, :, :D])
    reducer.along_two()
    for o in range(1, 9):

        @pl.when(mp + o < 16)
        def _():
            copies[o].wait_recv()

        own_k = own_k + r.recv_kv[o - 1, :, :HD].astype(F32)
        own_v = own_v + r.recv_kv[o - 1, :, HD:].astype(F32)
    dk = (own_k * cosine - swap(own_k) * sine).astype(BF16)
    dv = own_v.astype(BF16)
    dn = dn + dot_nt(dk, r.wa[0, :, D:]) + dot_nt(dv, r.wa[1, :, :HD])
    back, r.gg_three[...] = rms_back(dn, r.x2[...], r.gain_three[...])
    r.c2[...] = c + back
    keep(0, D, dot_tn(n, dk))
    keep(1, 0, dot_tn(n, dv))

    def lower(i, _):
        a, b = i // 4, i % 4
        r.gw_attn[0, a, b] = r.stage[a, 0, pl.ds(b * 4, 4)].reshape(64, PAIR).astype(BF16)
        r.gw_attn[1, a, b] = r.stage[a, 1, pl.ds(b * 4, 4)].reshape(64, PAIR).astype(BF16)
        return 0

    lax.fori_loop(0, 16, lower, 0)
    loc.store(r.gw_attn, r.out_gw_attn)
    total = r.outputs[...]
    for d in (1, 3, 2):
        back_o[d].wait_recv()
        total = total + r.recv_o[d - 1].astype(F32)
    r.outputs[...] = total
    a, b = reducer.finish()
    r.second_out[0:288, :] = a
    r.second_out[288:, :] = b
    loc.drain()
    net.drain()
    for o in range(1, 9):

        @pl.when(mp >= o)
        def _():
            copies[o].wait_send()


def middle(near, far):
    ins = [(k, v, "near") for k, v in near.items()]
    ins += [("far_" + k, v, "far") for k, v in far.items()]
    outs = [
        ("outputs", (ROWS, D), F32, "near"),
        ("c2", (ROWS, D), F32, "near"),
        ("gg_four", (1, D), F32, "near"),
        ("gg_three", (1, D), F32, "near"),
        ("second_out", (576, LANE), F32, "near"),
        ("out_gw_attn", (2, 4, 4, 64, PAIR), BF16, "far"),
    ]
    units = ((4, ROWS, UNITS), BF16)
    third = ((3, ROWS, D), BF16)
    scratch = [(k, vm(*SAVED[k])) for k in ("wa", "kv", "pb", "q", "att", "n3", "x2")]
    scratch += [
        ("w2", vm((3, UNITS, D), BF16)),
        ("c_all", vm((4, ROWS, D), BF16)),
        ("n4", vm((4, ROWS, D), BF16)),
        ("hid", vm(*units)),
        ("dpg", vm(*units)),
        ("dpu", vm(*units)),
        ("own_d", vm((ROWS, D), F32)),
        ("part_d", vm(*third)),
        ("recv_d", vm(*third)),
        ("part_o", vm(*third)),
        ("recv_o", vm(*third)),
        ("gw2", vm(*BLOCKS)),
        ("datt", vm((HEADS, ROWS, HD), BF16)),
        ("ds", vm((HEADS, ROWS, KEYS), BF16)),
        ("part_kv", vm((8, ROWS, 2 * HD), BF16)),
        ("recv_kv", vm((8, ROWS, 2 * HD), BF16)),
        ("dqkv", vm((ROWS, D), BF16)),
        ("stage", vm((4, 2, 16, 16, PAIR), F32)),
        ("gw_attn", vm((2, 4, 4, 64, PAIR), BF16)),
        *Reducer.scratch("red", 576, LANE),
        ("send", dma(36)),
        ("recv", dma(36)),
        ("sems", dma(112)),
    ]
    return run(middle_body, ins, outs, scratch, 2, 10**10)


def last_body(r):
    x, c, y, z = place()
    dp = lax.axis_index("dp")
    ready = greet(all_peers(False) + [xc_peer(d, 1) for d in (1, 2, 3)])
    net, loc = Net(r.send, r.recv), Local(r.sems)
    attn_in = loc.load(r.far_gw_attn, r.gw_attn)
    loads = {
        k: loc.load(getattr(r, "far_" + k), getattr(r, k))
        for k in ("w1", "pg", "pu", "n2", "wr", "gate", "state", "rate", "pr", "opened", "conv",
                  "mix", "n1", "gated")
    }
    need = lambda *names: [loads[k].wait() for k in names]
    upstream = r.c2[...]
    r.c2_all[z] = upstream.astype(BF16)
    ready()
    gather_c = spread_z(net, r.c2_all)
    attn_in.wait()
    red_attn = Reducer(net, r.gw_attn, r, "rat")
    red_attn.start()
    need("w1", "pg", "pu")
    back = {}
    for d in ORDER:
        s = (z + 4 - d) % 4
        if d:
            gather_c[d].wait_recv()
        if d == 1:
            red_attn.along_one()
        pg = r.pg[s]
        pu = r.pu[s]
        act, slope = gelu_both(pg)
        r.hid[s] = (act * pu).astype(BF16)
        dh = dot_nt(r.c2_all[s], r.w1[2])
        dpg = (dh * pu * slope).astype(BF16)
        dpu = (dh * act).astype(BF16)
        r.dpg[s] = dpg
        r.dpu[s] = dpu
        term = dot_nn(dpg, r.w1[0]) + dot_nn(dpu, r.w1[1])
        if d == 0:
            r.grad_tokens[...] = term
        else:
            r.part1[d - 1] = term.astype(BF16)
            back[d] = net.push(r.part1.at[d - 1], r.recv1.at[d - 1], z_peer(4 - d))
    need("n2")
    unit_grads(((r.dpg, r.n2), (r.dpu, r.n2), (r.hid, r.c2_all)), r.gw1)
    red_first = Reducer(net, r.gw1, r, "rff")
    red_first.start()
    red_attn.along_two()
    dn = r.grad_tokens[...]
    for d in (1, 3, 2):
        back[d].wait_recv()
        dn = dn + r.recv1[d - 1].astype(F32)
    dv, gg_two = rms_back(dn, r.x1[...], r.gain_two[...])
    upstream = upstream + dv
    r.c1[...] = upstream

    r.c1_all[z] = upstream.astype(BF16)
    gather_c = spread_z(net, r.c1_all)
    a, b = red_attn.finish()
    r.z_out[0:2] = a.astype(BF16).reshape(2, 16, PAIR)
    r.z_out[2:4] = b.astype(BF16).reshape(2, 16, PAIR)
    z_in = [
        net.push(r.z_out.at[(z + d) % 4], r.z_in.at[d - 1], z_peer(d)) for d in (1, 3, 2)
    ]
    need("wr")
    for d in ORDER:
        s = (z + 4 - d) % 4
        if d:
            gather_c[d].wait_recv()
        r.du[rows_at(s * ROWS, ROWS), :] = dot_nt(r.c1_all[s], r.wr[2])
        if d == 0:
            red_first.along_one()
    need("gate", "state", "rate", "pr")

    def decay_of(rows, first):
        pos = positions(r.length, y * SPAN + first, CHUNK)
        loga = -8.0 * r.rate[rows, :] * lanes_of(r.pr, VEC + 7)
        return loga, jnp.exp(loga), pos

    def first_chunk(i, _):
        first = pl.multiple_of(i * CHUNK, CHUNK)
        rows = pl.ds(first, CHUNK)
        act, slope = gelu_both(r.gate[rows, :])
        dgated = r.du[rows, :]
        r.dgate[rows, :] = (dgated * r.state[pl.ds(first + 8, CHUNK), :] * slope).astype(BF16)
        r.du[rows, :] = dgated * act
        _, decay, pos = decay_of(rows, first)
        r.fac[rows, :] = jnp.where(pos > 0, decay, 0.0)
        return 0

    lax.fori_loop(0, SPAN // CHUNK, first_chunk, 0)
    row = lax.broadcasted_iota(jnp.int32, (8, CH), 0)

    def step(i, carry):
        held, prod = carry
        rows = rows_at((SPAN // 8 - 1 - i) * 8, 8)
        m = r.fac[rows, :]
        u = r.du[rows, :]
        e = m * u
        for s in (1, 2, 4):
            inside = row < 8 - s
            e = e + m * jnp.where(inside, pltpu.roll(e, 8 - s, 0), 0.0)
            m = m * jnp.where(inside, pltpu.roll(m, 8 - s, 0), 1.0)
        e = e + m * held
        m = m * prod
        r.du[rows, :] = u + jnp.where(row < 7, pltpu.roll(e, 7, 0), held)
        r.acum[rows, :] = jnp.where(row < 7, pltpu.roll(m, 7, 0), prod)
        return e[0:1, :], m[0:1, :]

    zero = jnp.zeros((1, CH), F32)
    first_e, first_m = lax.fori_loop(0, SPAN // 8, step, (zero, zero + 1.0), unroll=4)
    edges_in = share_edges(net, r.edges, first_m, first_e)
    need("opened", "conv", "mix", "n1", "gated")

    def output_grads(w, left, right):
        for half in range(2):
            grad = dot_tn(left[:, half * 256 : half * 256 + 256], right[...].reshape(SPAN, D))
            for j in range(2):
                for part in range(8):
                    r.gwr[part % 2, part // 2, half * 2 + j, w * BW : (w + 1) * BW, :] = grad[
                        j * LANE : j * LANE + BW, part * LANE : (part + 1) * LANE
                    ].astype(BF16)

    output_grads(1, r.dgate, r.n1)
    output_grads(2, r.gated, r.c1_all)
    for copy in edges_in:
        copy.wait_recv()
    held = zero
    for b in (3, 2, 1):
        held = jnp.where(b > y, r.edges[b, 0:1, :] * held + r.edges[b, 1:2, :], held)

    def second_chunk(i, dsp):
        first = pl.multiple_of(i * CHUNK, CHUNK)
        rows = pl.ds(first, CHUNK)
        ds = r.du[rows, :] + r.acum[rows, :] * held
        loga, decay, pos = decay_of(rows, first)
        rate = r.rate[rows, :]
        opened = r.opened[rows, :]
        conv = r.conv[rows, :]
        before = r.state[pl.ds(first, CHUNK + 8), :][7 : 7 + CHUNK, :]
        beta = jnp.sqrt(neg_expm1(2.0 * loga))
        dloga = jnp.where(pos > 0, ds * before * decay, 0.0)
        dloga = dloga - ds * opened * conv * (decay * decay) / beta
        dopened = ds * beta * conv
        r.dconv[rows, :] = ds * beta * opened
        r.acum[rows, :] = dloga * (-8.0 * lanes_of(r.pr, VEC + 7)) * rate * (1.0 - rate)
        r.fac[rows, :] = dopened * opened * (1.0 - opened)
        return dsp + jnp.sum(dloga * (-8.0 * rate), axis=0, keepdims=True)

    dsp = lax.fori_loop(0, SPAN // CHUNK, second_chunk, zero)
    for b in range(4):
        cols = slice(b * LANE, (b + 1) * LANE)
        r.dconv[0:SPAN, cols] = (
            r.dconv[0:SPAN, cols]
            + jnp.pad(
                dot_nt(r.acum[:, cols], r.pr[b, 0:BW, :], precision=PRECISE)
                + dot_nt(r.fac[:, cols], r.pr[b, BW : 2 * BW, :], precision=PRECISE),
                ((0, 0), (0, LANE - BW)),
            )
        )
    halo = net.make(r.dconv.at[0:8], r.dconv.at[SPAN : SPAN + 8], y_peer(3))

    @pl.when(y > 0)
    def _():
        halo.start()

    @pl.when(y == 3)
    def _():
        r.dconv[SPAN : SPAN + 8, :] = jnp.zeros((8, CH), F32)

    red_first.along_two()
    for b in range(4):
        cols = slice(b * LANE, (b + 1) * LANE)
        left = r.conv[:, b * LANE : b * LANE + BW]
        r.gp[b, 0:BW, :] = dot_tn(left, r.acum[:, cols], precision=PRECISE)
        r.gp[b, BW : 2 * BW, :] = dot_tn(left, r.fac[:, cols], precision=PRECISE)

    @pl.when(y < 3)
    def _():
        halo.wait_recv()

    def third_chunk(i, sums):
        first = pl.multiple_of(i * CHUNK, CHUNK)
        rows = pl.ds(first, CHUNK)
        pos = positions(r.length, y * SPAN + first, CHUNK + 8)
        dwin = r.dconv[pl.ds(first, CHUNK + 8), :]
        mwin = r.mix[pl.ds(first, CHUNK + 8), :]
        dconv = dwin[:CHUNK, :]
        total = lanes_of(r.pr, VEC) * dconv
        taps = [jnp.sum(dconv * mwin[8:, :], axis=0, keepdims=True)]
        for k in (1, 2, 3):
            masked = jnp.where(pos >= k, dwin, 0.0)
            total = total + lanes_of(r.pr, VEC + k) * masked[k : k + CHUNK, :]
            taps.append(
                jnp.sum(masked[:CHUNK, :] * mwin[8 - k : 8 - k + CHUNK, :], axis=0, keepdims=True)
            )
        r.dmix[rows, :] = total.astype(BF16)
        taps.append(jnp.sum(dconv, axis=0, keepdims=True))
        taps.append(jnp.sum(r.acum[rows, :], axis=0, keepdims=True))
        taps.append(jnp.sum(r.fac[rows, :], axis=0, keepdims=True))
        return tuple(a + b for a, b in zip(sums, taps))

    sums = lax.fori_loop(0, SPAN // CHUNK, third_chunk, (zero,) * 7)
    back = {}
    for d in (1, 3, 2, 0):
        s = (z + 4 - d) % 4
        rows = rows_at(s * ROWS, ROWS)
        term = dot_nn(r.dmix[rows, :], r.wr[0]) + dot_nn(r.dgate[rows, :], r.wr[1])
        if d:
            r.part2[d - 1] = term.astype(BF16)
            back[d] = net.push(r.part2.at[d - 1], r.recv2.at[d - 1], z_peer(4 - d))
        else:
            r.grad_tokens[...] = term
    output_grads(0, r.dmix, r.n1)
    for b in range(4):
        cols = slice(b * LANE, (b + 1) * LANE)
        for k, row_sum in enumerate(sums + (dsp,)):
            r.gp[b, VEC + k : VEC + k + 1, :] = row_sum[:, cols]
        r.gp[b, 200:, :] = jnp.zeros((56, LANE), F32)
        for part in range(8):
            r.gwr[part % 2, part // 2, b, 288:, :] = r.gp[
                b, part * 32 : part * 32 + 32, :
            ].astype(BF16)
    red_recur = Reducer(net, r.gwr, r, "rec")
    red_recur.start()
    dn = r.grad_tokens[...]
    for d in (1, 3, 2):
        back[d].wait_recv()
        dn = dn + r.recv2[d - 1].astype(F32)
    dv, gg_one = rms_back(dn, r.tok[...].astype(F32), r.gain_one[...])
    r.grad_tokens[...] = r.c1[...] + dv
    r.gains[...] = jnp.concatenate(
        [gg_one, gg_two, r.gg_three[...], r.gg_four[...], jnp.zeros((4, D), F32)], axis=0
    )

    def spread(stage, first, peers):
        r.gain_out[stage] = r.gains[...]
        return [
            net.push(r.gain_out.at[stage], r.gain_in.at[first + i], peer)
            for i, peer in enumerate(peers)
        ]

    def collect(first, mine):
        total = r.gains[...]
        for i, copy in enumerate(mine):
            copy.wait_recv()
            total = total + r.gain_in[first + i]
        r.gains[...] = total

    mine = spread(0, 0, [xc_peer(0, 1)])
    red_recur.along_one()
    a, b = red_first.finish()
    r.first_out[0:288, :] = a
    r.first_out[288:, :] = b
    collect(0, mine)
    mine = spread(1, 1, [xc_peer(d, 0) for d in (1, 3, 2)])
    total = r.z_out[z].astype(F32)
    for copy in z_in:
        copy.wait_recv()
    for d in range(3):
        total = total + r.z_in[d].astype(F32)
    r.attn_out[...] = total
    collect(1, mine)
    mine = spread(2, 4, [y_peer(d) for d in (1, 3, 2)])
    red_recur.along_two()
    collect(4, mine)
    mine = spread(3, 7, [z_peer(d) for d in (1, 3, 2)])
    a, b = red_recur.finish()
    r.recur_all[dp, 0:160, :] = a.astype(BF16)
    r.recur_all[dp, 160:, :] = b.astype(BF16)
    cut = r.recur_all.at[dp]
    shares = [
        net.push(cut, cut, xc_peer(dx, dc))
        for dx, dc in ((1, 0), (3, 0), (2, 0), (1, 1), (3, 1), (2, 1), (0, 1))
    ]
    collect(7, mine)
    for copy in shares:
        copy.wait_recv()
    net.drain()

    @pl.when(y > 0)
    def _():
        halo.wait_send()


def last(near, far):
    ins = [(k, v, "near") for k, v in near.items()]
    ins += [("far_" + k, v, "far") for k, v in far.items()]
    outs = [
        ("grad_tokens", (ROWS, D), F32, "near"),
        ("gains", (8, D), F32, "near"),
        ("first_out", (576, LANE), F32, "near"),
        ("attn_out", (16, PAIR), F32, "near"),
        ("recur_all", (8, 320, LANE), BF16, "near"),
    ]
    units = ((4, ROWS, UNITS), BF16)
    third = ((3, ROWS, D), BF16)
    whole = ((4, ROWS, D), BF16)
    scratch = [(k, vm(*SAVED[k])) for k in far if k in SAVED]
    scratch += [
        ("gw_attn", vm((2, 4, 4, 64, PAIR), BF16)),
        ("c2_all", vm(*whole)),
        ("c1_all", vm(*whole)),
        ("c1", vm((ROWS, D), F32)),
        ("hid", vm(*units)),
        ("dpg", vm(*units)),
        ("dpu", vm(*units)),
        ("part1", vm(*third)),
        ("recv1", vm(*third)),
        ("part2", vm(*third)),
        ("recv2", vm(*third)),
        ("gw1", vm(*BLOCKS)),
        ("z_out", vm((4, 16, PAIR), BF16)),
        ("z_in", vm((3, 16, PAIR), BF16)),
        ("du", vm(*BIG)),
        ("fac", vm(*BIG)),
        ("acum", vm(*BIG)),
        ("dconv", vm(*TALL)),
        ("dmix", vm((SPAN, CH), BF16)),
        ("dgate", vm((SPAN, CH), BF16)),
        ("edges", vm((4, 8, CH), F32)),
        ("gp", vm((4, 256, LANE), F32)),
        ("gwr", vm((2, 4, 4, 320, LANE), BF16)),
        ("gain_in", vm((10, 8, D), F32)),
        ("gain_out", vm((4, 8, D), F32)),
        *Reducer.scratch("rat", 64, PAIR),
        *Reducer.scratch("rff", 576, LANE),
        *Reducer.scratch("rec", 320, LANE),
        ("send", dma(80)),
        ("recv", dma(80)),
        ("sems", dma(16)),
    ]
    return run(last_body, ins, outs, scratch, 3, 10**10)


def output_body(r):
    r.outputs[...] = r.in_outputs[...]
    r.tokens[...] = r.in_tokens[...]
    for i, name in enumerate(("norm_one", "norm_two", "norm_three", "norm_four")):
        getattr(r, name)[...] = r.gains[i : i + 1, :]
    for part in range(8):
        rows = slice(part * LANE, (part + 1) * LANE)
        r.recur_input[:, rows] = r.recur_all[part, 0:BW, :].astype(F32)
        r.recur_gate[:, rows] = r.recur_all[part, BW : 2 * BW, :].astype(F32)
        r.recur_output[:, rows] = r.recur_all[part, 2 * BW : 3 * BW, :].astype(F32)
    params = r.recur_all[:, 288:, :].astype(F32).reshape(256, LANE)
    r.decay_gate[0] = params[0:BW, :BW]
    r.input_gate[0] = params[BW : 2 * BW, :BW]
    r.conv_kernel[...] = params[VEC : VEC + 4, :BW]
    r.conv_bias[...] = params[VEC + 4 : VEC + 5, :BW]
    r.decay_shift[...] = params[VEC + 5 : VEC + 6, :BW]
    r.input_shift[...] = params[VEC + 6 : VEC + 7, :BW]
    r.decay_param[...] = params[VEC + 7 : VEC + 8, :BW] * r.slope[...]
    for name in ("first", "second"):
        summed = getattr(r, name)
        getattr(r, name + "_gate")[...] = summed[0:192, :]
        getattr(r, name + "_value")[...] = summed[192:384, :]
        getattr(r, name + "_down")[...] = summed[384:, :]
    r.query_proj[...] = r.attn[0:8, :D]
    r.key_proj[...] = r.attn[0:8, D:]
    r.value_proj[...] = r.attn[8:16, :HD]
    r.attn_output[...] = r.attn[8:16, HD:]


OUTPUTS = (
    ("outputs", (ROWS, D)), ("tokens", (ROWS, D)), ("norm_one", (1, D)),
    ("recur_input", (BW, D)), ("recur_gate", (BW, D)), ("conv_kernel", (4, BW)),
    ("conv_bias", (1, BW)), ("decay_gate", (1, BW, BW)), ("decay_shift", (1, BW)),
    ("input_gate", (1, BW, BW)), ("input_shift", (1, BW)), ("decay_param", (1, BW)),
    ("recur_output", (BW, D)), ("norm_two", (1, D)), ("first_gate", (192, 128)),
    ("first_value", (192, 128)), ("first_down", (192, 128)), ("norm_three", (1, D)),
    ("query_proj", (8, D)), ("key_proj", (8, HD)), ("value_proj", (8, HD)),
    ("attn_output", (8, D)), ("norm_four", (1, D)), ("second_gate", (192, 128)),
    ("second_value", (192, 128)), ("second_down", (192, 128)),
)
FLAT = (
    "norm_one", "conv_bias", "decay_shift", "input_shift", "decay_param", "norm_two",
    "norm_three", "norm_four",
)
TURNED = (
    "recur_input", "recur_gate", "first_gate", "first_value", "second_gate", "second_value",
)


def local(
    tokens, lengths, cotangent, norm_one, recur_input, recur_gate, conv_kernel, conv_bias,
    decay_gate, decay_shift, input_gate, input_shift, decay_param, recur_output, norm_two,
    first_gate, first_value, first_down, norm_three, query_proj, key_proj, value_proj,
    attn_output, norm_four, second_gate, second_value, second_down,
):
    length = jnp.broadcast_to(lengths.reshape(1, 1), (1, LANE))
    gain_one, gain_two, gain_three, gain_four = (
        g.reshape(1, D) for g in (norm_one, norm_two, norm_three, norm_four)
    )
    flat = lambda v: v.reshape(1, BW)

    index = lax.axis_index("mp") * ROWS + jnp.arange(ROWS, dtype=jnp.int32)
    position = jnp.where(index >= lengths[0], index - lengths[0], index)
    frequency = 10000.0 ** (-2.0 * jnp.arange(HD // 2, dtype=F32) / HD)
    angle = position.astype(F32)[:, None] * frequency[None, :]
    cosine = jnp.concatenate([jnp.cos(angle)] * 2, axis=1)
    sine = jnp.concatenate([-jnp.sin(angle), jnp.sin(angle)], axis=1)

    saved = forward(
        dict(
            tok=tokens, cot=cotangent, length=length, cosine=cosine, sine=sine,
            gain_one=gain_one, gain_two=gain_two, gain_three=gain_three,
            recur_input=recur_input.T, recur_gate=recur_gate.T, recur_output=recur_output,
            conv_kernel=conv_kernel, conv_bias=flat(conv_bias), decay_gate=decay_gate,
            decay_shift=flat(decay_shift), input_gate=input_gate,
            input_shift=flat(input_shift), softplus=flat(jax.nn.softplus(-decay_param)),
            first_gate=first_gate.T, first_value=first_value.T, first_down=first_down,
            query_proj=query_proj, key_proj=key_proj, value_proj=value_proj,
            attn_output=attn_output, second_gate=second_gate.T, second_value=second_value.T,
            second_down=second_down,
        )
    )
    kept = lambda *names: {k: saved["out_" + k] for k in names}
    mid = middle(
        dict(
            x3=saved["out_x3"], cot=cotangent, gain_four=gain_four, gain_three=gain_three,
            cosine=cosine, sine=sine,
        ),
        kept("w2", "c", "wa", "kv", "pb", "q", "att", "n3", "x2"),
    )
    end = last(
        dict(
            c2=mid["c2"], x1=saved["out_x1"], tok=tokens, length=length, gain_one=gain_one,
            gain_two=gain_two, gg_three=mid["gg_three"], gg_four=mid["gg_four"],
        ),
        dict(
            kept(
                "w1", "pg", "pu", "n2", "wr", "gate", "state", "rate", "pr", "opened", "conv",
                "mix", "n1", "gated",
            ),
            gw_attn=mid["out_gw_attn"],
        ),
    )
    results = run(
        output_body,
        [
            ("in_outputs", mid["outputs"], "near"),
            ("in_tokens", end["grad_tokens"], "near"),
            ("gains", end["gains"], "near"),
            ("recur_all", end["recur_all"], "near"),
            ("first", end["first_out"], "near"),
            ("second", mid["second_out"], "near"),
            ("attn", end["attn_out"], "near"),
            ("slope", flat(-jax.nn.sigmoid(-decay_param)), "near"),
        ],
        [(name, shape, F32, "near") for name, shape in OUTPUTS],
        [],
    )
    for name in FLAT:
        results[name] = results[name].reshape(-1)
    for name in TURNED:
        results[name] = results[name].T
    return tuple(results[name] for name, _ in OUTPUTS)


def solution(mesh):
    rows = P(("dp", "mp"), None)
    cols = P(None, "mp")
    one = P("mp")
    blocks = P("mp", None, None)
    tile = P("dp", "mp")
    weights = (
        P(), cols, cols, cols, one, blocks, one, blocks, one, one, P("mp", None),
        P(), tile, tile, P("mp", "dp"),
        P(), rows, rows, rows, rows,
        P(), tile, tile, P("mp", "dp"),
    )
    return jax.shard_map(
        local,
        mesh=mesh,
        in_specs=(rows, P("dp"), rows, *weights),
        out_specs=(rows, rows, *weights),
        check_vma=False,
    )
```

```python
import math
from types import SimpleNamespace

import jax
import jax.numpy as jnp
from jax import lax
from jax.experimental import pallas as pl
from jax.experimental.pallas import tpu as pltpu
from jax.sharding import PartitionSpec as P

MESH = pl.DeviceIdType.MESH
F32 = jnp.float32
BF16 = jnp.bfloat16
VMEM_BYTES = 63 * 2**20

D = 1024
ROWS = 128
SPAN = 512
LANE = 128
BW = 96
CH = 4 * LANE
PAR = 208
VEC = 192
UNITS = 768
HEADS = 8
HD = 128
WINDOW = 1024
KEYS = 1152
PAIR = 1152
CHUNK = 64
STEPS = ((0,), (1, 3), (2,))
HALVES = ((1, 3), (2, 0))
GELU_C = math.sqrt(2.0 / math.pi)


def place():
    dp, mp = lax.axis_index("dp"), lax.axis_index("mp")
    return dp // 2, dp % 2, mp // 4, mp % 4


def z_peer(d):
    _, _, y, z = place()
    return {"mp": y * 4 + (z + d) % 4}


def y_peer(d):
    _, _, y, z = place()
    return {"mp": ((y + d) % 4) * 4 + z}


def xc_peer(dx, dc):
    x, c, _, _ = place()
    return {"dp": ((x + dx) % 4) * 2 + (c + dc) % 2}


def row_peer(offset):
    return {"mp": lax.rem(lax.axis_index("mp") + 16 + offset, 16)}


def all_peers(window):
    peers = [xc_peer(0, 1)] + [xc_peer(d, 0) for d in (1, 2, 3)]
    if window:
        return peers + [row_peer(o) for o in range(1, 16)]
    for d in (1, 2, 3):
        peers += [y_peer(d), z_peer(d)]
    return peers


def greet(peers):
    barrier = pltpu.get_barrier_semaphore()
    for peer in peers:
        pl.semaphore_signal(barrier, inc=1, device_id=peer, device_id_type=MESH)
    return lambda: pl.semaphore_wait(barrier, len(peers))


class Net:
    def __init__(self, send, recv):
        self.send, self.recv, self.used, self.started = send, recv, 0, []
        self.landing = {}

    def make(self, src, dst, peer, shared=None):
        landing = self.landing.setdefault(shared, self.used) if shared else self.used
        copy = pltpu.make_async_remote_copy(
            src_ref=src,
            dst_ref=dst,
            send_sem=self.send.at[self.used],
            recv_sem=self.recv.at[landing],
            device_id=peer,
            device_id_type=MESH,
        )
        self.used += 1
        return copy

    def push(self, src, dst, peer):
        copy = self.make(src, dst, peer)
        copy.start()
        self.started.append(copy)
        return copy

    def drain(self):
        for copy in self.started:
            copy.wait_send()


class Local:
    def __init__(self, sems):
        self.sems, self.used, self.stores = sems, 0, []

    def load(self, src, dst):
        copy = pltpu.make_async_copy(src, dst, self.sems.at[self.used])
        self.used += 1
        copy.start()
        return copy

    def store(self, src, dst):
        self.stores.append(self.load(src, dst))

    def drain(self):
        for copy in self.stores:
            copy.wait()


def run(body, ins, outs, scratch, collective_id=None, flops=0):
    names = [n for n, _, _ in ins] + [n for n, _, _, _ in outs] + [n for n, _ in scratch]
    space = {"near": pltpu.VMEM, "far": pl.ANY}

    def kernel(*refs):
        body(SimpleNamespace(**dict(zip(names, refs))))

    results = pl.pallas_call(
        kernel,
        out_shape=[jax.ShapeDtypeStruct(s, t) for _, s, t, _ in outs],
        in_specs=[pl.BlockSpec(memory_space=space[where]) for _, _, where in ins],
        out_specs=[pl.BlockSpec(memory_space=space[where]) for _, _, _, where in outs],
        scratch_shapes=[s for _, s in scratch],
        compiler_params=pltpu.CompilerParams(
            collective_id=collective_id,
            has_side_effects=collective_id is not None,
            vmem_limit_bytes=VMEM_BYTES,
        ),
        cost_estimate=pl.CostEstimate(flops=flops, bytes_accessed=2**24, transcendentals=0),
    )(*[a for _, a, _ in ins])
    return dict(zip([n for n, _, _, _ in outs], results))


def vm(shape, dtype):
    return pltpu.VMEM(shape, dtype)


def dma(n):
    return pltpu.SemaphoreType.DMA((n,))


def dot_nn(a, b, **kw):
    return lax.dot_general(a, b, (((1,), (0,)), ((), ())), preferred_element_type=F32, **kw)


def dot_nt(a, b, **kw):
    return lax.dot_general(a, b, (((1,), (1,)), ((), ())), preferred_element_type=F32, **kw)


def dot_tn(a, b, **kw):
    return lax.dot_general(a, b, (((0,), (0,)), ((), ())), preferred_element_type=F32, **kw)


def gelu(v):
    return 0.5 * v * (1.0 + jnp.tanh(GELU_C * (v + 0.044715 * v * v * v)))


def gelu_both(v):
    t = jnp.tanh(GELU_C * (v + 0.044715 * v * v * v))
    value = 0.5 * v * (1.0 + t)
    slope = 0.5 * (1.0 + t) + 0.5 * v * (1.0 - t * t) * GELU_C * (1.0 + 3.0 * 0.044715 * v * v)
    return value, slope


def rms(v, gain):
    return v * lax.rsqrt(jnp.mean(v * v, axis=-1, keepdims=True) + 1e-06) * gain


def rms_back(dn, v, gain):
    r = lax.rsqrt(jnp.mean(v * v, axis=-1, keepdims=True) + 1e-06)
    grad_gain = jnp.sum(dn * v * r, axis=0, keepdims=True)
    dg = dn * gain
    dv = r * dg - v * (r * r * r) * jnp.mean(dg * v, axis=-1, keepdims=True)
    return dv, grad_gain


def stack(ref, slots):
    return jnp.concatenate([ref[s] for s in slots], axis=0) if len(slots) > 1 else ref[slots[0]]


def block(value, i):
    return value[i * ROWS : (i + 1) * ROWS]


def low_dot(left, right, dims):
    return lax.dot_general(
        left.astype(BF16), right.astype(BF16), (dims, ((), ())), preferred_element_type=F32
    )


def rows_at(first, count):
    return pl.ds(pl.multiple_of(first, count), count)


class Gatherer:
    def __init__(self, net, own, whole):
        self.net, self.own, self.whole, self.half = net, own, whole, whole.shape[3] // 2

    def start(self):
        x, c, y, _ = place()
        one, two = slice(0, self.half), slice(self.half, 2 * self.half)
        self.whole[c, x, y] = self.own[...]
        self.first = []
        for d in (1, 3, 2):
            for part, peer in ((one, xc_peer(d, 0)), (two, y_peer(d))):
                self.first.append(
                    self.net.push(self.own.at[part, :], self.whole.at[c, x, y, part, :], peer)
                )

    def along(self):
        x, c, y, _ = place()
        one, two = slice(0, self.half), slice(self.half, 2 * self.half)
        for copy in self.first:
            copy.wait_recv()
        self.second = []
        for d in (1, 3, 2):
            mine = self.whole.at[c, :, y, one, :]
            self.second.append(self.net.push(mine, mine, y_peer(d)))
            mine = self.whole.at[c, x, :, two, :]
            self.second.append(self.net.push(mine, mine, xc_peer(d, 0)))

    def across(self):
        _, c, _, _ = place()
        for copy in self.second:
            copy.wait_recv()
        mine = self.whole.at[c]
        self.third = self.net.push(mine, mine, xc_peer(0, 1))

    def finish(self):
        self.third.wait_recv()


class Reducer:
    @staticmethod
    def scratch(name, rows, lanes):
        half = rows // 2
        return [
            (name + "_other", vm((4, 4, rows, lanes), BF16)),
            (name + "_in_a", vm((3, 4, half, lanes), BF16)),
            (name + "_in_b", vm((3, 4, half, lanes), BF16)),
            (name + "_sum_a", vm((4, half, lanes), BF16)),
            (name + "_sum_b", vm((4, half, lanes), BF16)),
            (name + "_last_a", vm((3, half, lanes), BF16)),
            (name + "_last_b", vm((3, half, lanes), BF16)),
        ]

    def __init__(self, net, src, r, name):
        self.net, self.src, self.half = net, src, src.shape[3] // 2
        for part in ("other", "in_a", "in_b", "sum_a", "sum_b", "last_a", "last_b"):
            setattr(self, part, getattr(r, name + "_" + part))

    def start(self):
        _, c, _, _ = place()
        self.first = self.net.push(self.src.at[1 - c], self.other, xc_peer(0, 1))

    def along_one(self):
        x, c, y, _ = place()
        half = self.half
        self.first.wait_recv()

        def add(i, _):
            a, b = i // 4, i % 4
            total = self.src[c, a, b].astype(F32) + self.other[a, b].astype(F32)
            self.other[a, b] = total.astype(BF16)
            return 0

        lax.fori_loop(0, 16, add, 0)
        self.second = []
        for d in (1, 3, 2):
            mine = self.other.at[(x + d) % 4, :, 0:half, :]
            self.second.append(self.net.push(mine, self.in_a.at[d - 1], xc_peer(d, 0)))
            mine = self.other.at[:, (y + d) % 4, half : 2 * half, :]
            self.second.append(self.net.push(mine, self.in_b.at[d - 1], y_peer(d)))

    def along_two(self):
        x, _, y, _ = place()
        half = self.half
        for copy in self.second:
            copy.wait_recv()

        def add(i, _):
            a = self.other[x, i, 0:half, :].astype(F32)
            b = self.other[i, y, half : 2 * half, :].astype(F32)
            for d in range(3):
                a = a + self.in_a[d, i].astype(F32)
                b = b + self.in_b[d, i].astype(F32)
            self.sum_a[i] = a.astype(BF16)
            self.sum_b[i] = b.astype(BF16)
            return 0

        lax.fori_loop(0, 4, add, 0)
        self.third = []
        for d in (1, 3, 2):
            mine = self.sum_a.at[(y + d) % 4]
            self.third.append(self.net.push(mine, self.last_a.at[d - 1], y_peer(d)))
            mine = self.sum_b.at[(x + d) % 4]
            self.third.append(self.net.push(mine, self.last_b.at[d - 1], xc_peer(d, 0)))

    def finish(self):
        x, _, y, _ = place()
        for copy in self.third:
            copy.wait_recv()
        a = self.sum_a[y].astype(F32)
        b = self.sum_b[x].astype(F32)
        for d in range(3):
            a = a + self.last_a[d].astype(F32)
            b = b + self.last_b[d].astype(F32)
        return a, b


def spread_z(net, ref):
    z = place()[3]
    return {d: net.push(ref.at[z], ref.at[z], z_peer(d)) for d in (1, 3, 2)}


def place_units(local, whole, w_ref):
    copies = []
    for part in range(8):
        for y in range(4):
            for w in range(3):
                copies.append(
                    local.load(
                        whole.at[part % 2, part // 2, y, w * 192 : (w + 1) * 192, :],
                        w_ref.at[
                            w, y * 192 : (y + 1) * 192, part * LANE : (part + 1) * LANE
                        ],
                    )
                )
    return copies


def unit_grads(sides, out):
    for w, (left, right) in enumerate(sides):
        right = right[...].reshape(SPAN, D)
        for tile in range(3):
            cut = left[:, :, tile * 256 : tile * 256 + 256].reshape(SPAN, 256)
            grad = dot_tn(cut, right)
            first = tile * 256
            while first < tile * 256 + 256:
                block = first // 192
                last = min((block + 1) * 192, tile * 256 + 256)
                rows = grad[first - tile * 256 : last - tile * 256]
                start = w * 192 + first - block * 192
                for part in range(8):
                    out[part % 2, part // 2, block, start : start + last - first, :] = rows[
                        :, part * LANE : (part + 1) * LANE
                    ].astype(BF16)
                first = last


def positions(length, first, rows):
    t = lax.broadcasted_iota(jnp.int32, (rows, CH), 0) + first
    wide = jnp.concatenate([length[...]] * 4, axis=1)
    return jnp.where(t >= wide, t - wide, t)


def lanes_of(pr, row):
    return jnp.concatenate([pr[b, row : row + 1, :] for b in range(4)], axis=1)


def neg_expm1(v):
    series = v * (
        1.0 + v * (0.5 + v * (1.0 / 6 + v * (1.0 / 24 + v * (1.0 / 120 + v * (1.0 / 720)))))
    )
    return -jnp.where(v > -0.25, series, jnp.exp(v) - 1.0)


def share_edges(net, edges, prod, last):
    y = place()[2]
    edges[y, 0:1, :] = prod
    edges[y, 1:2, :] = last
    return [net.push(edges.at[y], edges.at[y], y_peer(d)) for d in (1, 3, 2)]


def forward_body(r):
    x, c, y, z = place()
    mp = lax.axis_index("mp")
    ready = greet(all_peers(True))
    net, loc = Net(r.send, r.recv), Local(r.sems)

    tokens = r.tok[...].astype(F32)
    r.n1[z] = rms(tokens, r.gain_one[...]).astype(BF16)
    mine = pl.ds(pl.multiple_of(y * LANE, LANE), BW)
    r.wr[0, mine, :] = r.recur_input[...]
    r.wr[1, mine, :] = r.recur_gate[...]
    r.wr[2, mine, :] = r.recur_output[...]
    for b in range(4):
        r.wr[:, b * LANE + BW : (b + 1) * LANE, :] = jnp.zeros((3, LANE - BW, D), BF16)
    r.pr[y] = jnp.zeros((PAR, LANE), F32)
    r.pr[y, 0:BW, 0:BW] = r.decay_gate[0]
    r.pr[y, BW : 2 * BW, 0:BW] = r.input_gate[0]
    r.pr[y, VEC : VEC + 4, 0:BW] = r.conv_kernel[...]
    r.pr[y, VEC + 4 : VEC + 5, 0:BW] = r.conv_bias[...]
    r.pr[y, VEC + 5 : VEC + 6, 0:BW] = r.decay_shift[...]
    r.pr[y, VEC + 6 : VEC + 7, 0:BW] = r.input_shift[...]
    r.pr[y, VEC + 7 : VEC + 8, :] = jnp.ones((1, LANE), F32)
    r.pr[y, VEC + 7 : VEC + 8, 0:BW] = r.softplus[...]
    ready()
    gather_n1 = spread_z(net, r.n1)
    half = pl.ds(pl.multiple_of(c * 512, 512), 512)
    part_p = pl.ds(pl.multiple_of(c * 104, 8), 104)
    weights_in, shared = {}, []
    for d in (1, 3, 2):
        cut = r.wr.at[0, mine, half]
        weights_in[d, 0] = net.push(cut, cut, y_peer(d))
    for d in (1, 3, 2):
        cut = r.pr.at[y, part_p, :]
        weights_in[d, 1] = net.push(cut, cut, y_peer(d))

    tail = r.n1.at[3, ROWS - 16 :, :]
    halos = [net.make(tail, r.halo, {"mp": (y * 4 + 4 + i) % 16}, "halo") for i in range(4)]

    @pl.when((z == 3) & (y < 3))
    def _():
        for halo in halos:
            halo.start()

    @pl.when(y == 0)
    def _():
        r.halo[...] = jnp.zeros((16, D), BF16)

    r.own_first[0:192, :] = r.first_gate[...]
    r.own_first[192:384, :] = r.first_value[...]
    r.own_first[384:576, :] = r.first_down[...]
    left = jnp.concatenate([r.query_proj[...], r.key_proj[...]], axis=1).astype(F32)
    right = jnp.concatenate([r.value_proj[...], r.attn_output[...]], axis=1).astype(F32)
    r.own_attn[rows_at(z * 16, 16), :] = jnp.concatenate([left, right], axis=0).astype(BF16)
    r.own_second[0:192, :] = r.second_gate[...]
    r.own_second[192:384, :] = r.second_value[...]
    r.own_second[384:576, :] = r.second_down[...]
    first_w = Gatherer(net, r.own_first, r.all_first)
    attn_w = Gatherer(net, r.own_attn, r.all_attn)
    second_w = Gatherer(net, r.own_second, r.all_second)

    def pass_on(kind):
        for d in (1, 3, 2):
            weights_in[d, kind].wait_recv()
            start = (y + 4 - d) % 4
            rows = pl.ds(pl.multiple_of(start * LANE, LANE), BW)
            if kind == 0:
                cut = r.wr.at[0, rows, half]
            elif kind == 1:
                cut = r.pr.at[start, part_p, :]
            else:
                cut = r.wr.at[1:3, rows, half]
            shared.append((kind, net.push(cut, cut, xc_peer(0, 1))))

    def arrived(kind):
        for k, copy in shared:
            if k == kind:
                copy.wait_recv()

    pass_on(0)
    for d in (1, 3, 2):
        cut = r.wr.at[1:3, mine, half]
        weights_in[d, 2] = net.push(cut, cut, y_peer(d))
    pass_on(1)
    for d in (1, 3, 2):
        gather_n1[d].wait_recv()
    r.c_all[z] = r.cot[...]
    gather_c = spread_z(net, r.c_all)
    cut = r.own_attn.at[rows_at(z * 16, 16), :]
    attn_z = [net.push(cut, cut, z_peer(d)) for d in (1, 3, 2)]
    arrived(0)
    rows_n = r.n1[...].reshape(SPAN, D)
    r.mix[8:, :] = dot_nt(rows_n, r.wr[0])

    @pl.when(y > 0)
    def _():
        halos[0].wait_recv()

    r.mix[0:8, :] = dot_nt(r.halo[...], r.wr[0])[8:, :]
    loc.store(r.n1, r.out_n1)
    loc.store(r.mix, r.out_mix)
    arrived(1)
    loc.store(r.pr, r.out_pr)
    def conv_chunk(i, _):
        first = pl.multiple_of(i * CHUNK, CHUNK)
        pos = positions(r.length, y * SPAN + first, CHUNK)
        window = r.mix[pl.ds(first, CHUNK + 8), :]
        total = lanes_of(r.pr, VEC + 4) + lanes_of(r.pr, VEC) * window[8:, :]
        for k in (1, 2, 3):
            lagged = window[8 - k : 8 - k + CHUNK, :]
            total = total + jnp.where(pos >= k, lanes_of(r.pr, VEC + k) * lagged, 0.0)
        r.conv[pl.ds(first, CHUNK), :] = total
        return 0

    lax.fori_loop(0, SPAN // CHUNK, conv_chunk, 0)
    loc.store(r.conv, r.out_conv)
    for b in range(4):
        cols = slice(b * LANE, (b + 1) * LANE)
        left = r.conv[:, b * LANE : b * LANE + BW]
        r.rate[:, cols] = low_dot(left, r.pr[b, 0:BW, :], ((1,), (0,)))
        r.opened[:, cols] = low_dot(left, r.pr[b, BW : 2 * BW, :], ((1,), (0,)))

    def gates_chunk(i, _):
        first = pl.multiple_of(i * CHUNK, CHUNK)
        rows = pl.ds(first, CHUNK)
        pos = positions(r.length, y * SPAN + first, CHUNK)
        rate = jax.nn.sigmoid(r.rate[rows, :] + lanes_of(r.pr, VEC + 5))
        opened = jax.nn.sigmoid(r.opened[rows, :] + lanes_of(r.pr, VEC + 6))
        loga = -8.0 * rate * lanes_of(r.pr, VEC + 7)
        r.rate[rows, :] = rate
        r.opened[rows, :] = opened
        r.fac[rows, :] = jnp.where(pos > 0, jnp.exp(loga), 0.0)
        r.state[pl.ds(first + 8, CHUNK), :] = (
            jnp.sqrt(neg_expm1(2.0 * loga)) * opened * r.conv[rows, :]
        )
        return 0

    lax.fori_loop(0, SPAN // CHUNK, gates_chunk, 0)
    loc.store(r.rate, r.out_rate)
    loc.store(r.opened, r.out_opened)
    row = lax.broadcasted_iota(jnp.int32, (8, CH), 0)

    def step(i, carry):
        held, prod = carry
        rows = rows_at(i * 8, 8)
        srows = rows_at(i * 8 + 8, 8)
        a = r.fac[rows, :]
        h = r.state[srows, :]
        for s in (1, 2, 4):
            h = h + a * jnp.where(row >= s, pltpu.roll(h, s, 0), 0.0)
            a = a * jnp.where(row >= s, pltpu.roll(a, s, 0), 1.0)
        h = h + a * held
        a = a * prod
        r.state[srows, :] = h
        r.acum[rows, :] = a
        return h[7:8, :], a[7:8, :]

    zero = jnp.zeros((1, CH), F32)
    last_h, last_a = lax.fori_loop(0, SPAN // 8, step, (zero, zero + 1.0), unroll=4)
    edges_in = share_edges(net, r.edges, last_a, last_h)
    pass_on(2)
    first_w.start()
    arrived(2)
    loc.store(r.wr, r.out_wr)
    r.gate[...] = dot_nt(rows_n, r.wr[1])
    loc.store(r.gate, r.out_gate)
    for copy in edges_in:
        copy.wait_recv()
    held = zero
    for b in range(3):
        held = jnp.where(b < y, r.edges[b, 0:1, :] * held + r.edges[b, 1:2, :], held)
    r.state[0:8, :] = jnp.broadcast_to(held, (8, CH))

    def gated_chunk(i, _):
        first = pl.multiple_of(i * CHUNK, CHUNK)
        rows = pl.ds(first, CHUNK)
        srows = pl.ds(first + 8, CHUNK)
        state = r.state[srows, :] + r.acum[rows, :] * held
        r.state[srows, :] = state
        r.gated[i // 2, rows_at(i % 2 * CHUNK, CHUNK), :] = (
            gelu(r.gate[rows, :]) * state
        ).astype(BF16)
        return 0

    lax.fori_loop(0, SPAN // CHUNK, gated_chunk, 0)
    loc.store(r.state, r.out_state)
    loc.store(r.gated, r.out_gated)
    back = {}
    for ds in HALVES:
        term = dot_nn(stack(r.gated, [(z + 4 - d) % 4 for d in ds]), r.wr[2])
        for i, d in enumerate(ds):
            if d:
                r.part1[d - 1] = block(term, i).astype(BF16)
                back[d] = net.push(r.part1.at[d - 1], r.recv1.at[d - 1], z_peer(4 - d))
            else:
                r.x1[...] = tokens + block(term, i)
    first_w.along()
    for copy in attn_z:
        copy.wait_recv()
    attn_w.start()
    total = r.x1[...]
    for d in (1, 3, 2):
        back[d].wait_recv()
        total = total + r.recv1[d - 1].astype(F32)
    r.x1[...] = total

    r.n2[z] = rms(total, r.gain_two[...]).astype(BF16)
    gather_n2 = spread_z(net, r.n2)
    loc.store(r.x1, r.out_x1)
    first_w.across()
    attn_w.along()
    first_w.finish()
    for copy in place_units(loc, r.all_first, r.w1):
        copy.wait()
    loc.store(r.w1, r.out_w1)
    back = {}
    for ds in HALVES:
        slots = [(z + 4 - d) % 4 for d in ds]
        for d in ds:
            if d:
                gather_n2[d].wait_recv()
        nb = stack(r.n2, slots)
        pg = dot_nt(nb, r.w1[0])
        pu = dot_nt(nb, r.w1[1])
        term = dot_nn((gelu(pg) * pu).astype(BF16), r.w1[2])
        for i, (d, s) in enumerate(zip(ds, slots)):
            r.pg[s] = block(pg, i)
            r.pu[s] = block(pu, i)
            if d:
                r.part2[d - 1] = block(term, i).astype(BF16)
                back[d] = net.push(r.part2.at[d - 1], r.recv2.at[d - 1], z_peer(4 - d))
            else:
                r.x2[...] = total + block(term, i)
        if ds == HALVES[0]:
            attn_w.across()
            second_w.start()
    loc.store(r.n2, r.out_n2)
    loc.store(r.pg, r.out_pg)
    loc.store(r.pu, r.out_pu)
    second_w.along()
    attn_w.finish()

    def split(i, _):
        a, b, e = i // 16, (i // 4) % 4, i % 4
        block = r.all_attn[a, b, e].astype(F32).reshape(4, 16, PAIR)
        rows = rows_at((b * 2 + a) * 128 + e * 32, 32)
        r.wa[0, rows, :] = block[:, 0:8, :].reshape(32, PAIR).astype(BF16)
        r.wa[1, rows, :] = block[:, 8:16, :].reshape(32, PAIR).astype(BF16)
        return 0

    lax.fori_loop(0, 32, split, 0)
    loc.store(r.wa, r.out_wa)
    total = r.x2[...]
    for d in (1, 3, 2):
        back[d].wait_recv()
        total = total + r.recv2[d - 1].astype(F32)
    r.x2[...] = total
    loc.store(r.x2, r.out_x2)

    n = rms(total, r.gain_three[...]).astype(BF16)
    r.n3[...] = n
    cosine = r.cosine[...]
    sine = r.sine[...]
    swap = lambda v: pltpu.roll(v, HD // 2, 1)
    key = dot_nn(n, r.wa[0, :, D:])
    r.kv[8, :, :HD] = (key * cosine + swap(key) * sine).astype(BF16)
    r.kv[8, :, HD:] = dot_nn(n, r.wa[1, :, :HD]).astype(BF16)
    copies = []
    for o in range(1, 9):
        copy = net.make(r.kv.at[8], r.kv.at[8 - o], row_peer(o))
        copies.append(copy)

        @pl.when(mp + o < 16)
        def _():
            copy.start()

        @pl.when(mp < o)
        def _():
            r.kv[8 - o] = jnp.zeros((ROWS, 2 * HD), BF16)

    loc.store(r.n3, r.out_n3)
    queries = dot_nn(n, r.wa[0, :, :D])
    for h in range(HEADS):
        query = queries[:, h * HD : (h + 1) * HD]
        r.q[h] = ((query * cosine + swap(query) * sine) * (1.0 / math.sqrt(HD))).astype(BF16)
    loc.store(r.q, r.out_q)
    row = lax.broadcasted_iota(jnp.int32, (ROWS, KEYS), 0)
    col = lax.broadcasted_iota(jnp.int32, (ROWS, KEYS), 1) - (KEYS - ROWS)
    base = mp * ROWS
    length = jnp.concatenate([r.length[...]] * 9, axis=1)
    allowed = (col + base >= 0) & (row >= col) & (row - col < WINDOW)
    allowed = allowed & ((row + base >= length) == (col + base >= length))
    r.bias[...] = jnp.where(allowed, 0.0, -1e30)
    second_w.across()
    for o in range(1, 9):

        @pl.when(mp >= o)
        def _():
            copies[o - 1].wait_recv()

    loc.store(r.kv, r.out_kv)
    pairs = r.kv[...].reshape(KEYS, 2 * HD)
    r.keys[...] = pairs[:, :HD]
    r.values[...] = pairs[:, HD:]
    r.score[...] = dot_nt(r.q[...].reshape(HEADS * ROWS, HD), r.keys[...])

    def softmax(i, _):
        rows, own = rows_at(i % 2 * 64, 64), rows_at(i * 64, 64)
        s = r.score[own, :] + r.bias[rows, :]
        e = jnp.exp(s - jnp.max(s, axis=-1, keepdims=True))
        p = e * (1.0 / jnp.sum(e, axis=-1, keepdims=True))
        r.pb[own, :] = p.astype(BF16)
        return 0

    lax.fori_loop(0, HEADS * 2, softmax, 0)
    mixed = dot_nn(r.pb[...], r.values[...])
    for h in range(HEADS):
        r.att[:, h * HD : (h + 1) * HD] = block(mixed, h).astype(BF16)
    loc.store(r.pb, r.out_pb)
    loc.store(r.att, r.out_att)
    total = total + dot_nn(r.att[...], r.wa[1, :, HD:])
    r.x3[...] = total
    r.n4[z] = rms(total, r.gain_four[...]).astype(BF16)
    gather_n4 = spread_z(net, r.n4)
    loc.store(r.x3, r.out_x3)
    for d in (1, 3, 2):
        gather_c[d].wait_recv()
    loc.store(r.c_all, r.out_c_all)
    second_w.finish()
    loc.stores += place_units(loc, r.all_second, r.out_w2)
    for d in (1, 3, 2):
        gather_n4[d].wait_recv()
    loc.store(r.n4, r.out_n4)
    loc.drain()
    net.drain()
    for o in range(1, 9):

        @pl.when(mp + o < 16)
        def _():
            copies[o - 1].wait_send()

    @pl.when((z == 3) & (y < 3))
    def _():
        for halo in halos:
            halo.wait_send()


BIG = ((SPAN, CH), F32)
TALL = ((SPAN + 8, CH), F32)
SAVED = {
    "n1": ((4, ROWS, D), BF16),
    "wr": ((3, CH, D), BF16),
    "pr": ((4, PAR, LANE), F32),
    "mix": TALL,
    "gate": BIG,
    "conv": BIG,
    "rate": BIG,
    "opened": BIG,
    "state": TALL,
    "gated": ((4, ROWS, CH), BF16),
    "x1": ((ROWS, D), F32),
    "w1": ((3, UNITS, D), BF16),
    "n2": ((4, ROWS, D), BF16),
    "pg": ((4, ROWS, UNITS), F32),
    "pu": ((4, ROWS, UNITS), F32),
    "x2": ((ROWS, D), F32),
    "wa": ((2, D, PAIR), BF16),
    "n3": ((ROWS, D), BF16),
    "q": ((HEADS, ROWS, HD), BF16),
    "kv": ((9, ROWS, 2 * HD), BF16),
    "pb": ((HEADS * ROWS, KEYS), BF16),
    "att": ((ROWS, D), BF16),
    "x3": ((ROWS, D), F32),
    "n4": ((4, ROWS, D), BF16),
    "c_all": ((4, ROWS, D), BF16),
}
BLOCKS = ((2, 4, 4, 576, LANE), BF16)


def forward(inputs):
    outs = [("out_" + k, *v, "far") for k, v in SAVED.items()]
    outs += [("out_w2", (3, UNITS, D), BF16, "far")]
    scratch = [(k, vm(*v)) for k, v in SAVED.items()]
    scratch += [
        ("fac", vm(*BIG)),
        ("acum", vm(*BIG)),
        ("edges", vm((4, 8, CH), F32)),
        ("part1", vm((3, ROWS, D), BF16)),
        ("recv1", vm((3, ROWS, D), BF16)),
        ("part2", vm((3, ROWS, D), BF16)),
        ("recv2", vm((3, ROWS, D), BF16)),
        ("own_first", vm((576, LANE), BF16)),
        ("own_second", vm((576, LANE), BF16)),
        ("own_attn", vm((64, PAIR), BF16)),
        ("all_first", vm(*BLOCKS)),
        ("all_second", vm(*BLOCKS)),
        ("all_attn", vm((2, 4, 4, 64, PAIR), BF16)),
        ("halo", vm((16, D), BF16)),
        ("bias", vm((ROWS, KEYS), F32)),
        ("score", vm((HEADS * ROWS, KEYS), F32)),
        ("keys", vm((KEYS, HD), BF16)),
        ("values", vm((KEYS, HD), BF16)),
        ("send", dma(100)),
        ("recv", dma(100)),
        ("sems", dma(230)),
    ]
    return run(
        forward_body, [(k, v, "near") for k, v in inputs.items()], outs, scratch, 1, 10**10
    )


def middle_body(r):
    _, _, _, z = place()
    mp = lax.axis_index("mp")
    ready = greet(all_peers(True))
    net, loc = Net(r.send, r.recv), Local(r.sems)
    loads = {
        k: loc.load(getattr(r, "far_" + k), getattr(r, k))
        for k in ("w2", "n4", "c_all", "wa", "kv", "pb", "q", "att", "n3", "x2")
    }
    x = r.x3[...]
    c = r.cot[...].astype(F32)
    for k in ("w2", "n4", "c_all"):
        loads[k].wait()
    back_d, back_o = {}, {}
    for ds in HALVES:
        slots = [(z + 4 - d) % 4 for d in ds]
        nb = stack(r.n4, slots)
        pg = dot_nt(nb, r.w2[0])
        pu = dot_nt(nb, r.w2[1])
        act, slope = gelu_both(pg)
        hid = (act * pu).astype(BF16)
        dh = dot_nt(stack(r.c_all, slots), r.w2[2])
        dpg = (dh * pu * slope).astype(BF16)
        dpu = (dh * act).astype(BF16)
        term = dot_nn(dpg, r.w2[0]) + dot_nn(dpu, r.w2[1])
        if ds == HALVES[0]:
            ready()
        for i, (d, s) in enumerate(zip(ds, slots)):
            r.hid[s] = block(hid, i)
            r.dpg[s] = block(dpg, i)
            r.dpu[s] = block(dpu, i)
            if d == 0:
                r.own_d[...] = block(term, i)
            else:
                r.part_d[d - 1] = block(term, i).astype(BF16)
                back_d[d] = net.push(r.part_d.at[d - 1], r.recv_d.at[d - 1], z_peer(4 - d))
    unit_grads(((r.dpg, r.n4), (r.dpu, r.n4), (r.hid, r.c_all)), r.gw2)
    reducer = Reducer(net, r.gw2, r, "red")
    reducer.start()
    dn = r.own_d[...]
    for d in (1, 3, 2):
        back_d[d].wait_recv()
        dn = dn + r.recv_d[d - 1].astype(F32)
    dv, r.gg_four[...] = rms_back(dn, x, r.gain_four[...])
    c = c + dv

    for ds in HALVES:
        slots = [(z + 4 - d) % 4 for d in ds]
        term = dot_nn(stack(r.hid, slots), r.w2[2])
        for i, d in enumerate(ds):
            if d == 0:
                r.outputs[...] = x + block(term, i)
            else:
                r.part_o[d - 1] = block(term, i).astype(BF16)
                back_o[d] = net.push(r.part_o.at[d - 1], r.recv_o.at[d - 1], z_peer(4 - d))

    for k in ("wa", "kv", "pb", "q", "att", "n3", "x2"):
        loads[k].wait()
    cb = c.astype(BF16)
    datt = dot_nt(cb, r.wa[1, :, HD:]).astype(BF16)
    for h in range(HEADS):
        r.datt[h] = datt[:, h * HD : (h + 1) * HD]
    cosine = r.cosine[...]
    sine = r.sine[...]
    swap = lambda v: pltpu.roll(v, HD // 2, 1)
    pairs = r.kv[...].reshape(KEYS, 2 * HD)
    r.keys[...] = pairs[:, :HD]
    r.values[...] = pairs[:, HD:]
    datts = r.datt[...].reshape(HEADS * ROWS, HD)
    r.score[...] = dot_nt(datts, r.values[...])

    def scores(i, _):
        own = rows_at(i * 64, 64)
        dp = r.score[own, :]
        p = r.pb[own, :].astype(F32)
        ds = p * (dp - jnp.sum(p * dp, axis=-1, keepdims=True))
        r.ds[own, :] = ds.astype(BF16)
        return 0

    lax.fori_loop(0, HEADS * 2, scores, 0)
    dqs = dot_nn(r.ds[...], r.keys[...])
    for h in range(HEADS):
        dq = block(dqs, h) * (1.0 / math.sqrt(HD))
        r.dqkv[:, h * HD : (h + 1) * HD] = (dq * cosine - swap(dq) * sine).astype(BF16)
    r.turned[0] = dot_tn(r.q[...].reshape(HEADS * ROWS, HD), r.ds[...])
    r.turned[1] = dot_tn(datts, r.pb[...])
    copies = {}
    for o in (1, 2, 3, 4, 5, 6, 7, 8):
        keys = slice((8 - o) * ROWS, (9 - o) * ROWS)
        r.part_kv[o - 1, :, :HD] = r.turned[0, :, keys].T.astype(BF16)
        r.part_kv[o - 1, :, HD:] = r.turned[1, :, keys].T.astype(BF16)
        copy = net.make(r.part_kv.at[o - 1], r.recv_kv.at[o - 1], row_peer(-o))
        copies[o] = copy

        @pl.when(mp >= o)
        def _():
            copy.start()

        @pl.when(mp + o >= 16)
        def _():
            r.recv_kv[o - 1] = jnp.zeros((ROWS, 2 * HD), BF16)

    dn = dot_nt(r.dqkv[...], r.wa[0, :, :D])
    own_k = r.turned[0, :, KEYS - ROWS :].T
    own_v = r.turned[1, :, KEYS - ROWS :].T
    reducer.along_one()
    for o in range(1, 9):

        @pl.when(mp + o < 16)
        def _():
            copies[o].wait_recv()

        own_k = own_k + r.recv_kv[o - 1, :, :HD].astype(F32)
        own_v = own_v + r.recv_kv[o - 1, :, HD:].astype(F32)
    dk = (own_k * cosine - swap(own_k) * sine).astype(BF16)
    dv = own_v.astype(BF16)
    dn = dn + dot_nt(dk, r.wa[0, :, D:]) + dot_nt(dv, r.wa[1, :, :HD])
    back, r.gg_three[...] = rms_back(dn, r.x2[...], r.gain_three[...])
    c = c + back
    r.c2[...] = c
    r.c2_all[z] = c.astype(BF16)
    gather_c = spread_z(net, r.c2_all)
    n = r.n3[...].T
    att = r.att[...].T

    for t in range(4):
        cols = slice(t * 256, (t + 1) * 256)
        r.right[:, HD + t * 256 : HD + (t + 1) * 256] = dot_nn(att, cb[:, cols])
        r.score[:, cols] = dot_nn(n, r.dqkv[:, cols])
    r.score[:, D:] = dot_nn(n, dk)
    r.right[:, :HD] = dot_nn(n, dv)
    reducer.along_two()

    def lower(i, _):
        a, e, b = i // 8, i // 4 % 2, i % 4
        rows = rows_at(i * 32, 32)
        left = r.score[rows, :].reshape(4, 8, PAIR)
        right = r.right[rows, :].reshape(4, 8, PAIR)
        both = jnp.concatenate([left, right], axis=1)
        r.gw_attn[e, a, b] = both.reshape(64, PAIR).astype(BF16)
        return 0

    lax.fori_loop(0, 32, lower, 0)
    loc.store(r.gw_attn, r.out_gw_attn)
    total = r.outputs[...]
    for d in (1, 3, 2):
        back_o[d].wait_recv()
        total = total + r.recv_o[d - 1].astype(F32)
    r.outputs[...] = total
    for d in (1, 3, 2):
        gather_c[d].wait_recv()
    loc.store(r.c2_all, r.out_c2_all)
    a, b = reducer.finish()
    r.second_out[0:288, :] = a
    r.second_out[288:, :] = b
    loc.drain()
    net.drain()
    for o in range(1, 9):

        @pl.when(mp >= o)
        def _():
            copies[o].wait_send()


def middle(near, far):
    ins = [(k, v, "near") for k, v in near.items()]
    ins += [("far_" + k, v, "far") for k, v in far.items()]
    outs = [
        ("outputs", (ROWS, D), F32, "near"),
        ("c2", (ROWS, D), F32, "near"),
        ("gg_four", (1, D), F32, "near"),
        ("gg_three", (1, D), F32, "near"),
        ("second_out", (576, LANE), F32, "near"),
        ("out_gw_attn", (2, 4, 4, 64, PAIR), BF16, "far"),
        ("out_c2_all", (4, ROWS, D), BF16, "far"),
    ]
    units = ((4, ROWS, UNITS), BF16)
    third = ((3, ROWS, D), BF16)
    scratch = [(k, vm(*SAVED[k])) for k in far if k in SAVED]
    scratch += [
        ("w2", vm((3, UNITS, D), BF16)),
        ("c2_all", vm((4, ROWS, D), BF16)),
        ("score", vm((HEADS * ROWS, KEYS), F32)),
        ("keys", vm((KEYS, HD), BF16)),
        ("values", vm((KEYS, HD), BF16)),
        ("turned", vm((2, HD, KEYS), F32)),
        ("hid", vm(*units)),
        ("dpg", vm(*units)),
        ("dpu", vm(*units)),
        ("own_d", vm((ROWS, D), F32)),
        ("part_d", vm(*third)),
        ("recv_d", vm(*third)),
        ("part_o", vm(*third)),
        ("recv_o", vm(*third)),
        ("gw2", vm(*BLOCKS)),
        ("datt", vm((HEADS, ROWS, HD), BF16)),
        ("ds", vm((HEADS * ROWS, KEYS), BF16)),
        ("part_kv", vm((8, ROWS, 2 * HD), BF16)),
        ("recv_kv", vm((8, ROWS, 2 * HD), BF16)),
        ("dqkv", vm((ROWS, D), BF16)),
        ("right", vm((D, PAIR), F32)),
        ("gw_attn", vm((2, 4, 4, 64, PAIR), BF16)),
        *Reducer.scratch("red", 576, LANE),
        ("send", dma(40)),
        ("recv", dma(40)),
        ("sems", dma(16)),
    ]
    return run(middle_body, ins, outs, scratch, 2, 10**10)


def last_body(r):
    x, c, y, z = place()
    dp = lax.axis_index("dp")
    ready = greet(all_peers(False) + [xc_peer(d, 1) for d in (1, 2, 3)])
    net, loc = Net(r.send, r.recv), Local(r.sems)
    attn_in = loc.load(r.far_gw_attn, r.gw_attn)
    loads = {
        k: loc.load(getattr(r, "far_" + k), getattr(r, k))
        for k in ("w1", "pg", "pu", "c2_all", "n2", "wr", "gate", "state", "rate", "pr", "opened", "conv",
                  "mix", "n1", "gated")
    }
    need = lambda *names: [loads[k].wait() for k in names]
    upstream = r.c2[...]
    need("w1", "pg", "pu", "c2_all")
    red_attn = Reducer(net, r.gw_attn, r, "rat")
    back = {}
    for ds in HALVES:
        slots = [(z + 4 - d) % 4 for d in ds]
        pg = stack(r.pg, slots)
        pu = stack(r.pu, slots)
        act, slope = gelu_both(pg)
        hid = (act * pu).astype(BF16)
        dh = dot_nt(stack(r.c2_all, slots), r.w1[2])
        dpg = (dh * pu * slope).astype(BF16)
        dpu = (dh * act).astype(BF16)
        term = dot_nn(dpg, r.w1[0]) + dot_nn(dpu, r.w1[1])
        if ds == HALVES[0]:
            ready()
        for i, (d, s) in enumerate(zip(ds, slots)):
            r.hid[s] = block(hid, i)
            r.dpg[s] = block(dpg, i)
            r.dpu[s] = block(dpu, i)
            if d == 0:
                r.grad_tokens[...] = block(term, i)
            else:
                r.part1[d - 1] = block(term, i).astype(BF16)
                back[d] = net.push(r.part1.at[d - 1], r.recv1.at[d - 1], z_peer(4 - d))
        if ds == HALVES[0]:
            attn_in.wait()
            red_attn.start()
    red_attn.along_one()
    need("n2")
    unit_grads(((r.dpg, r.n2), (r.dpu, r.n2), (r.hid, r.c2_all)), r.gw1)
    red_first = Reducer(net, r.gw1, r, "rff")
    red_first.start()
    red_attn.along_two()
    dn = r.grad_tokens[...]
    for d in (1, 3, 2):
        back[d].wait_recv()
        dn = dn + r.recv1[d - 1].astype(F32)
    dv, gg_two = rms_back(dn, r.x1[...], r.gain_two[...])
    upstream = upstream + dv
    r.c1[...] = upstream

    r.c1_all[z] = upstream.astype(BF16)
    gather_c = spread_z(net, r.c1_all)
    a, b = red_attn.finish()
    r.z_out[0:2] = a.astype(BF16).reshape(2, 16, PAIR)
    r.z_out[2:4] = b.astype(BF16).reshape(2, 16, PAIR)
    z_in = [
        net.push(r.z_out.at[(z + d) % 4], r.z_in.at[d - 1], z_peer(d)) for d in (1, 3, 2)
    ]
    need("wr")
    for ds in STEPS:
        slots = [(z + 4 - d) % 4 for d in ds]
        for d in ds:
            if d:
                gather_c[d].wait_recv()
        term = dot_nt(stack(r.c1_all, slots), r.wr[2])
        for i, (d, s) in enumerate(zip(ds, slots)):
            r.du[rows_at(s * ROWS, ROWS), :] = block(term, i)
            if d == 0:
                red_first.along_one()
    need("gate", "state", "rate", "pr")

    def decay_of(rows, first):
        pos = positions(r.length, y * SPAN + first, CHUNK)
        loga = -8.0 * r.rate[rows, :] * lanes_of(r.pr, VEC + 7)
        return loga, jnp.exp(loga), pos

    def first_chunk(i, _):
        first = pl.multiple_of(i * CHUNK, CHUNK)
        rows = pl.ds(first, CHUNK)
        act, slope = gelu_both(r.gate[rows, :])
        dgated = r.du[rows, :]
        dgate = dgated * r.state[pl.ds(first + 8, CHUNK), :] * slope
        r.hid[i // 2, rows_at(i % 2 * CHUNK, CHUNK), 0:CH] = dgate.astype(BF16)
        r.du[rows, :] = dgated * act
        _, decay, pos = decay_of(rows, first)
        r.fac[rows, :] = jnp.where(pos > 0, decay, 0.0)
        return 0

    lax.fori_loop(0, SPAN // CHUNK, first_chunk, 0)
    row = lax.broadcasted_iota(jnp.int32, (8, CH), 0)

    def step(i, carry):
        held, prod = carry
        rows = rows_at((SPAN // 8 - 1 - i) * 8, 8)
        m = r.fac[rows, :]
        u = r.du[rows, :]
        e = m * u
        for s in (1, 2, 4):
            inside = row < 8 - s
            e = e + m * jnp.where(inside, pltpu.roll(e, 8 - s, 0), 0.0)
            m = m * jnp.where(inside, pltpu.roll(m, 8 - s, 0), 1.0)
        e = e + m * held
        m = m * prod
        r.du[rows, :] = u + jnp.where(row < 7, pltpu.roll(e, 7, 0), held)
        r.acum[rows, :] = jnp.where(row < 7, pltpu.roll(m, 7, 0), prod)
        return e[0:1, :], m[0:1, :]

    zero = jnp.zeros((1, CH), F32)
    first_e, first_m = lax.fori_loop(0, SPAN // 8, step, (zero, zero + 1.0), unroll=4)
    edges_in = share_edges(net, r.edges, first_m, first_e)
    need("opened", "conv", "mix", "n1", "gated")

    def output_grads(out, w, left, right):
        for half in range(2):
            cut = left[:, :, half * 256 : half * 256 + 256].reshape(SPAN, 256)
            grad = dot_tn(cut, right[...].reshape(SPAN, D))
            for j in range(2):
                for part in range(8):
                    out[part % 2, part // 2, half * 2 + j, w * BW : (w + 1) * BW, :] = grad[
                        j * LANE : j * LANE + BW, part * LANE : (part + 1) * LANE
                    ].astype(BF16)

    output_grads(r.gwa, 0, r.hid, r.n1)
    output_grads(r.gwa, 1, r.gated, r.c1_all)
    red_a = Reducer(net, r.gwa, r, "rea")
    red_a.start()
    for copy in edges_in:
        copy.wait_recv()
    held = zero
    for b in (3, 2, 1):
        held = jnp.where(b > y, r.edges[b, 0:1, :] * held + r.edges[b, 1:2, :], held)

    def second_chunk(i, dsp):
        first = pl.multiple_of(i * CHUNK, CHUNK)
        rows = pl.ds(first, CHUNK)
        ds = r.du[rows, :] + r.acum[rows, :] * held
        loga, decay, pos = decay_of(rows, first)
        rate = r.rate[rows, :]
        opened = r.opened[rows, :]
        conv = r.conv[rows, :]
        before = r.state[pl.ds(first, CHUNK + 8), :][7 : 7 + CHUNK, :]
        beta = jnp.sqrt(neg_expm1(2.0 * loga))
        dloga = jnp.where(pos > 0, ds * before * decay, 0.0)
        dloga = dloga - ds * opened * conv * (decay * decay) / beta
        dopened = ds * beta * conv
        r.du[rows, :] = ds * beta * opened
        r.acum[rows, :] = dloga * (-8.0 * lanes_of(r.pr, VEC + 7)) * rate * (1.0 - rate)
        r.fac[rows, :] = dopened * opened * (1.0 - opened)
        return dsp + jnp.sum(dloga * (-8.0 * rate), axis=0, keepdims=True)

    dsp = lax.fori_loop(0, SPAN // CHUNK, second_chunk, zero)
    for b in range(4):
        cols = slice(b * LANE, (b + 1) * LANE)
        r.du[0:SPAN, cols] = (
            r.du[0:SPAN, cols]
            + jnp.pad(
                low_dot(r.acum[:, cols], r.pr[b, 0:BW, :], ((1,), (1,)))
                + low_dot(r.fac[:, cols], r.pr[b, BW : 2 * BW, :], ((1,), (1,))),
                ((0, 0), (0, LANE - BW)),
            )
        )
    halo = net.make(r.du.at[0:8], r.du.at[SPAN : SPAN + 8], y_peer(3))

    @pl.when(y > 0)
    def _():
        halo.start()

    @pl.when(y == 3)
    def _():
        r.du[SPAN : SPAN + 8, :] = jnp.zeros((8, CH), F32)

    red_first.along_two()
    for b in range(4):
        cols = slice(b * LANE, (b + 1) * LANE)
        left = r.conv[:, b * LANE : b * LANE + BW]
        r.gp[b, 0:BW, :] = low_dot(left, r.acum[:, cols], ((0,), (0,)))
        r.gp[b, BW : 2 * BW, :] = low_dot(left, r.fac[:, cols], ((0,), (0,)))
    red_a.along_one()

    @pl.when(y < 3)
    def _():
        halo.wait_recv()

    def third_chunk(i, sums):
        first = pl.multiple_of(i * CHUNK, CHUNK)
        rows = pl.ds(first, CHUNK)
        pos = positions(r.length, y * SPAN + first, CHUNK + 8)
        dwin = r.du[pl.ds(first, CHUNK + 8), :]
        mwin = r.mix[pl.ds(first, CHUNK + 8), :]
        dconv = dwin[:CHUNK, :]
        total = lanes_of(r.pr, VEC) * dconv
        taps = [jnp.sum(dconv * mwin[8:, :], axis=0, keepdims=True)]
        for k in (1, 2, 3):
            masked = jnp.where(pos >= k, dwin, 0.0)
            total = total + lanes_of(r.pr, VEC + k) * masked[k : k + CHUNK, :]
            taps.append(
                jnp.sum(masked[:CHUNK, :] * mwin[8 - k : 8 - k + CHUNK, :], axis=0, keepdims=True)
            )
        r.dpg[i // 2, rows_at(i % 2 * CHUNK, CHUNK), 0:CH] = total.astype(BF16)
        taps.append(jnp.sum(dconv, axis=0, keepdims=True))
        taps.append(jnp.sum(r.acum[rows, :], axis=0, keepdims=True))
        taps.append(jnp.sum(r.fac[rows, :], axis=0, keepdims=True))
        return tuple(a + b for a, b in zip(sums, taps))

    sums = lax.fori_loop(0, SPAN // CHUNK, third_chunk, (zero,) * 7)
    back = {}
    for ds in HALVES:
        slots = [(z + 4 - d) % 4 for d in ds]
        mixes = stack(r.dpg, slots)[:, 0:CH]
        gates = stack(r.hid, slots)[:, 0:CH]
        term = dot_nn(mixes, r.wr[0]) + dot_nn(gates, r.wr[1])
        for i, d in enumerate(ds):
            if d:
                r.part2[d - 1] = block(term, i).astype(BF16)
                back[d] = net.push(r.part2.at[d - 1], r.recv2.at[d - 1], z_peer(4 - d))
            else:
                r.grad_tokens[...] = block(term, i)
    output_grads(r.gwb, 0, r.dpg, r.n1)
    for b in range(4):
        cols = slice(b * LANE, (b + 1) * LANE)
        for k, row_sum in enumerate(sums + (dsp,)):
            r.gp[b, VEC + k : VEC + k + 1, :] = row_sum[:, cols]
        r.gp[b, 200:, :] = jnp.zeros((56, LANE), F32)
        for part in range(8):
            r.gwb[part % 2, part // 2, b, BW:, :] = r.gp[
                b, part * 32 : part * 32 + 32, :
            ].astype(BF16)
    red_b = Reducer(net, r.gwb, r, "reb")
    red_b.start()
    red_a.along_two()

    def spread(stage, first, peers):
        r.gain_out[stage] = r.gains[...]
        return [
            net.push(r.gain_out.at[stage], r.gain_in.at[first + i], peer)
            for i, peer in enumerate(peers)
        ]

    def collect(first, mine):
        total = r.gains[...]
        for i, copy in enumerate(mine):
            copy.wait_recv()
            total = total + r.gain_in[first + i]
        r.gains[...] = total

    def share(reducer, whole):
        a, b = reducer.finish()
        half = reducer.half
        whole[dp, 0:half, :] = a.astype(BF16)
        whole[dp, half:, :] = b.astype(BF16)
        cut = whole.at[dp]
        return [
            net.push(cut, cut, xc_peer(dx, dc))
            for dx, dc in ((1, 0), (3, 0), (2, 0), (1, 1), (3, 1), (2, 1), (0, 1))
        ]

    red_b.along_one()
    dn = r.grad_tokens[...]
    for d in (1, 3, 2):
        back[d].wait_recv()
        dn = dn + r.recv2[d - 1].astype(F32)
    dv, gg_one = rms_back(dn, r.tok[...].astype(F32), r.gain_one[...])
    r.grad_tokens[...] = r.c1[...] + dv
    r.gains[...] = jnp.concatenate(
        [gg_one, gg_two, r.gg_three[...], r.gg_four[...], jnp.zeros((4, D), F32)], axis=0
    )
    mine = spread(0, 0, [xc_peer(0, 1)])
    shares = share(red_a, r.recur_a)
    collect(0, mine)
    mine = spread(1, 1, [xc_peer(d, 0) for d in (1, 3, 2)])
    red_b.along_two()
    a, b = red_first.finish()
    r.first_out[0:288, :] = a
    r.first_out[288:, :] = b
    collect(1, mine)
    mine = spread(2, 4, [y_peer(d) for d in (1, 3, 2)])
    shares += share(red_b, r.recur_b)
    total = r.z_out[z].astype(F32)
    for copy in z_in:
        copy.wait_recv()
    for d in range(3):
        total = total + r.z_in[d].astype(F32)
    r.attn_out[...] = total
    collect(4, mine)
    mine = spread(3, 7, [z_peer(d) for d in (1, 3, 2)])
    collect(7, mine)
    for copy in shares:
        copy.wait_recv()
    net.drain()

    @pl.when(y > 0)
    def _():
        halo.wait_send()


def last(near, far):
    ins = [(k, v, "near") for k, v in near.items()]
    ins += [("far_" + k, v, "far") for k, v in far.items()]
    outs = [
        ("grad_tokens", (ROWS, D), F32, "near"),
        ("gains", (8, D), F32, "near"),
        ("first_out", (576, LANE), F32, "near"),
        ("attn_out", (16, PAIR), F32, "near"),
        ("recur_a", (8, 192, LANE), BF16, "near"),
        ("recur_b", (8, 128, LANE), BF16, "near"),
    ]
    units = ((4, ROWS, UNITS), BF16)
    third = ((3, ROWS, D), BF16)
    whole = ((4, ROWS, D), BF16)
    scratch = [(k, vm(*SAVED[k])) for k in far if k in SAVED]
    scratch += [
        ("gw_attn", vm((2, 4, 4, 64, PAIR), BF16)),
        ("c2_all", vm(*whole)),
        ("c1_all", vm(*whole)),
        ("c1", vm((ROWS, D), F32)),
        ("hid", vm(*units)),
        ("dpg", vm(*units)),
        ("dpu", vm(*units)),
        ("part1", vm(*third)),
        ("recv1", vm(*third)),
        ("part2", vm(*third)),
        ("recv2", vm(*third)),
        ("gw1", vm(*BLOCKS)),
        ("z_out", vm((4, 16, PAIR), BF16)),
        ("z_in", vm((3, 16, PAIR), BF16)),
        ("du", vm(*TALL)),
        ("fac", vm(*BIG)),
        ("acum", vm(*BIG)),
        ("edges", vm((4, 8, CH), F32)),
        ("gp", vm((4, 256, LANE), F32)),
        ("gwa", vm((2, 4, 4, 192, LANE), BF16)),
        ("gwb", vm((2, 4, 4, 128, LANE), BF16)),
        ("gain_in", vm((10, 8, D), F32)),
        ("gain_out", vm((4, 8, D), F32)),
        *Reducer.scratch("rat", 64, PAIR),
        *Reducer.scratch("rff", 576, LANE),
        *Reducer.scratch("rea", 192, LANE),
        *Reducer.scratch("reb", 128, LANE),
        ("send", dma(96)),
        ("recv", dma(96)),
        ("sems", dma(17)),
    ]
    return run(last_body, ins, outs, scratch, 3, 10**10)


def output_body(r):
    r.outputs[...] = r.in_outputs[...]
    r.tokens[...] = r.in_tokens[...]
    for i, name in enumerate(("norm_one", "norm_two", "norm_three", "norm_four")):
        getattr(r, name)[...] = r.gains[i : i + 1, :]
    for part in range(8):
        rows = slice(part * LANE, (part + 1) * LANE)
        r.recur_gate[:, rows] = r.recur_a[part, 0:BW, :].astype(F32)
        r.recur_output[:, rows] = r.recur_a[part, BW:, :].astype(F32)
        r.recur_input[:, rows] = r.recur_b[part, 0:BW, :].astype(F32)
    params = r.recur_b[:, BW:, :].astype(F32).reshape(256, LANE)
    r.decay_gate[0] = params[0:BW, :BW]
    r.input_gate[0] = params[BW : 2 * BW, :BW]
    r.conv_kernel[...] = params[VEC : VEC + 4, :BW]
    r.conv_bias[...] = params[VEC + 4 : VEC + 5, :BW]
    r.decay_shift[...] = params[VEC + 5 : VEC + 6, :BW]
    r.input_shift[...] = params[VEC + 6 : VEC + 7, :BW]
    r.decay_param[...] = params[VEC + 7 : VEC + 8, :BW] * r.slope[...]
    for name in ("first", "second"):
        summed = getattr(r, name)
        getattr(r, name + "_gate")[...] = summed[0:192, :]
        getattr(r, name + "_value")[...] = summed[192:384, :]
        getattr(r, name + "_down")[...] = summed[384:, :]
    r.query_proj[...] = r.attn[0:8, :D]
    r.key_proj[...] = r.attn[0:8, D:]
    r.value_proj[...] = r.attn[8:16, :HD]
    r.attn_output[...] = r.attn[8:16, HD:]


OUTPUTS = (
    ("outputs", (ROWS, D)), ("tokens", (ROWS, D)), ("norm_one", (1, D)),
    ("recur_input", (BW, D)), ("recur_gate", (BW, D)), ("conv_kernel", (4, BW)),
    ("conv_bias", (1, BW)), ("decay_gate", (1, BW, BW)), ("decay_shift", (1, BW)),
    ("input_gate", (1, BW, BW)), ("input_shift", (1, BW)), ("decay_param", (1, BW)),
    ("recur_output", (BW, D)), ("norm_two", (1, D)), ("first_gate", (192, 128)),
    ("first_value", (192, 128)), ("first_down", (192, 128)), ("norm_three", (1, D)),
    ("query_proj", (8, D)), ("key_proj", (8, HD)), ("value_proj", (8, HD)),
    ("attn_output", (8, D)), ("norm_four", (1, D)), ("second_gate", (192, 128)),
    ("second_value", (192, 128)), ("second_down", (192, 128)),
)
FLAT = (
    "norm_one", "conv_bias", "decay_shift", "input_shift", "decay_param", "norm_two",
    "norm_three", "norm_four",
)
TURNED = (
    "recur_input", "recur_gate", "first_gate", "first_value", "second_gate", "second_value",
)


def local(
    tokens, lengths, cotangent, norm_one, recur_input, recur_gate, conv_kernel, conv_bias,
    decay_gate, decay_shift, input_gate, input_shift, decay_param, recur_output, norm_two,
    first_gate, first_value, first_down, norm_three, query_proj, key_proj, value_proj,
    attn_output, norm_four, second_gate, second_value, second_down,
):
    length = jnp.broadcast_to(lengths.reshape(1, 1), (1, LANE))
    gain_one, gain_two, gain_three, gain_four = (
        g.reshape(1, D) for g in (norm_one, norm_two, norm_three, norm_four)
    )
    flat = lambda v: v.reshape(1, BW)

    index = lax.axis_index("mp") * ROWS + jnp.arange(ROWS, dtype=jnp.int32)
    position = jnp.where(index >= lengths[0], index - lengths[0], index)
    frequency = 10000.0 ** (-2.0 * jnp.arange(HD // 2, dtype=F32) / HD)
    angle = position.astype(F32)[:, None] * frequency[None, :]
    cosine = jnp.concatenate([jnp.cos(angle)] * 2, axis=1)
    sine = jnp.concatenate([-jnp.sin(angle), jnp.sin(angle)], axis=1)

    saved = forward(
        dict(
            tok=tokens, cot=cotangent, length=length, cosine=cosine, sine=sine,
            gain_one=gain_one, gain_two=gain_two, gain_three=gain_three,
            gain_four=gain_four, recur_input=recur_input.T, recur_gate=recur_gate.T, recur_output=recur_output,
            conv_kernel=conv_kernel, conv_bias=flat(conv_bias), decay_gate=decay_gate,
            decay_shift=flat(decay_shift), input_gate=input_gate,
            input_shift=flat(input_shift), softplus=flat(jax.nn.softplus(-decay_param)),
            first_gate=first_gate.T, first_value=first_value.T, first_down=first_down,
            query_proj=query_proj, key_proj=key_proj, value_proj=value_proj,
            attn_output=attn_output, second_gate=second_gate.T, second_value=second_value.T,
            second_down=second_down,
        )
    )
    kept = lambda *names: {k: saved["out_" + k] for k in names}
    mid = middle(
        dict(
            x3=saved["out_x3"], cot=cotangent, gain_four=gain_four, gain_three=gain_three,
            cosine=cosine, sine=sine,
        ),
        kept("w2", "n4", "c_all", "wa", "kv", "pb", "q", "att", "n3", "x2"),
    )
    end = last(
        dict(
            c2=mid["c2"], x1=saved["out_x1"], tok=tokens, length=length, gain_one=gain_one,
            gain_two=gain_two, gg_three=mid["gg_three"], gg_four=mid["gg_four"],
        ),
        dict(
            kept(
                "w1", "pg", "pu", "n2", "wr", "gate", "state", "rate", "pr", "opened", "conv",
                "mix", "n1", "gated",
            ),
            gw_attn=mid["out_gw_attn"],
            c2_all=mid["out_c2_all"],
        ),
    )
    results = run(
        output_body,
        [
            ("in_outputs", mid["outputs"], "near"),
            ("in_tokens", end["grad_tokens"], "near"),
            ("gains", end["gains"], "near"),
            ("recur_a", end["recur_a"], "near"),
            ("recur_b", end["recur_b"], "near"),
            ("first", end["first_out"], "near"),
            ("second", mid["second_out"], "near"),
            ("attn", end["attn_out"], "near"),
            ("slope", flat(-jax.nn.sigmoid(-decay_param)), "near"),
        ],
        [(name, shape, F32, "near") for name, shape in OUTPUTS],
        [],
    )
    for name in FLAT:
        results[name] = results[name].reshape(-1)
    for name in TURNED:
        results[name] = results[name].T
    return tuple(results[name] for name, _ in OUTPUTS)


def solution(mesh):
    rows = P(("dp", "mp"), None)
    cols = P(None, "mp")
    one = P("mp")
    blocks = P("mp", None, None)
    tile = P("dp", "mp")
    weights = (
        P(), cols, cols, cols, one, blocks, one, blocks, one, one, P("mp", None),
        P(), tile, tile, P("mp", "dp"),
        P(), rows, rows, rows, rows,
        P(), tile, tile, P("mp", "dp"),
    )
    return jax.shard_map(
        local,
        mesh=mesh,
        in_specs=(rows, P("dp"), rows, *weights),
        out_specs=(rows, rows, *weights),
        check_vma=False,
    )
```

```python
import math
from types import SimpleNamespace

import jax
import jax.numpy as jnp
from jax import lax
from jax.experimental import pallas as pl
from jax.experimental.pallas import tpu as pltpu
from jax.sharding import PartitionSpec as P

MESH = pl.DeviceIdType.MESH
F32 = jnp.float32
BF16 = jnp.bfloat16
VMEM_BYTES = 63 * 2**20

D = 1024
ROWS = 128
SPAN = 512
LANE = 128
BW = 96
CH = 4 * LANE
PAR = 208
VEC = 192
UNITS = 768
HEADS = 8
HD = 128
WINDOW = 1024
KEYS = 1152
PAIR = 1152
CHUNK = 64
STEPS = ((0,), (1, 3), (2,))
HALVES = ((1, 3), (2, 0))
OTHERS = ((0, 1), (1, 0), (3, 0), (2, 0), (1, 1), (3, 1), (2, 1))
GELU_C = math.sqrt(2.0 / math.pi)


def place():
    dp, mp = lax.axis_index("dp"), lax.axis_index("mp")
    return dp // 2, dp % 2, mp // 4, mp % 4


def z_peer(d):
    _, _, y, z = place()
    return {"mp": y * 4 + (z + d) % 4}


def y_peer(d):
    _, _, y, z = place()
    return {"mp": ((y + d) % 4) * 4 + z}


def xc_peer(dx, dc):
    x, c, _, _ = place()
    return {"dp": ((x + dx) % 4) * 2 + (c + dc) % 2}


def row_peer(offset):
    return {"mp": lax.rem(lax.axis_index("mp") + 16 + offset, 16)}


def all_peers():
    return [xc_peer(0, 1)] + [xc_peer(d, 0) for d in (1, 2, 3)] + [row_peer(o) for o in range(1, 16)]


def greet(peers):
    barrier = pltpu.get_barrier_semaphore()
    for peer in peers:
        pl.semaphore_signal(barrier, inc=1, device_id=peer, device_id_type=MESH)
    return lambda: pl.semaphore_wait(barrier, len(peers))


class Net:
    def __init__(self, send, recv):
        self.send, self.recv, self.used, self.started = send, recv, 0, []
        self.landing = {}

    def make(self, src, dst, peer, shared=None):
        landing = self.landing.setdefault(shared, self.used) if shared else self.used
        copy = pltpu.make_async_remote_copy(
            src_ref=src,
            dst_ref=dst,
            send_sem=self.send.at[self.used],
            recv_sem=self.recv.at[landing],
            device_id=peer,
            device_id_type=MESH,
        )
        self.used += 1
        return copy

    def push(self, src, dst, peer):
        copy = self.make(src, dst, peer)
        copy.start()
        self.started.append(copy)
        return copy

    def drain(self):
        for copy in self.started:
            copy.wait_send()


class Local:
    def __init__(self, sems):
        self.sems, self.used, self.stores = sems, 0, []

    def load(self, src, dst):
        copy = pltpu.make_async_copy(src, dst, self.sems.at[self.used])
        self.used += 1
        copy.start()
        return copy

    def store(self, src, dst):
        self.stores.append(self.load(src, dst))

    def drain(self):
        for copy in self.stores:
            copy.wait()


def run(body, ins, outs, scratch, collective_id=None, flops=0):
    names = [n for n, _, _ in ins] + [n for n, _, _, _ in outs] + [n for n, _ in scratch]
    space = {"near": pltpu.VMEM, "far": pl.ANY}

    def kernel(*refs):
        body(SimpleNamespace(**dict(zip(names, refs))))

    results = pl.pallas_call(
        kernel,
        out_shape=[jax.ShapeDtypeStruct(s, t) for _, s, t, _ in outs],
        in_specs=[pl.BlockSpec(memory_space=space[where]) for _, _, where in ins],
        out_specs=[pl.BlockSpec(memory_space=space[where]) for _, _, _, where in outs],
        scratch_shapes=[s for _, s in scratch],
        compiler_params=pltpu.CompilerParams(
            collective_id=collective_id,
            has_side_effects=collective_id is not None,
            vmem_limit_bytes=VMEM_BYTES,
        ),
        cost_estimate=pl.CostEstimate(flops=flops, bytes_accessed=2**24, transcendentals=0),
    )(*[a for _, a, _ in ins])
    return dict(zip([n for n, _, _, _ in outs], results))


def vm(shape, dtype):
    return pltpu.VMEM(shape, dtype)


def dma(n):
    return pltpu.SemaphoreType.DMA((n,))


def dot_nn(a, b, **kw):
    return lax.dot_general(a, b, (((1,), (0,)), ((), ())), preferred_element_type=F32, **kw)


def dot_nt(a, b, **kw):
    return lax.dot_general(a, b, (((1,), (1,)), ((), ())), preferred_element_type=F32, **kw)


def dot_tn(a, b, **kw):
    return lax.dot_general(a, b, (((0,), (0,)), ((), ())), preferred_element_type=F32, **kw)


def gelu(v):
    return 0.5 * v * (1.0 + jnp.tanh(GELU_C * (v + 0.044715 * v * v * v)))


def gelu_both(v):
    t = jnp.tanh(GELU_C * (v + 0.044715 * v * v * v))
    value = 0.5 * v * (1.0 + t)
    slope = 0.5 * (1.0 + t) + 0.5 * v * (1.0 - t * t) * GELU_C * (1.0 + 3.0 * 0.044715 * v * v)
    return value, slope


def rms(v, gain):
    return v * lax.rsqrt(jnp.mean(v * v, axis=-1, keepdims=True) + 1e-06) * gain


def rms_back(dn, v, gain):
    r = lax.rsqrt(jnp.mean(v * v, axis=-1, keepdims=True) + 1e-06)
    grad_gain = jnp.sum(dn * v * r, axis=0, keepdims=True)
    dg = dn * gain
    dv = r * dg - v * (r * r * r) * jnp.mean(dg * v, axis=-1, keepdims=True)
    return dv, grad_gain


def stack(ref, slots):
    return jnp.concatenate([ref[s] for s in slots], axis=0) if len(slots) > 1 else ref[slots[0]]


def block(value, i):
    return value[i * ROWS : (i + 1) * ROWS]


def low_dot(left, right, dims):
    return lax.dot_general(
        left.astype(BF16), right.astype(BF16), (dims, ((), ())), preferred_element_type=F32
    )


def rows_at(first, count):
    return pl.ds(pl.multiple_of(first, count), count)


class Gatherer:
    def __init__(self, net, own, whole):
        self.net, self.own, self.whole, self.half = net, own, whole, whole.shape[3] // 2

    def start(self):
        x, c, y, _ = place()
        one, two = slice(0, self.half), slice(self.half, 2 * self.half)
        self.whole[c, x, y] = self.own[...]
        self.first = []
        for d in (1, 3, 2):
            for part, peer in ((one, xc_peer(d, 0)), (two, y_peer(d))):
                self.first.append(
                    self.net.push(self.own.at[part, :], self.whole.at[c, x, y, part, :], peer)
                )

    def along(self):
        x, c, y, _ = place()
        one, two = slice(0, self.half), slice(self.half, 2 * self.half)
        for copy in self.first:
            copy.wait_recv()
        self.second = []
        for d in (1, 3, 2):
            mine = self.whole.at[c, :, y, one, :]
            self.second.append(self.net.push(mine, mine, y_peer(d)))
            mine = self.whole.at[c, x, :, two, :]
            self.second.append(self.net.push(mine, mine, xc_peer(d, 0)))

    def across(self):
        _, c, _, _ = place()
        for copy in self.second:
            copy.wait_recv()
        mine = self.whole.at[c]
        self.third = self.net.push(mine, mine, xc_peer(0, 1))

    def finish(self):
        self.third.wait_recv()


class Reducer:
    @staticmethod
    def scratch(name, rows, lanes):
        half = rows // 2
        return [
            (name + "_other", vm((4, 4, rows, lanes), BF16)),
            (name + "_in_a", vm((3, 4, half, lanes), BF16)),
            (name + "_in_b", vm((3, 4, half, lanes), BF16)),
            (name + "_sum_a", vm((4, half, lanes), BF16)),
            (name + "_sum_b", vm((4, half, lanes), BF16)),
            (name + "_last_a", vm((3, half, lanes), BF16)),
            (name + "_last_b", vm((3, half, lanes), BF16)),
        ]

    def __init__(self, net, src, r, name):
        self.net, self.src, self.half = net, src, src.shape[3] // 2
        for part in ("other", "in_a", "in_b", "sum_a", "sum_b", "last_a", "last_b"):
            setattr(self, part, getattr(r, name + "_" + part))

    def start(self):
        _, c, _, _ = place()
        self.first = self.net.push(self.src.at[1 - c], self.other, xc_peer(0, 1))

    def along_one(self):
        x, c, y, _ = place()
        half = self.half
        self.first.wait_recv()

        def add(i, _):
            a, b = i // 4, i % 4
            total = self.src[c, a, b].astype(F32) + self.other[a, b].astype(F32)
            self.other[a, b] = total.astype(BF16)
            return 0

        lax.fori_loop(0, 16, add, 0)
        self.second = []
        for d in (1, 3, 2):
            mine = self.other.at[(x + d) % 4, :, 0:half, :]
            self.second.append(self.net.push(mine, self.in_a.at[d - 1], xc_peer(d, 0)))
            mine = self.other.at[:, (y + d) % 4, half : 2 * half, :]
            self.second.append(self.net.push(mine, self.in_b.at[d - 1], y_peer(d)))

    def along_two(self):
        x, _, y, _ = place()
        half = self.half
        for copy in self.second:
            copy.wait_recv()

        def add(i, _):
            a = self.other[x, i, 0:half, :].astype(F32)
            b = self.other[i, y, half : 2 * half, :].astype(F32)
            for d in range(3):
                a = a + self.in_a[d, i].astype(F32)
                b = b + self.in_b[d, i].astype(F32)
            self.sum_a[i] = a.astype(BF16)
            self.sum_b[i] = b.astype(BF16)
            return 0

        lax.fori_loop(0, 4, add, 0)
        self.third = []
        for d in (1, 3, 2):
            mine = self.sum_a.at[(y + d) % 4]
            self.third.append(self.net.push(mine, self.last_a.at[d - 1], y_peer(d)))
            mine = self.sum_b.at[(x + d) % 4]
            self.third.append(self.net.push(mine, self.last_b.at[d - 1], xc_peer(d, 0)))

    def finish(self):
        x, _, y, _ = place()
        for copy in self.third:
            copy.wait_recv()
        a = self.sum_a[y].astype(F32)
        b = self.sum_b[x].astype(F32)
        for d in range(3):
            a = a + self.last_a[d].astype(F32)
            b = b + self.last_b[d].astype(F32)
        return a, b


def spread_z(net, ref):
    z = place()[3]
    return {d: net.push(ref.at[z], ref.at[z], z_peer(d)) for d in (1, 3, 2)}


def place_units(local, whole, w_ref):
    copies = []
    for part in range(8):
        for y in range(4):
            for w in range(3):
                copies.append(
                    local.load(
                        whole.at[part % 2, part // 2, y, w * 192 : (w + 1) * 192, :],
                        w_ref.at[
                            w, y * 192 : (y + 1) * 192, part * LANE : (part + 1) * LANE
                        ],
                    )
                )
    return copies


def unit_grads(sides, out):
    for w, (left, right) in enumerate(sides):
        right = right[...].reshape(SPAN, D)
        for tile in range(3):
            cut = left[:, :, tile * 256 : tile * 256 + 256].reshape(SPAN, 256)
            grad = dot_tn(cut, right)
            first = tile * 256
            while first < tile * 256 + 256:
                block = first // 192
                last = min((block + 1) * 192, tile * 256 + 256)
                rows = grad[first - tile * 256 : last - tile * 256]
                start = w * 192 + first - block * 192
                for part in range(8):
                    out[part % 2, part // 2, block, start : start + last - first, :] = rows[
                        :, part * LANE : (part + 1) * LANE
                    ].astype(BF16)
                first = last


def positions(length, first, rows):
    t = lax.broadcasted_iota(jnp.int32, (rows, CH), 0) + first
    wide = jnp.concatenate([length[...]] * 4, axis=1)
    return jnp.where(t >= wide, t - wide, t)


def lanes_of(pr, row):
    return jnp.concatenate([pr[b, row : row + 1, :] for b in range(4)], axis=1)


def neg_expm1(v):
    series = v * (
        1.0 + v * (0.5 + v * (1.0 / 6 + v * (1.0 / 24 + v * (1.0 / 120 + v * (1.0 / 720)))))
    )
    return -jnp.where(v > -0.25, series, jnp.exp(v) - 1.0)


def share_edges(net, edges, prod, last):
    y = place()[2]
    edges[y, 0:1, :] = prod
    edges[y, 1:2, :] = last
    return [net.push(edges.at[y], edges.at[y], y_peer(d)) for d in (1, 3, 2)]


def forward_body(r):
    x, c, y, z = place()
    mp = lax.axis_index("mp")
    ready = greet(all_peers())
    net, loc = Net(r.send, r.recv), Local(r.sems)

    tokens = r.tok[...].astype(F32)
    r.n1[z] = rms(tokens, r.gain_one[...]).astype(BF16)
    mine = pl.ds(pl.multiple_of(y * LANE, LANE), BW)
    r.wr[0, mine, :] = r.recur_input[...]
    r.wr[1, mine, :] = r.recur_gate[...]
    r.wr[2, mine, :] = r.recur_output[...]
    for b in range(4):
        r.wr[:, b * LANE + BW : (b + 1) * LANE, :] = jnp.zeros((3, LANE - BW, D), BF16)
    r.pr[y] = jnp.zeros((PAR, LANE), F32)
    r.pr[y, 0:BW, 0:BW] = r.decay_gate[0]
    r.pr[y, BW : 2 * BW, 0:BW] = r.input_gate[0]
    r.pr[y, VEC : VEC + 4, 0:BW] = r.conv_kernel[...]
    r.pr[y, VEC + 4 : VEC + 5, 0:BW] = r.conv_bias[...]
    r.pr[y, VEC + 5 : VEC + 6, 0:BW] = r.decay_shift[...]
    r.pr[y, VEC + 6 : VEC + 7, 0:BW] = r.input_shift[...]
    r.pr[y, VEC + 7 : VEC + 8, :] = jnp.ones((1, LANE), F32)
    decay = r.decay_param[...]
    r.pr[y, VEC + 7 : VEC + 8, 0:BW] = jnp.maximum(-decay, 0.0) + jnp.log1p(
        jnp.exp(-jnp.abs(decay))
    )
    ready()
    gather_n1 = spread_z(net, r.n1)
    half = pl.ds(pl.multiple_of(c * 512, 512), 512)
    part_p = pl.ds(pl.multiple_of(c * 104, 8), 104)
    weights_in, shared = {}, []
    for d in (1, 3, 2):
        cut = r.wr.at[0, mine, half]
        weights_in[d, 0] = net.push(cut, cut, y_peer(d))
    for d in (1, 3, 2):
        cut = r.pr.at[y, part_p, :]
        weights_in[d, 1] = net.push(cut, cut, y_peer(d))

    tail = r.n1.at[3, ROWS - 16 :, :]
    halos = [net.make(tail, r.halo, {"mp": (y * 4 + 4 + i) % 16}, "halo") for i in range(4)]

    @pl.when((z == 3) & (y < 3))
    def _():
        for halo in halos:
            halo.start()

    @pl.when(y == 0)
    def _():
        r.halo[...] = jnp.zeros((16, D), BF16)

    r.own_first[0:192, :] = r.first_gate[...]
    r.own_first[192:384, :] = r.first_value[...]
    r.own_first[384:576, :] = r.first_down[...]
    left = jnp.concatenate([r.query_proj[...], r.key_proj[...]], axis=1).astype(F32)
    right = jnp.concatenate([r.value_proj[...], r.attn_output[...]], axis=1).astype(F32)
    r.own_attn[rows_at(z * 16, 16), :] = jnp.concatenate([left, right], axis=0).astype(BF16)
    r.own_second[0:192, :] = r.second_gate[...]
    r.own_second[192:384, :] = r.second_value[...]
    r.own_second[384:576, :] = r.second_down[...]
    first_w = Gatherer(net, r.own_first, r.all_first)
    attn_w = Gatherer(net, r.own_attn, r.all_attn)
    second_w = Gatherer(net, r.own_second, r.all_second)

    def pass_on(kind):
        for d in (1, 3, 2):
            weights_in[d, kind].wait_recv()
            start = (y + 4 - d) % 4
            rows = pl.ds(pl.multiple_of(start * LANE, LANE), BW)
            if kind == 0:
                cut = r.wr.at[0, rows, half]
            elif kind == 1:
                cut = r.pr.at[start, part_p, :]
            else:
                cut = r.wr.at[1:3, rows, half]
            shared.append((kind, net.push(cut, cut, xc_peer(0, 1))))

    def arrived(kind):
        for k, copy in shared:
            if k == kind:
                copy.wait_recv()

    pass_on(0)
    for d in (1, 3, 2):
        cut = r.wr.at[1:3, mine, half]
        weights_in[d, 2] = net.push(cut, cut, y_peer(d))
    pass_on(1)
    for d in (1, 3, 2):
        gather_n1[d].wait_recv()
    r.c_all[z] = r.cot[...]
    gather_c = spread_z(net, r.c_all)
    cut = r.own_attn.at[rows_at(z * 16, 16), :]
    attn_z = [net.push(cut, cut, z_peer(d)) for d in (1, 3, 2)]
    arrived(0)
    rows_n = r.n1[...].reshape(SPAN, D)
    r.mix[8:, :] = dot_nt(rows_n, r.wr[0])

    @pl.when(y > 0)
    def _():
        halos[0].wait_recv()

    r.mix[0:8, :] = dot_nt(r.halo[...], r.wr[0])[8:, :]
    loc.store(r.n1, r.out_n1)
    loc.store(r.mix, r.out_mix)
    arrived(1)
    loc.store(r.pr, r.out_pr)
    def conv_chunk(i, _):
        first = pl.multiple_of(i * CHUNK, CHUNK)
        pos = positions(r.length, y * SPAN + first, CHUNK)
        window = r.mix[pl.ds(first, CHUNK + 8), :]
        total = lanes_of(r.pr, VEC + 4) + lanes_of(r.pr, VEC) * window[8:, :]
        for k in (1, 2, 3):
            lagged = window[8 - k : 8 - k + CHUNK, :]
            total = total + jnp.where(pos >= k, lanes_of(r.pr, VEC + k) * lagged, 0.0)
        r.conv[pl.ds(first, CHUNK), :] = total
        return 0

    lax.fori_loop(0, SPAN // CHUNK, conv_chunk, 0)
    loc.store(r.conv, r.out_conv)
    for b in range(4):
        cols = slice(b * LANE, (b + 1) * LANE)
        left = r.conv[:, b * LANE : b * LANE + BW]
        r.rate[:, cols] = low_dot(left, r.pr[b, 0:BW, :], ((1,), (0,)))
        r.opened[:, cols] = low_dot(left, r.pr[b, BW : 2 * BW, :], ((1,), (0,)))

    def gates_chunk(i, _):
        first = pl.multiple_of(i * CHUNK, CHUNK)
        rows = pl.ds(first, CHUNK)
        pos = positions(r.length, y * SPAN + first, CHUNK)
        rate = jax.nn.sigmoid(r.rate[rows, :] + lanes_of(r.pr, VEC + 5))
        opened = jax.nn.sigmoid(r.opened[rows, :] + lanes_of(r.pr, VEC + 6))
        loga = -8.0 * rate * lanes_of(r.pr, VEC + 7)
        r.rate[rows, :] = rate
        r.opened[rows, :] = opened
        r.fac[rows, :] = jnp.where(pos > 0, jnp.exp(loga), 0.0)
        r.state[pl.ds(first + 8, CHUNK), :] = (
            jnp.sqrt(neg_expm1(2.0 * loga)) * opened * r.conv[rows, :]
        )
        return 0

    lax.fori_loop(0, SPAN // CHUNK, gates_chunk, 0)
    loc.store(r.rate, r.out_rate)
    loc.store(r.opened, r.out_opened)
    row = lax.broadcasted_iota(jnp.int32, (8, CH), 0)

    def step(i, carry):
        held, prod = carry
        rows = rows_at(i * 8, 8)
        srows = rows_at(i * 8 + 8, 8)
        a = r.fac[rows, :]
        h = r.state[srows, :]
        for s in (1, 2, 4):
            h = h + a * jnp.where(row >= s, pltpu.roll(h, s, 0), 0.0)
            a = a * jnp.where(row >= s, pltpu.roll(a, s, 0), 1.0)
        h = h + a * held
        a = a * prod
        r.state[srows, :] = h
        r.acum[rows, :] = a
        return h[7:8, :], a[7:8, :]

    zero = jnp.zeros((1, CH), F32)
    last_h, last_a = lax.fori_loop(0, SPAN // 8, step, (zero, zero + 1.0), unroll=4)
    edges_in = share_edges(net, r.edges, last_a, last_h)
    pass_on(2)
    first_w.start()
    arrived(2)
    loc.store(r.wr, r.out_wr)
    r.gate[...] = dot_nt(rows_n, r.wr[1])
    loc.store(r.gate, r.out_gate)
    for copy in edges_in:
        copy.wait_recv()
    held = zero
    for b in range(3):
        held = jnp.where(b < y, r.edges[b, 0:1, :] * held + r.edges[b, 1:2, :], held)
    r.state[0:8, :] = jnp.broadcast_to(held, (8, CH))

    def gated_chunk(i, _):
        first = pl.multiple_of(i * CHUNK, CHUNK)
        rows = pl.ds(first, CHUNK)
        srows = pl.ds(first + 8, CHUNK)
        state = r.state[srows, :] + r.acum[rows, :] * held
        r.state[srows, :] = state
        r.gated[i // 2, rows_at(i % 2 * CHUNK, CHUNK), :] = (
            gelu(r.gate[rows, :]) * state
        ).astype(BF16)
        return 0

    lax.fori_loop(0, SPAN // CHUNK, gated_chunk, 0)
    loc.store(r.state, r.out_state)
    loc.store(r.gated, r.out_gated)
    back = {}
    for ds in HALVES:
        term = dot_nn(stack(r.gated, [(z + 4 - d) % 4 for d in ds]), r.wr[2])
        for i, d in enumerate(ds):
            if d:
                r.part1[d - 1] = block(term, i).astype(BF16)
                back[d] = net.push(r.part1.at[d - 1], r.recv1.at[d - 1], z_peer(4 - d))
            else:
                r.x1[...] = tokens + block(term, i)
    first_w.along()
    for copy in attn_z:
        copy.wait_recv()
    attn_w.start()
    total = r.x1[...]
    for d in (1, 3, 2):
        back[d].wait_recv()
        total = total + r.recv1[d - 1].astype(F32)
    r.x1[...] = total

    r.n2[z] = rms(total, r.gain_two[...]).astype(BF16)
    gather_n2 = spread_z(net, r.n2)
    loc.store(r.x1, r.out_x1)
    first_w.across()
    attn_w.along()
    first_w.finish()
    for copy in place_units(loc, r.all_first, r.w1):
        copy.wait()
    loc.store(r.w1, r.out_w1)
    back = {}
    for ds in HALVES:
        slots = [(z + 4 - d) % 4 for d in ds]
        for d in ds:
            if d:
                gather_n2[d].wait_recv()
        nb = stack(r.n2, slots)
        pg = dot_nt(nb, r.w1[0])
        pu = dot_nt(nb, r.w1[1])
        term = dot_nn((gelu(pg) * pu).astype(BF16), r.w1[2])
        for i, (d, s) in enumerate(zip(ds, slots)):
            r.pg[s] = block(pg, i)
            r.pu[s] = block(pu, i)
            if d:
                r.part2[d - 1] = block(term, i).astype(BF16)
                back[d] = net.push(r.part2.at[d - 1], r.recv2.at[d - 1], z_peer(4 - d))
            else:
                r.x2[...] = total + block(term, i)
        if ds == HALVES[0]:
            attn_w.across()
            second_w.start()
    loc.store(r.n2, r.out_n2)
    loc.store(r.pg, r.out_pg)
    loc.store(r.pu, r.out_pu)
    second_w.along()
    attn_w.finish()

    def split(i, _):
        a, b, e = i // 16, (i // 4) % 4, i % 4
        block = r.all_attn[a, b, e].astype(F32).reshape(4, 16, PAIR)
        rows = rows_at((b * 2 + a) * 128 + e * 32, 32)
        r.wa[0, rows, :] = block[:, 0:8, :].reshape(32, PAIR).astype(BF16)
        r.wa[1, rows, :] = block[:, 8:16, :].reshape(32, PAIR).astype(BF16)
        return 0

    lax.fori_loop(0, 32, split, 0)
    loc.store(r.wa, r.out_wa)
    total = r.x2[...]
    for d in (1, 3, 2):
        back[d].wait_recv()
        total = total + r.recv2[d - 1].astype(F32)
    r.x2[...] = total
    loc.store(r.x2, r.out_x2)

    n = rms(total, r.gain_three[...]).astype(BF16)
    r.n3[...] = n
    cosine = r.cosine[...]
    sine = r.sine[...]
    swap = lambda v: pltpu.roll(v, HD // 2, 1)
    key = dot_nn(n, r.wa[0, :, D:])
    r.kv[8, :, :HD] = (key * cosine + swap(key) * sine).astype(BF16)
    r.kv[8, :, HD:] = dot_nn(n, r.wa[1, :, :HD]).astype(BF16)
    copies = []
    for o in range(1, 9):
        copy = net.make(r.kv.at[8], r.kv.at[8 - o], row_peer(o))
        copies.append(copy)

        @pl.when(mp + o < 16)
        def _():
            copy.start()

        @pl.when(mp < o)
        def _():
            r.kv[8 - o] = jnp.zeros((ROWS, 2 * HD), BF16)

    loc.store(r.n3, r.out_n3)
    queries = dot_nn(n, r.wa[0, :, :D])
    for h in range(HEADS):
        query = queries[:, h * HD : (h + 1) * HD]
        r.q[h] = ((query * cosine + swap(query) * sine) * (1.0 / math.sqrt(HD))).astype(BF16)
    loc.store(r.q, r.out_q)
    row = lax.broadcasted_iota(jnp.int32, (ROWS, KEYS), 0)
    col = lax.broadcasted_iota(jnp.int32, (ROWS, KEYS), 1) - (KEYS - ROWS)
    base = mp * ROWS
    length = jnp.concatenate([r.length[...]] * 9, axis=1)
    allowed = (col + base >= 0) & (row >= col) & (row - col < WINDOW)
    allowed = allowed & ((row + base >= length) == (col + base >= length))
    r.bias[...] = jnp.where(allowed, 0.0, -1e30)
    second_w.across()
    for o in range(1, 9):

        @pl.when(mp >= o)
        def _():
            copies[o - 1].wait_recv()

    loc.store(r.kv, r.out_kv)
    pairs = r.kv[...].reshape(KEYS, 2 * HD)
    r.keys[...] = pairs[:, :HD]
    r.values[...] = pairs[:, HD:]
    r.score[...] = dot_nt(r.q[...].reshape(HEADS * ROWS, HD), r.keys[...])

    def softmax(i, _):
        rows, own = rows_at(i % 2 * 64, 64), rows_at(i * 64, 64)
        s = r.score[own, :] + r.bias[rows, :]
        e = jnp.exp(s - jnp.max(s, axis=-1, keepdims=True))
        p = e * (1.0 / jnp.sum(e, axis=-1, keepdims=True))
        r.pb[own, :] = p.astype(BF16)
        return 0

    lax.fori_loop(0, HEADS * 2, softmax, 0)
    mixed = dot_nn(r.pb[...], r.values[...])
    for h in range(HEADS):
        r.att[:, h * HD : (h + 1) * HD] = block(mixed, h).astype(BF16)
    loc.store(r.pb, r.out_pb)
    loc.store(r.att, r.out_att)
    total = total + dot_nn(r.att[...], r.wa[1, :, HD:])
    r.x3[...] = total
    r.n4[z] = rms(total, r.gain_four[...]).astype(BF16)
    gather_n4 = spread_z(net, r.n4)
    loc.store(r.x3, r.out_x3)
    for d in (1, 3, 2):
        gather_c[d].wait_recv()
    loc.store(r.c_all, r.out_c_all)
    second_w.finish()
    loc.stores += place_units(loc, r.all_second, r.out_w2)
    for d in (1, 3, 2):
        gather_n4[d].wait_recv()
    loc.store(r.n4, r.out_n4)
    loc.drain()
    net.drain()
    for o in range(1, 9):

        @pl.when(mp + o < 16)
        def _():
            copies[o - 1].wait_send()

    @pl.when((z == 3) & (y < 3))
    def _():
        for halo in halos:
            halo.wait_send()


BIG = ((SPAN, CH), F32)
TALL = ((SPAN + 8, CH), F32)
SAVED = {
    "n1": ((4, ROWS, D), BF16),
    "wr": ((3, CH, D), BF16),
    "pr": ((4, PAR, LANE), F32),
    "mix": TALL,
    "gate": BIG,
    "conv": BIG,
    "rate": BIG,
    "opened": BIG,
    "state": TALL,
    "gated": ((4, ROWS, CH), BF16),
    "x1": ((ROWS, D), F32),
    "w1": ((3, UNITS, D), BF16),
    "n2": ((4, ROWS, D), BF16),
    "pg": ((4, ROWS, UNITS), F32),
    "pu": ((4, ROWS, UNITS), F32),
    "x2": ((ROWS, D), F32),
    "wa": ((2, D, PAIR), BF16),
    "n3": ((ROWS, D), BF16),
    "q": ((HEADS, ROWS, HD), BF16),
    "kv": ((9, ROWS, 2 * HD), BF16),
    "pb": ((HEADS * ROWS, KEYS), BF16),
    "att": ((ROWS, D), BF16),
    "x3": ((ROWS, D), F32),
    "n4": ((4, ROWS, D), BF16),
    "c_all": ((4, ROWS, D), BF16),
}
BLOCKS = ((2, 4, 4, 576, LANE), BF16)


def forward(inputs):
    outs = [("out_" + k, *v, "far") for k, v in SAVED.items()]
    outs += [("out_w2", (3, UNITS, D), BF16, "far")]
    scratch = [(k, vm(*v)) for k, v in SAVED.items()]
    scratch += [
        ("fac", vm(*BIG)),
        ("acum", vm(*BIG)),
        ("edges", vm((4, 8, CH), F32)),
        ("part1", vm((3, ROWS, D), BF16)),
        ("recv1", vm((3, ROWS, D), BF16)),
        ("part2", vm((3, ROWS, D), BF16)),
        ("recv2", vm((3, ROWS, D), BF16)),
        ("own_first", vm((576, LANE), BF16)),
        ("own_second", vm((576, LANE), BF16)),
        ("own_attn", vm((64, PAIR), BF16)),
        ("all_first", vm(*BLOCKS)),
        ("all_second", vm(*BLOCKS)),
        ("all_attn", vm((2, 4, 4, 64, PAIR), BF16)),
        ("halo", vm((16, D), BF16)),
        ("bias", vm((ROWS, KEYS), F32)),
        ("score", vm((HEADS * ROWS, KEYS), F32)),
        ("keys", vm((KEYS, HD), BF16)),
        ("values", vm((KEYS, HD), BF16)),
        ("send", dma(100)),
        ("recv", dma(100)),
        ("sems", dma(230)),
    ]
    return run(
        forward_body, [(k, v, "near") for k, v in inputs.items()], outs, scratch, 1, 10**10
    )


def middle_body(r):
    _, _, _, z = place()
    mp = lax.axis_index("mp")
    ready = greet(all_peers())
    net, loc = Net(r.send, r.recv), Local(r.sems)
    loads = {
        k: loc.load(getattr(r, "far_" + k), getattr(r, k))
        for k in ("w2", "n4", "c_all", "wa", "kv", "pb", "q", "att", "n3", "x2")
    }
    x = r.x3[...]
    c = r.cot[...].astype(F32)
    for k in ("w2", "n4", "c_all"):
        loads[k].wait()
    back_d, back_o = {}, {}
    for ds in HALVES:
        slots = [(z + 4 - d) % 4 for d in ds]
        nb = stack(r.n4, slots)
        pg = dot_nt(nb, r.w2[0])
        pu = dot_nt(nb, r.w2[1])
        act, slope = gelu_both(pg)
        hid = (act * pu).astype(BF16)
        dh = dot_nt(stack(r.c_all, slots), r.w2[2])
        dpg = (dh * pu * slope).astype(BF16)
        dpu = (dh * act).astype(BF16)
        term = dot_nn(dpg, r.w2[0]) + dot_nn(dpu, r.w2[1])
        if ds == HALVES[0]:
            ready()
        for i, (d, s) in enumerate(zip(ds, slots)):
            r.hid[s] = block(hid, i)
            r.dpg[s] = block(dpg, i)
            r.dpu[s] = block(dpu, i)
            if d == 0:
                r.own_d[...] = block(term, i)
            else:
                r.part_d[d - 1] = block(term, i).astype(BF16)
                back_d[d] = net.push(r.part_d.at[d - 1], r.recv_d.at[d - 1], z_peer(4 - d))
    unit_grads(((r.dpg, r.n4), (r.dpu, r.n4), (r.hid, r.c_all)), r.gw2)
    reducer = Reducer(net, r.gw2, r, "red")
    reducer.start()

    for ds in HALVES:
        slots = [(z + 4 - d) % 4 for d in ds]
        term = dot_nn(stack(r.hid, slots), r.w2[2])
        for i, d in enumerate(ds):
            if d == 0:
                r.outputs[...] = x + block(term, i)
            else:
                r.part_o[d - 1] = block(term, i).astype(BF16)
                back_o[d] = net.push(r.part_o.at[d - 1], r.recv_o.at[d - 1], z_peer(4 - d))

    dn = r.own_d[...]
    for d in (1, 3, 2):
        back_d[d].wait_recv()
        dn = dn + r.recv_d[d - 1].astype(F32)
    dv, r.gg_four[...] = rms_back(dn, x, r.gain_four[...])
    c = c + dv

    for k in ("wa", "kv", "pb", "q", "att", "n3", "x2"):
        loads[k].wait()
    cb = c.astype(BF16)
    datt = dot_nt(cb, r.wa[1, :, HD:]).astype(BF16)
    for h in range(HEADS):
        r.datt[h] = datt[:, h * HD : (h + 1) * HD]
    cosine = r.cosine[...]
    sine = r.sine[...]
    swap = lambda v: pltpu.roll(v, HD // 2, 1)
    pairs = r.kv[...].reshape(KEYS, 2 * HD)
    r.keys[...] = pairs[:, :HD]
    r.values[...] = pairs[:, HD:]
    datts = r.datt[...].reshape(HEADS * ROWS, HD)
    r.score[...] = dot_nt(datts, r.values[...])

    def scores(i, _):
        own = rows_at(i * 64, 64)
        dp = r.score[own, :]
        p = r.pb[own, :].astype(F32)
        ds = p * (dp - jnp.sum(p * dp, axis=-1, keepdims=True))
        r.ds[own, :] = ds.astype(BF16)
        return 0

    lax.fori_loop(0, HEADS * 2, scores, 0)
    dqs = dot_nn(r.ds[...], r.keys[...])
    for h in range(HEADS):
        dq = block(dqs, h) * (1.0 / math.sqrt(HD))
        r.dqkv[:, h * HD : (h + 1) * HD] = (dq * cosine - swap(dq) * sine).astype(BF16)
    r.turned[0] = dot_tn(r.q[...].reshape(HEADS * ROWS, HD), r.ds[...])
    r.turned[1] = dot_tn(datts, r.pb[...])
    copies = {}
    for o in (1, 2, 3, 4, 5, 6, 7, 8):
        keys = slice((8 - o) * ROWS, (9 - o) * ROWS)
        r.part_kv[o - 1, :, :HD] = r.turned[0, :, keys].T.astype(BF16)
        r.part_kv[o - 1, :, HD:] = r.turned[1, :, keys].T.astype(BF16)
        copy = net.make(r.part_kv.at[o - 1], r.recv_kv.at[o - 1], row_peer(-o))
        copies[o] = copy

        @pl.when(mp >= o)
        def _():
            copy.start()

        @pl.when(mp + o >= 16)
        def _():
            r.recv_kv[o - 1] = jnp.zeros((ROWS, 2 * HD), BF16)

    dn = dot_nt(r.dqkv[...], r.wa[0, :, :D])
    own_k = r.turned[0, :, KEYS - ROWS :].T
    own_v = r.turned[1, :, KEYS - ROWS :].T
    reducer.along_one()
    for o in range(1, 9):

        @pl.when(mp + o < 16)
        def _():
            copies[o].wait_recv()

        own_k = own_k + r.recv_kv[o - 1, :, :HD].astype(F32)
        own_v = own_v + r.recv_kv[o - 1, :, HD:].astype(F32)
    dk = (own_k * cosine - swap(own_k) * sine).astype(BF16)
    dv = own_v.astype(BF16)
    dn = dn + dot_nt(dk, r.wa[0, :, D:]) + dot_nt(dv, r.wa[1, :, :HD])
    back, r.gg_three[...] = rms_back(dn, r.x2[...], r.gain_three[...])
    c = c + back
    r.c2[...] = c
    r.c2_all[z] = c.astype(BF16)
    gather_c = spread_z(net, r.c2_all)
    n = r.n3[...].T
    att = r.att[...].T

    for t in range(4):
        cols = slice(t * 256, (t + 1) * 256)
        r.right[:, HD + t * 256 : HD + (t + 1) * 256] = dot_nn(att, cb[:, cols])
        r.score[:, cols] = dot_nn(n, r.dqkv[:, cols])
    r.score[:, D:] = dot_nn(n, dk)
    r.right[:, :HD] = dot_nn(n, dv)
    reducer.along_two()

    def lower(i, _):
        a, e, b = i // 8, i // 4 % 2, i % 4
        rows = rows_at(i * 32, 32)
        left = r.score[rows, :].reshape(4, 8, PAIR)
        right = r.right[rows, :].reshape(4, 8, PAIR)
        both = jnp.concatenate([left, right], axis=1)
        r.gw_attn[e, a, b] = both.reshape(64, PAIR).astype(BF16)
        return 0

    lax.fori_loop(0, 32, lower, 0)
    loc.store(r.gw_attn, r.out_gw_attn)
    total = r.outputs[...]
    for d in (1, 3, 2):
        back_o[d].wait_recv()
        total = total + r.recv_o[d - 1].astype(F32)
    r.outputs[...] = total
    for d in (1, 3, 2):
        gather_c[d].wait_recv()
    loc.store(r.c2_all, r.out_c2_all)
    a, b = reducer.finish()
    r.second_out[0:288, :] = a
    r.second_out[288:, :] = b
    loc.drain()
    net.drain()
    for o in range(1, 9):

        @pl.when(mp >= o)
        def _():
            copies[o].wait_send()


def middle(near, far):
    ins = [(k, v, "near") for k, v in near.items()]
    ins += [("far_" + k, v, "far") for k, v in far.items()]
    outs = [
        ("outputs", (ROWS, D), F32, "near"),
        ("c2", (ROWS, D), F32, "near"),
        ("gg_four", (1, D), F32, "near"),
        ("gg_three", (1, D), F32, "near"),
        ("second_out", (576, LANE), F32, "near"),
        ("out_gw_attn", (2, 4, 4, 64, PAIR), BF16, "far"),
        ("out_c2_all", (4, ROWS, D), BF16, "far"),
    ]
    units = ((4, ROWS, UNITS), BF16)
    third = ((3, ROWS, D), BF16)
    scratch = [(k, vm(*SAVED[k])) for k in far if k in SAVED]
    scratch += [
        ("w2", vm((3, UNITS, D), BF16)),
        ("c2_all", vm((4, ROWS, D), BF16)),
        ("score", vm((HEADS * ROWS, KEYS), F32)),
        ("keys", vm((KEYS, HD), BF16)),
        ("values", vm((KEYS, HD), BF16)),
        ("turned", vm((2, HD, KEYS), F32)),
        ("hid", vm(*units)),
        ("dpg", vm(*units)),
        ("dpu", vm(*units)),
        ("own_d", vm((ROWS, D), F32)),
        ("part_d", vm(*third)),
        ("recv_d", vm(*third)),
        ("part_o", vm(*third)),
        ("recv_o", vm(*third)),
        ("gw2", vm(*BLOCKS)),
        ("datt", vm((HEADS, ROWS, HD), BF16)),
        ("ds", vm((HEADS * ROWS, KEYS), BF16)),
        ("part_kv", vm((8, ROWS, 2 * HD), BF16)),
        ("recv_kv", vm((8, ROWS, 2 * HD), BF16)),
        ("dqkv", vm((ROWS, D), BF16)),
        ("right", vm((D, PAIR), F32)),
        ("gw_attn", vm((2, 4, 4, 64, PAIR), BF16)),
        *Reducer.scratch("red", 576, LANE),
        ("send", dma(40)),
        ("recv", dma(40)),
        ("sems", dma(16)),
    ]
    return run(middle_body, ins, outs, scratch, 2, 10**10)


def last_body(r):
    x, c, y, z = place()
    dp = lax.axis_index("dp")
    ready = greet([xc_peer(*o) for o in OTHERS] + [row_peer(o) for o in range(1, 16)])
    net, loc = Net(r.send, r.recv), Local(r.sems)
    loads = {
        k: loc.load(getattr(r, "far_" + k), getattr(r, k))
        for k in ("c2_all", "w1", "pg", "pu", "gw_attn", "n2", "wr", "gate", "state", "rate", "pr", "opened", "conv",
                  "mix", "n1", "gated")
    }
    need = lambda *names: [loads[k].wait() for k in names]
    upstream = r.c2[...]
    need("w1", "pg", "pu", "c2_all")
    red_attn = Reducer(net, r.gw_attn, r, "rat")
    back = {}
    for ds in HALVES:
        slots = [(z + 4 - d) % 4 for d in ds]
        pg = stack(r.pg, slots)
        pu = stack(r.pu, slots)
        act, slope = gelu_both(pg)
        hid = (act * pu).astype(BF16)
        dh = dot_nt(stack(r.c2_all, slots), r.w1[2])
        dpg = (dh * pu * slope).astype(BF16)
        dpu = (dh * act).astype(BF16)
        term = dot_nn(dpg, r.w1[0]) + dot_nn(dpu, r.w1[1])
        if ds == HALVES[0]:
            ready()
        for i, (d, s) in enumerate(zip(ds, slots)):
            r.hid[s] = block(hid, i)
            r.dpg[s] = block(dpg, i)
            r.dpu[s] = block(dpu, i)
            if d == 0:
                r.grad_tokens[...] = block(term, i)
            else:
                r.part1[d - 1] = block(term, i).astype(BF16)
                back[d] = net.push(r.part1.at[d - 1], r.recv1.at[d - 1], z_peer(4 - d))
        if ds == HALVES[0]:
            need("gw_attn")
            red_attn.start()
    red_attn.along_one()
    need("n2")
    unit_grads(((r.dpg, r.n2), (r.dpu, r.n2), (r.hid, r.c2_all)), r.gw1)
    red_first = Reducer(net, r.gw1, r, "rff")
    red_first.start()
    red_attn.along_two()
    dn = r.grad_tokens[...]
    for d in (1, 3, 2):
        back[d].wait_recv()
        dn = dn + r.recv1[d - 1].astype(F32)
    dv, gg_two = rms_back(dn, r.x1[...], r.gain_two[...])
    upstream = upstream + dv
    r.c1[...] = upstream

    r.c1_all[z] = upstream.astype(BF16)
    gather_c = spread_z(net, r.c1_all)
    a, b = red_attn.finish()
    r.z_out[0:2] = a.astype(BF16).reshape(2, 16, PAIR)
    r.z_out[2:4] = b.astype(BF16).reshape(2, 16, PAIR)
    z_in = [
        net.push(r.z_out.at[(z + d) % 4], r.z_in.at[d - 1], z_peer(d)) for d in (1, 3, 2)
    ]
    need("wr")
    for ds in STEPS:
        slots = [(z + 4 - d) % 4 for d in ds]
        for d in ds:
            if d:
                gather_c[d].wait_recv()
        term = dot_nt(stack(r.c1_all, slots), r.wr[2])
        for i, (d, s) in enumerate(zip(ds, slots)):
            r.du[rows_at(s * ROWS, ROWS), :] = block(term, i)
            if d == 0:
                red_first.along_one()
    need("gate", "state", "rate", "pr")

    def decay_of(rows, first):
        pos = positions(r.length, y * SPAN + first, CHUNK)
        loga = -8.0 * r.rate[rows, :] * lanes_of(r.pr, VEC + 7)
        return loga, jnp.exp(loga), pos

    def first_chunk(i, _):
        first = pl.multiple_of(i * CHUNK, CHUNK)
        rows = pl.ds(first, CHUNK)
        act, slope = gelu_both(r.gate[rows, :])
        dgated = r.du[rows, :]
        dgate = dgated * r.state[pl.ds(first + 8, CHUNK), :] * slope
        r.hid[i // 2, rows_at(i % 2 * CHUNK, CHUNK), 0:CH] = dgate.astype(BF16)
        r.du[rows, :] = dgated * act
        _, decay, pos = decay_of(rows, first)
        r.fac[rows, :] = jnp.where(pos > 0, decay, 0.0)
        return 0

    lax.fori_loop(0, SPAN // CHUNK, first_chunk, 0)
    row = lax.broadcasted_iota(jnp.int32, (8, CH), 0)

    def step(i, carry):
        held, prod = carry
        rows = rows_at((SPAN // 8 - 1 - i) * 8, 8)
        m = r.fac[rows, :]
        u = r.du[rows, :]
        e = m * u
        for s in (1, 2, 4):
            inside = row < 8 - s
            e = e + m * jnp.where(inside, pltpu.roll(e, 8 - s, 0), 0.0)
            m = m * jnp.where(inside, pltpu.roll(m, 8 - s, 0), 1.0)
        e = e + m * held
        m = m * prod
        r.du[rows, :] = u + jnp.where(row < 7, pltpu.roll(e, 7, 0), held)
        r.acum[rows, :] = jnp.where(row < 7, pltpu.roll(m, 7, 0), prod)
        return e[0:1, :], m[0:1, :]

    zero = jnp.zeros((1, CH), F32)
    first_e, first_m = lax.fori_loop(0, SPAN // 8, step, (zero, zero + 1.0), unroll=4)
    edges_in = share_edges(net, r.edges, first_m, first_e)
    need("opened", "conv", "mix", "n1", "gated")

    def output_grads(out, w, left, right):
        for half in range(2):
            cut = left[:, :, half * 256 : half * 256 + 256].reshape(SPAN, 256)
            grad = dot_tn(cut, right[...].reshape(SPAN, D))
            for j in range(2):
                for part in range(8):
                    out[part % 2, part // 2, half * 2 + j, w * BW : (w + 1) * BW, :] = grad[
                        j * LANE : j * LANE + BW, part * LANE : (part + 1) * LANE
                    ].astype(BF16)

    output_grads(r.gwa, 0, r.hid, r.n1)
    output_grads(r.gwa, 1, r.gated, r.c1_all)
    red_a = Reducer(net, r.gwa, r, "rea")
    red_a.start()
    for copy in edges_in:
        copy.wait_recv()
    held = zero
    for b in (3, 2, 1):
        held = jnp.where(b > y, r.edges[b, 0:1, :] * held + r.edges[b, 1:2, :], held)

    def second_chunk(i, dsp):
        first = pl.multiple_of(i * CHUNK, CHUNK)
        rows = pl.ds(first, CHUNK)
        ds = r.du[rows, :] + r.acum[rows, :] * held
        loga, decay, pos = decay_of(rows, first)
        rate = r.rate[rows, :]
        opened = r.opened[rows, :]
        conv = r.conv[rows, :]
        before = r.state[pl.ds(first, CHUNK + 8), :][7 : 7 + CHUNK, :]
        beta = jnp.sqrt(neg_expm1(2.0 * loga))
        dloga = jnp.where(pos > 0, ds * before * decay, 0.0)
        dloga = dloga - ds * opened * conv * (decay * decay) / beta
        dopened = ds * beta * conv
        r.du[rows, :] = ds * beta * opened
        r.acum[rows, :] = dloga * (-8.0 * lanes_of(r.pr, VEC + 7)) * rate * (1.0 - rate)
        r.fac[rows, :] = dopened * opened * (1.0 - opened)
        return dsp + jnp.sum(dloga * (-8.0 * rate), axis=0, keepdims=True)

    dsp = lax.fori_loop(0, SPAN // CHUNK, second_chunk, zero)
    for b in range(4):
        cols = slice(b * LANE, (b + 1) * LANE)
        r.du[0:SPAN, cols] = (
            r.du[0:SPAN, cols]
            + jnp.pad(
                low_dot(r.acum[:, cols], r.pr[b, 0:BW, :], ((1,), (1,)))
                + low_dot(r.fac[:, cols], r.pr[b, BW : 2 * BW, :], ((1,), (1,))),
                ((0, 0), (0, LANE - BW)),
            )
        )
    halo = net.make(r.du.at[0:8], r.du.at[SPAN : SPAN + 8], y_peer(3))

    @pl.when(y > 0)
    def _():
        halo.start()

    @pl.when(y == 3)
    def _():
        r.du[SPAN : SPAN + 8, :] = jnp.zeros((8, CH), F32)

    red_first.along_two()

    @pl.when(y < 3)
    def _():
        halo.wait_recv()

    def third_chunk(i, sums):
        first = pl.multiple_of(i * CHUNK, CHUNK)
        rows = pl.ds(first, CHUNK)
        pos = positions(r.length, y * SPAN + first, CHUNK + 8)
        dwin = r.du[pl.ds(first, CHUNK + 8), :]
        mwin = r.mix[pl.ds(first, CHUNK + 8), :]
        dconv = dwin[:CHUNK, :]
        total = lanes_of(r.pr, VEC) * dconv
        taps = [jnp.sum(dconv * mwin[8:, :], axis=0, keepdims=True)]
        for k in (1, 2, 3):
            masked = jnp.where(pos >= k, dwin, 0.0)
            total = total + lanes_of(r.pr, VEC + k) * masked[k : k + CHUNK, :]
            taps.append(
                jnp.sum(masked[:CHUNK, :] * mwin[8 - k : 8 - k + CHUNK, :], axis=0, keepdims=True)
            )
        r.dpg[i // 2, rows_at(i % 2 * CHUNK, CHUNK), 0:CH] = total.astype(BF16)
        taps.append(jnp.sum(dconv, axis=0, keepdims=True))
        taps.append(jnp.sum(r.acum[rows, :], axis=0, keepdims=True))
        taps.append(jnp.sum(r.fac[rows, :], axis=0, keepdims=True))
        return tuple(a + b for a, b in zip(sums, taps))

    sums = lax.fori_loop(0, SPAN // CHUNK, third_chunk, (zero,) * 7)
    back = {}
    for ds in HALVES:
        slots = [(z + 4 - d) % 4 for d in ds]
        mixes = stack(r.dpg, slots)[:, 0:CH]
        gates = stack(r.hid, slots)[:, 0:CH]
        term = dot_nn(mixes, r.wr[0]) + dot_nn(gates, r.wr[1])
        for i, d in enumerate(ds):
            if d:
                r.part2[d - 1] = block(term, i).astype(BF16)
                back[d] = net.push(r.part2.at[d - 1], r.recv2.at[d - 1], z_peer(4 - d))
            else:
                r.grad_tokens[...] = block(term, i)
    red_a.along_one()
    output_grads(r.gwb, 0, r.dpg, r.n1)
    for b in range(4):
        cols = slice(b * LANE, (b + 1) * LANE)
        left = r.conv[:, b * LANE : b * LANE + BW]
        r.gp[b, 0:BW, :] = low_dot(left, r.acum[:, cols], ((0,), (0,)))
        r.gp[b, BW : 2 * BW, :] = low_dot(left, r.fac[:, cols], ((0,), (0,)))
    for b in range(4):
        cols = slice(b * LANE, (b + 1) * LANE)
        for k, row_sum in enumerate(sums + (dsp,)):
            r.gp[b, VEC + k : VEC + k + 1, :] = row_sum[:, cols]
        r.gp[b, 200:, :] = jnp.zeros((56, LANE), F32)
        for part in range(8):
            r.gwb[part % 2, part // 2, b, BW:, :] = r.gp[
                b, part * 32 : part * 32 + 32, :
            ].astype(BF16)
    red_b = Reducer(net, r.gwb, r, "reb")
    red_b.start()
    red_a.along_two()

    def spread(stage, first, peers):
        r.gain_out[stage] = r.gains[...]
        return [
            net.push(r.gain_out.at[stage], r.gain_in.at[first + i], peer)
            for i, peer in enumerate(peers)
        ]

    def collect(first, mine):
        total = r.gains[...]
        for i, copy in enumerate(mine):
            copy.wait_recv()
            total = total + r.gain_in[first + i]
        r.gains[...] = total

    def share(reducer, whole):
        a, b = reducer.finish()
        half = reducer.half
        whole[dp, 0:half, :] = a.astype(BF16)
        whole[dp, half:, :] = b.astype(BF16)
        cut = whole.at[dp]
        return [
            net.push(cut, cut, xc_peer(dx, dc))
            for dx, dc in OTHERS
        ]

    red_b.along_one()
    dn = r.grad_tokens[...]
    for d in (1, 3, 2):
        back[d].wait_recv()
        dn = dn + r.recv2[d - 1].astype(F32)
    dv, gg_one = rms_back(dn, r.tok[...].astype(F32), r.gain_one[...])
    r.grad_tokens[...] = r.c1[...] + dv
    for k, grad in enumerate((gg_one, gg_two, r.gg_three[...], r.gg_four[...])):
        for j in range(8):
            r.gains[k * 8 + j : k * 8 + j + 1, :] = grad[:, j * LANE : (j + 1) * LANE]
    mine = spread(0, 0, [xc_peer(dx, dc) for dx, dc in OTHERS])
    shares = share(red_a, r.recur_a)
    red_b.along_two()
    a, b = red_first.finish()
    r.first_out[0:288, :] = a
    r.first_out[288:, :] = b
    collect(0, mine)
    mine = spread(1, 7, [row_peer(o) for o in range(1, 16)])
    shares += share(red_b, r.recur_b)
    total = r.z_out[z].astype(F32)
    for copy in z_in:
        copy.wait_recv()
    for d in range(3):
        total = total + r.z_in[d].astype(F32)
    r.attn_out[...] = total
    collect(7, mine)
    for copy in shares:
        copy.wait_recv()
    net.drain()

    @pl.when(y > 0)
    def _():
        halo.wait_send()


def last(near, far):
    ins = [(k, v, "near") for k, v in near.items()]
    ins += [("far_" + k, v, "far") for k, v in far.items()]
    outs = [
        ("grad_tokens", (ROWS, D), F32, "near"),
        ("gains", (32, LANE), F32, "near"),
        ("first_out", (576, LANE), F32, "near"),
        ("attn_out", (16, PAIR), F32, "near"),
        ("recur_a", (8, 192, LANE), BF16, "near"),
        ("recur_b", (8, 128, LANE), BF16, "near"),
    ]
    units = ((4, ROWS, UNITS), BF16)
    third = ((3, ROWS, D), BF16)
    whole = ((4, ROWS, D), BF16)
    scratch = [(k, vm(*SAVED[k])) for k in far if k in SAVED]
    scratch += [
        ("gw_attn", vm((2, 4, 4, 64, PAIR), BF16)),
        ("c2_all", vm(*whole)),
        ("c1_all", vm(*whole)),
        ("c1", vm((ROWS, D), F32)),
        ("hid", vm(*units)),
        ("dpg", vm(*units)),
        ("dpu", vm(*units)),
        ("part1", vm(*third)),
        ("recv1", vm(*third)),
        ("part2", vm(*third)),
        ("recv2", vm(*third)),
        ("gw1", vm(*BLOCKS)),
        ("z_out", vm((4, 16, PAIR), BF16)),
        ("z_in", vm((3, 16, PAIR), BF16)),
        ("du", vm(*TALL)),
        ("fac", vm(*BIG)),
        ("acum", vm(*BIG)),
        ("edges", vm((4, 8, CH), F32)),
        ("gp", vm((4, 256, LANE), F32)),
        ("gwa", vm((2, 4, 4, 192, LANE), BF16)),
        ("gwb", vm((2, 4, 4, 128, LANE), BF16)),
        ("gain_in", vm((22, 32, LANE), F32)),
        ("gain_out", vm((2, 32, LANE), F32)),
        *Reducer.scratch("rat", 64, PAIR),
        *Reducer.scratch("rff", 576, LANE),
        *Reducer.scratch("rea", 192, LANE),
        *Reducer.scratch("reb", 128, LANE),
        ("send", dma(112)),
        ("recv", dma(112)),
        ("sems", dma(17)),
    ]
    return run(last_body, ins, outs, scratch, 3, 10**10)


def output_body(r):
    r.outputs[...] = r.in_outputs[...]
    r.tokens[...] = r.in_tokens[...]
    for i, name in enumerate(("norm_one", "norm_two", "norm_three", "norm_four")):
        for j in range(8):
            getattr(r, name)[:, j * LANE : (j + 1) * LANE] = r.gains[i * 8 + j : i * 8 + j + 1, :]
    for part in range(8):
        rows = slice(part * LANE, (part + 1) * LANE)
        r.recur_gate[:, rows] = r.recur_a[part, 0:BW, :].astype(F32)
        r.recur_output[:, rows] = r.recur_a[part, BW:, :].astype(F32)
        r.recur_input[:, rows] = r.recur_b[part, 0:BW, :].astype(F32)
    params = r.recur_b[:, BW:, :].astype(F32).reshape(256, LANE)
    r.decay_gate[0] = params[0:BW, :BW]
    r.input_gate[0] = params[BW : 2 * BW, :BW]
    r.conv_kernel[...] = params[VEC : VEC + 4, :BW]
    r.conv_bias[...] = params[VEC + 4 : VEC + 5, :BW]
    r.decay_shift[...] = params[VEC + 5 : VEC + 6, :BW]
    r.input_shift[...] = params[VEC + 6 : VEC + 7, :BW]
    slope = -jax.nn.sigmoid(-r.decay[...])
    r.decay_param[...] = params[VEC + 7 : VEC + 8, :BW] * slope
    for name in ("first", "second"):
        summed = getattr(r, name)
        getattr(r, name + "_gate")[...] = summed[0:192, :]
        getattr(r, name + "_value")[...] = summed[192:384, :]
        getattr(r, name + "_down")[...] = summed[384:, :]
    r.query_proj[...] = r.attn[0:8, :D]
    r.key_proj[...] = r.attn[0:8, D:]
    r.value_proj[...] = r.attn[8:16, :HD]
    r.attn_output[...] = r.attn[8:16, HD:]


OUTPUTS = (
    ("outputs", (ROWS, D)), ("tokens", (ROWS, D)), ("norm_one", (1, D)),
    ("recur_input", (BW, D)), ("recur_gate", (BW, D)), ("conv_kernel", (4, BW)),
    ("conv_bias", (1, BW)), ("decay_gate", (1, BW, BW)), ("decay_shift", (1, BW)),
    ("input_gate", (1, BW, BW)), ("input_shift", (1, BW)), ("decay_param", (1, BW)),
    ("recur_output", (BW, D)), ("norm_two", (1, D)), ("first_gate", (192, 128)),
    ("first_value", (192, 128)), ("first_down", (192, 128)), ("norm_three", (1, D)),
    ("query_proj", (8, D)), ("key_proj", (8, HD)), ("value_proj", (8, HD)),
    ("attn_output", (8, D)), ("norm_four", (1, D)), ("second_gate", (192, 128)),
    ("second_value", (192, 128)), ("second_down", (192, 128)),
)
FLAT = (
    "norm_one", "conv_bias", "decay_shift", "input_shift", "decay_param", "norm_two",
    "norm_three", "norm_four",
)
TURNED = (
    "recur_input", "recur_gate", "first_gate", "first_value", "second_gate", "second_value",
)


def local(
    tokens, lengths, cotangent, norm_one, recur_input, recur_gate, conv_kernel, conv_bias,
    decay_gate, decay_shift, input_gate, input_shift, decay_param, recur_output, norm_two,
    first_gate, first_value, first_down, norm_three, query_proj, key_proj, value_proj,
    attn_output, norm_four, second_gate, second_value, second_down,
):
    length = jnp.broadcast_to(lengths.reshape(1, 1), (1, LANE))
    gain_one, gain_two, gain_three, gain_four = (
        g.reshape(1, D) for g in (norm_one, norm_two, norm_three, norm_four)
    )
    flat = lambda v: v.reshape(1, BW)

    index = lax.axis_index("mp") * ROWS + jnp.arange(ROWS, dtype=jnp.int32)
    position = jnp.where(index >= lengths[0], index - lengths[0], index)
    frequency = 10000.0 ** (-2.0 * jnp.arange(HD // 2, dtype=F32) / HD)
    angle = position.astype(F32)[:, None] * frequency[None, :]
    cosine = jnp.concatenate([jnp.cos(angle)] * 2, axis=1)
    sine = jnp.concatenate([-jnp.sin(angle), jnp.sin(angle)], axis=1)

    saved = forward(
        dict(
            tok=tokens, cot=cotangent, length=length, cosine=cosine, sine=sine,
            gain_one=gain_one, gain_two=gain_two, gain_three=gain_three,
            gain_four=gain_four, recur_input=recur_input.T, recur_gate=recur_gate.T, recur_output=recur_output,
            conv_kernel=conv_kernel, conv_bias=flat(conv_bias), decay_gate=decay_gate,
            decay_shift=flat(decay_shift), input_gate=input_gate,
            input_shift=flat(input_shift), decay_param=flat(decay_param),
            first_gate=first_gate.T, first_value=first_value.T, first_down=first_down,
            query_proj=query_proj, key_proj=key_proj, value_proj=value_proj,
            attn_output=attn_output, second_gate=second_gate.T, second_value=second_value.T,
            second_down=second_down,
        )
    )
    kept = lambda *names: {k: saved["out_" + k] for k in names}
    mid = middle(
        dict(
            x3=saved["out_x3"], cot=cotangent, gain_four=gain_four, gain_three=gain_three,
            cosine=cosine, sine=sine,
        ),
        kept("w2", "n4", "c_all", "wa", "kv", "pb", "q", "att", "n3", "x2"),
    )
    end = last(
        dict(
            c2=mid["c2"], x1=saved["out_x1"], tok=tokens, length=length, gain_one=gain_one,
            gain_two=gain_two, gg_three=mid["gg_three"], gg_four=mid["gg_four"],
        ),
        dict(
            kept(
                "w1", "pg", "pu", "n2", "wr", "gate", "state", "rate", "pr", "opened", "conv",
                "mix", "n1", "gated",
            ),
            gw_attn=mid["out_gw_attn"],
            c2_all=mid["out_c2_all"],
        ),
    )
    results = run(
        output_body,
        [
            ("in_outputs", mid["outputs"], "near"),
            ("in_tokens", end["grad_tokens"], "near"),
            ("gains", end["gains"], "near"),
            ("recur_a", end["recur_a"], "near"),
            ("recur_b", end["recur_b"], "near"),
            ("first", end["first_out"], "near"),
            ("second", mid["second_out"], "near"),
            ("attn", end["attn_out"], "near"),
            ("decay", flat(decay_param), "near"),
        ],
        [(name, shape, F32, "near") for name, shape in OUTPUTS],
        [],
    )
    for name in FLAT:
        results[name] = results[name].reshape(-1)
    for name in TURNED:
        results[name] = results[name].T
    return tuple(results[name] for name, _ in OUTPUTS)


def solution(mesh):
    rows = P(("dp", "mp"), None)
    cols = P(None, "mp")
    one = P("mp")
    blocks = P("mp", None, None)
    tile = P("dp", "mp")
    weights = (
        P(), cols, cols, cols, one, blocks, one, blocks, one, one, P("mp", None),
        P(), tile, tile, P("mp", "dp"),
        P(), rows, rows, rows, rows,
        P(), tile, tile, P("mp", "dp"),
    )
    return jax.shard_map(
        local,
        mesh=mesh,
        in_specs=(rows, P("dp"), rows, *weights),
        out_specs=(rows, rows, *weights),
        check_vma=False,
    )
```
